256 devices in a mesh: member: 8 (over z_lo, core), space: 32 (over z_hi, x, y).
Axes of the slice: x: 4, y: 4, z: 8 (z_hi: 2, z_lo: 4; z = z_hi * 4 + z_lo), core: 2. Of those that a mesh axis runs over, the one named last changes fastest.
Arguments:
- ensemble: bfloat16 [8, 512, 64, 256], P('member', 'space'), may hold values from -6 to 6
- shifts: int32 [2], replicated, may hold values from 0 to 15
- land_sea: int32 [512, 64], replicated, may hold values 0 or 1
- member_gain: float32 [256], replicated, may hold values from 0.25 to 1.75
- member_qkv: bfloat16 [256, 768], replicated, may hold values from -0.375 to 0.375
- member_out: bfloat16 [256, 256], replicated, may hold values from -0.375 to 0.375
- first_gain: float32 [256], replicated, may hold values from 0.25 to 1.75
- first_in: bfloat16 [256, 1024], replicated, may hold values from -0.375 to 0.375
- first_out: bfloat16 [1024, 256], replicated, may hold values from -0.1875 to 0.1875
- window_gain: float32 [256], replicated, may hold values from 0.25 to 1.75
- window_qkv: bfloat16 [256, 768], replicated, may hold values from -0.375 to 0.375
- window_out: bfloat16 [256, 256], replicated, may hold values from -0.375 to 0.375
- second_gain: float32 [256], replicated, may hold values from 0.25 to 1.75
- second_in: bfloat16 [256, 1024], replicated, may hold values from -0.375 to 0.375
- second_out: bfloat16 [1024, 256], replicated, may hold values from -0.1875 to 0.1875
Outputs:
- processed: bfloat16 [8, 512, 64, 256], P('member', 'space')
The draws below stay inside these ranges and needn't reach their ends.
Inputs may be any that keep to these rules, and one draw needn't show every extreme that they name: `land_sea`: 1 marks land, 0 sea.
All inputs are finite; a program needn't handle non-finite values.
Results may differ from the reference program's by a relative error of at most 0.015.
Values may be sent and summed in bfloat16 or wider, within the bound.
No kernel may reach another device: no remote copies, remote signals or barrier semaphores. Data moves between devices by JAX's collectives and lax.ppermute only.
A program may use at most 128 MiB of HBM per device.

```python
import math
import jax
import jax.numpy as jnp
from jax import lax

D = 256
HEADS = 8
FF = 1024
WIN = 16
LON = 64
MEMBERS = 8
LAT = 512


def with_ends(values, key, least, largest):
    longest = values.shape.index(max(values.shape))
    spots = []
    for shift in (0, 1):
        where = [jax.random.randint(jax.random.fold_in(key, axis), (), 0, length) for axis, length in enumerate(values.shape)]
        where[longest] = (where[longest] + shift) % values.shape[longest]
        spots.append(tuple(where))
    return values.at[spots[0]].set(least).at[spots[1]].set(largest)


def levels(key, dims, cuts, smallest, top_value):
    gain = 1.0
    for dim, blocks in cuts:
        steps = jax.random.uniform(jax.random.fold_in(jax.random.fold_in(key, 6), dim), (blocks,), jnp.float32, smallest / len(cuts), top_value / len(cuts))
        gain = gain * jnp.repeat(jnp.exp(steps), dims[dim] // blocks).reshape((-1,) + (1,) * (len(dims) - 1 - dim))
    return gain


def noise(key, dims, width, limit, split=(), dtype=jnp.bfloat16):
    drawn = jax.random.normal(key, dims, jnp.float32) * width
    if len(split) > 0:
        drawn = levels(key, dims, split, -0.22, 0.18) * drawn
    return jnp.clip(drawn, min=-limit, max=limit).astype(dtype)


def setup_inputs(seed: int = 0) -> dict:
    splits = jax.random.split(jax.random.key(seed), 16)
    ensemble = noise(splits[0], (MEMBERS, LAT, LON, D), 1.0, 6.0, ((0, 8), (1, 32)))
    shifts = jax.random.randint(splits[1], (2,), 0, WIN).astype(jnp.int32)
    land_sea = with_ends((jax.random.randint(splits[2], (LAT, LON), 0, 3) < 1).astype(jnp.int32), jax.random.fold_in(splits[2], 1), 0, 1)
    member_gain = jnp.clip(1.0 + 0.15 * jax.random.normal(splits[3], (D,), jnp.float32), 0.25, 1.75)
    member_qkv = noise(splits[4], (D, 3 * D), D ** -0.5, 0.375)
    member_out = noise(splits[5], (D, D), D ** -0.5, 0.375)
    first_gain = jnp.clip(1.0 + 0.15 * jax.random.normal(splits[6], (D,), jnp.float32), 0.25, 1.75)
    first_in = noise(splits[7], (D, FF), D ** -0.5, 0.375)
    first_out = noise(splits[8], (FF, D), FF ** -0.5, 0.1875)
    window_gain = jnp.clip(1.0 + 0.15 * jax.random.normal(splits[9], (D,), jnp.float32), 0.25, 1.75)
    window_qkv = noise(splits[10], (D, 3 * D), D ** -0.5, 0.375)
    window_out = noise(splits[11], (D, D), D ** -0.5, 0.375)
    second_gain = jnp.clip(1.0 + 0.15 * jax.random.normal(splits[12], (D,), jnp.float32), 0.25, 1.75)
    second_in = noise(splits[13], (D, FF), D ** -0.5, 0.375)
    second_out = noise(splits[14], (FF, D), FF ** -0.5, 0.1875)
    return {"ensemble": ensemble, "shifts": shifts, "land_sea": land_sea, "member_gain": member_gain, "member_qkv": member_qkv, "member_out": member_out, "first_gain": first_gain, "first_in": first_in, "first_out": first_out, "window_gain": window_gain, "window_qkv": window_qkv, "window_out": window_out, "second_gain": second_gain, "second_in": second_in, "second_out": second_out}


EPSILON = 1e-05

def layer_norm(values, gains):
    values = values.astype(jnp.float32)
    center = lax.optimization_barrier(jnp.mean(values, axis=-1, keepdims=True))
    spread = lax.optimization_barrier(jnp.mean(jnp.square(values - center), axis=-1, keepdims=True))
    return ((values - center) * lax.rsqrt(spread + EPSILON) * gains.astype(jnp.float32)).astype(jnp.bfloat16)

def to_wide(values):
    return lax.optimization_barrier(values.astype(jnp.bfloat16)).astype(jnp.float32)

def attend(normed, w_qkv, w_out, allowed):
    groups, length, features = normed.shape
    head_size = features // HEADS
    projected = jnp.dot(normed.reshape(-1, features), w_qkv, preferred_element_type=jnp.float32)
    projected = to_wide(projected).reshape(groups, length, 3, HEADS, head_size)
    scores = jnp.einsum('bqhd,bkhd->bhqk', projected[:, :, 0], projected[:, :, 1]) / math.sqrt(head_size)
    if allowed is not None:
        scores = jnp.where(allowed[:, None], scores, -1e+30)
    weights = to_wide(jax.nn.softmax(scores, axis=-1))
    attended = jnp.einsum('bhqk,bkhd->bqhd', weights, projected[:, :, 2]).astype(jnp.bfloat16)
    result = jnp.dot(attended.reshape(-1, features), w_out, preferred_element_type=jnp.float32)
    return result.reshape(groups, length, features)

def feed_forward(stream, gains, w_in, w_out):
    features = stream.shape[-1]
    normed = layer_norm(stream, gains).reshape(-1, features)
    hidden = jax.nn.gelu(jnp.dot(normed, w_in, preferred_element_type=jnp.float32)).astype(jnp.bfloat16)
    update = jnp.dot(hidden, w_out, preferred_element_type=jnp.float32).reshape(stream.shape)
    return (stream.astype(jnp.float32) + update).astype(jnp.bfloat16)

def reference(ensemble, shifts, land_sea, member_gain, member_qkv, member_out, first_gain, first_in, first_out, window_gain, window_qkv, window_out, second_gain, second_in, second_out):
    members, latitudes, longitudes, features = ensemble.shape
    blocks = ensemble.reshape(members, latitudes // WIN, WIN, longitudes, features).transpose(1, 0, 2, 3, 4)

    def member_section(row_block):
        points = row_block.transpose(1, 2, 0, 3).reshape(WIN * longitudes, members, features)
        attended = attend(layer_norm(points, member_gain), member_qkv, member_out, None)
        stream = (points.astype(jnp.float32) + attended).astype(jnp.bfloat16)
        stream = feed_forward(stream, first_gain, first_in, first_out)
        return stream.reshape(WIN, longitudes, members, features).transpose(2, 0, 1, 3)
    sectioned = lax.map(member_section, blocks)
    gridded = sectioned.transpose(1, 0, 2, 3, 4).reshape(members, latitudes, longitudes, features)
    rolled = jnp.roll(gridded, (-shifts[0], -shifts[1]), axis=(1, 2))
    surface = jnp.roll(land_sea, (-shifts[0], -shifts[1]), axis=(0, 1))
    window_blocks = rolled.reshape(members, latitudes // WIN, WIN, longitudes // WIN, WIN, features).transpose(1, 0, 3, 2, 4, 5)
    surface_blocks = surface.reshape(latitudes // WIN, WIN, longitudes // WIN, WIN).transpose(0, 2, 1, 3)

    def window_section(operands):
        row_block, surface_kinds = operands
        tokens_in = row_block.reshape(members * (longitudes // WIN), WIN * WIN, features)
        flat_kinds = surface_kinds.reshape(longitudes // WIN, WIN * WIN)
        allowed = flat_kinds[:, :, None] == flat_kinds[:, None, :]
        allowed = jnp.tile(allowed, (members, 1, 1))
        attended = attend(layer_norm(tokens_in, window_gain), window_qkv, window_out, allowed)
        stream = (tokens_in.astype(jnp.float32) + attended).astype(jnp.bfloat16)
        stream = feed_forward(stream, second_gain, second_in, second_out)
        return stream.reshape(row_block.shape)
    finished = lax.map(window_section, (window_blocks, surface_blocks))
    result = finished.transpose(1, 0, 3, 2, 4, 5).reshape(members, latitudes, longitudes, features)
    return jnp.roll(result, (shifts[0], shifts[1]), axis=(1, 2))
```

```python
import math

import jax
import jax.numpy as jnp
from jax import lax
from jax.experimental import pallas as pl
from jax.experimental.pallas import tpu as pltpu
from jax.sharding import PartitionSpec as P

HEADS = 8
WIN = 16
EPSILON = 1e-05
BLOCK = 256
FAR = 1e30


def normalise(values, gains):
    center = jnp.mean(values, axis=-1, keepdims=True)
    shifted = values - center
    spread = jnp.mean(shifted * shifted, axis=-1, keepdims=True)
    return (shifted * lax.rsqrt(spread + EPSILON) * gains).astype(jnp.bfloat16)


def wide_dot(a, b):
    return jnp.dot(a, b, preferred_element_type=jnp.float32)


def gelu(x):
    inner = x * (0.7978845608028654 + 0.035677408136300125 * (x * x))
    return (x * (0.5 + 0.5 * jnp.tanh(inner))).astype(jnp.bfloat16)


def feed_forward(stream, gain_ref, in_ref, out_ref):
    wide = stream.astype(jnp.float32)
    normed = normalise(wide, gain_ref[...])
    hidden_size = in_ref.shape[1]
    total = wide
    for start in range(0, hidden_size, BLOCK):
        hidden = gelu(wide_dot(normed, in_ref[:, start : start + BLOCK]))
        total = total + wide_dot(hidden, out_ref[start : start + BLOCK, :])
    return total.astype(jnp.bfloat16)


def member_kernel(x_ref, gain_ref, qkv_ref, out_ref, gain2_ref, in2_ref, out2_ref, o_ref):
    members, points, features = x_ref.shape
    tokens = members * points
    size = features // HEADS
    stream = x_ref[...].astype(jnp.float32).reshape(tokens, features)
    normed = normalise(stream, gain_ref[...])
    query = wide_dot(normed, qkv_ref[:, :features]).astype(jnp.bfloat16)
    key = wide_dot(normed, qkv_ref[:, features : 2 * features]).astype(jnp.bfloat16)
    value = wide_dot(normed, qkv_ref[:, 2 * features :])
    query = query.reshape(members, points, features)
    key = key.reshape(members, points, features)
    value = value.astype(jnp.bfloat16).astype(jnp.float32).reshape(members, points, features)

    lane = lax.broadcasted_iota(jnp.int32, (features, 128), 1) % 64
    head = lax.broadcasted_iota(jnp.int32, (features, 128), 0) // size
    place = lane - head
    scores = jnp.zeros((tokens, 128), jnp.float32)
    for j in range(members):
        pick = jnp.where((place == j * HEADS) & (lane // HEADS == j), 1.0, 0.0).astype(jnp.bfloat16)
        product = (query * key[j][None]).reshape(tokens, features)
        scores = scores + wide_dot(product, pick)
    top = scores
    for step in (8, 16, 32):
        top = jnp.maximum(top, pltpu.roll(top, step, 1))
    weights = jnp.exp((scores - top) * (1.0 / math.sqrt(size)))
    total = weights
    for step in (8, 16, 32):
        total = total + pltpu.roll(total, step, 1)
    weights = (weights / total).astype(jnp.bfloat16)

    lane = lax.broadcasted_iota(jnp.int32, (128, features), 0)
    head = lax.broadcasted_iota(jnp.int32, (128, features), 1) // size
    place = lane - head
    mixed = jnp.zeros((members, points, features), jnp.float32)
    for j in range(members):
        spread = jnp.where(place == j * HEADS, 1.0, 0.0).astype(jnp.bfloat16)
        widened = wide_dot(weights, spread).reshape(members, points, features)
        mixed = mixed + widened * value[j][None]
    mixed = mixed.reshape(tokens, features).astype(jnp.bfloat16)
    stream = (stream + wide_dot(mixed, out_ref[...])).astype(jnp.bfloat16)
    result = feed_forward(stream, gain2_ref, in2_ref, out2_ref)
    o_ref[...] = result.reshape(members, points, features)


def window_kernel(
    place_ref, x_ref, kinds_ref, gain_ref, qkv_ref, out_ref, gain2_ref, in2_ref, out2_ref, o_ref
):
    rows, longitudes, features = x_ref.shape
    windows = longitudes // WIN
    size = features // HEADS
    half = features // 2
    tokens = WIN * WIN
    lat_shift = place_ref[0]
    lon_shift = place_ref[1]
    w = pl.program_id(0)
    here = pl.ds(pl.multiple_of(w * WIN, WIN), WIN)
    following = lax.rem(w + 1, windows)
    there = pl.ds(pl.multiple_of(following * WIN, WIN), WIN)

    column = lax.broadcasted_iota(jnp.int32, (WIN, WIN, features), 1)
    inside = column >= lon_shift
    stream = jnp.where(
        inside, x_ref[:, here, :].astype(jnp.float32), x_ref[:, there, :].astype(jnp.float32)
    ).reshape(tokens, features)

    upper = kinds_ref[place_ref[2]].astype(jnp.float32)
    lower = kinds_ref[place_ref[3]].astype(jnp.float32)
    row = lax.broadcasted_iota(jnp.int32, (rows, longitudes), 0)
    kinds = jnp.where(row >= lat_shift, upper, lower)
    kinds = jnp.broadcast_to(kinds[:, None, :], (WIN, WIN, longitudes))
    column = lax.broadcasted_iota(jnp.int32, (WIN, WIN, longitudes), 1)
    lane = lax.broadcasted_iota(jnp.int32, (WIN, WIN, longitudes), 2)
    wanted = jnp.where(column >= lon_shift, w * WIN, following * WIN) + column
    kinds = jnp.where(lane == wanted, kinds, 0.0).reshape(tokens, longitudes)
    kind = jnp.sum(kinds, axis=-1, keepdims=True)
    kind = jnp.broadcast_to(kind, (tokens, features))

    normed = normalise(stream, gain_ref[...])
    query = wide_dot(normed, qkv_ref[:, :features])
    key = wide_dot(normed, qkv_ref[:, features : 2 * features])
    value = wide_dot(normed, qkv_ref[:, 2 * features :])

    lane = lax.broadcasted_iota(jnp.int32, (tokens, features), 1)
    query_marks, key_marks = [], []
    for first in (features - size, 0):
        query_marks.append(
            jnp.where(
                lane == first, -FAR * kind, jnp.where(lane == first + 1, -FAR * (1.0 - kind), 0.0)
            )
        )
        marked = jnp.where(lane == first, 1.0 - kind, jnp.where(lane == first + 1, kind, 0.0))
        free = (lane >= first) & (lane < first + size)
        key_marks.append(jnp.where(free, marked, key).astype(jnp.bfloat16))
    scale = 1.0 / math.sqrt(size)
    outputs = []
    for group in range(2):
        total = jnp.zeros((tokens, features), jnp.float32)
        for h in range(group * HEADS // 2, (group + 1) * HEADS // 2):
            own = (lane >= h * size) & (lane < (h + 1) * size)
            q = jnp.where(own, query, query_marks[group]).astype(jnp.bfloat16)
            scores = lax.dot_general(
                q, key_marks[group], (((1,), (1,)), ((), ())), preferred_element_type=jnp.float32
            )
            top = jnp.max(scores, axis=-1, keepdims=True)
            weights = jnp.exp((scores - top) * scale).astype(jnp.bfloat16)
            opposite = h * size + (half if group == 0 else -half)
            ones = (lane >= opposite) & (lane < opposite + size)
            v = jnp.where(own, value, jnp.where(ones, 1.0, 0.0)).astype(jnp.bfloat16)
            total = total + wide_dot(weights, v)
        if group == 0:
            outputs.append(total[:, :half] / total[:, half:])
        else:
            outputs.append(total[:, half:] / total[:, :half])
    mixed = jnp.concatenate(outputs, axis=-1).astype(jnp.bfloat16)
    stream = (stream + wide_dot(mixed, out_ref[...])).astype(jnp.bfloat16)
    result = feed_forward(stream, gain2_ref, in2_ref, out2_ref).astype(jnp.float32)
    result = result.reshape(WIN, WIN, features)
    column = lax.broadcasted_iota(jnp.int32, (WIN, WIN, features), 1)
    inside = column >= lon_shift
    kept = o_ref[:, here, :].astype(jnp.float32)
    o_ref[:, here, :] = jnp.where(inside, result, kept).astype(jnp.bfloat16)
    kept = o_ref[:, there, :].astype(jnp.float32)
    o_ref[:, there, :] = jnp.where(inside, kept, result).astype(jnp.bfloat16)


def whole(array):
    return pl.BlockSpec(array.shape, lambda b, n=array.ndim: (0,) * n)


def member_layer(points, *params):
    members, count, features = points.shape
    block = BLOCK // members
    spec = pl.BlockSpec((members, block, features), lambda b: (0, b, 0))
    return pl.pallas_call(
        member_kernel,
        grid=(count // block,),
        out_shape=jax.ShapeDtypeStruct(points.shape, jnp.bfloat16),
        in_specs=[spec] + [whole(p) for p in params],
        out_specs=spec,
        compiler_params=pltpu.CompilerParams(vmem_limit_bytes=32 * 2**20),
    )(points, *params)


def window_layer(place, region, kinds, *params):
    return pl.pallas_call(
        window_kernel,
        grid=(region.shape[1] // WIN,),
        out_shape=jax.ShapeDtypeStruct(region.shape, jnp.bfloat16),
        in_specs=[pl.BlockSpec(memory_space=pltpu.SMEM)]
        + [whole(a) for a in (region, kinds) + params],
        out_specs=whole(region),
        compiler_params=pltpu.CompilerParams(vmem_limit_bytes=32 * 2**20),
    )(place, region, kinds, *params)


def on_device(
    ensemble,
    shifts,
    land_sea,
    member_gain,
    member_qkv,
    member_out,
    first_gain,
    first_in,
    first_out,
    window_gain,
    window_qkv,
    window_out,
    second_gain,
    second_in,
    second_out,
):
    _, rows, longitudes, features = ensemble.shape
    half = rows // 2
    members = lax.axis_size("member")
    spaces = lax.axis_size("space")
    space = lax.axis_index("space")
    up = [(i, (i + 1) % spaces) for i in range(spaces)]
    down = [(j, i) for i, j in up]
    lat_shift, lon_shift = shifts[0], shifts[1]
    kinds = land_sea.reshape(spaces, rows, longitudes)
    own = ensemble[0]
    row = jnp.arange(rows, dtype=jnp.int32)[:, None, None]
    gains = [g.reshape(1, features) for g in (member_gain, first_gain, window_gain, second_gain)]

    def run(window_below):
        if window_below:
            other = lax.ppermute(own[:half], "space", down)
            low = jnp.where(row[:half] >= lat_shift, own[:half], other)
            merged = jnp.concatenate([low, own[half:]])
            blocks = (space, lax.rem(space + 1, spaces))
        else:
            other = lax.ppermute(own[half:], "space", up)
            high = jnp.where(row[half:] >= lat_shift, other, own[half:])
            merged = jnp.concatenate([own[:half], high])
            blocks = (lax.rem(space + spaces - 1, spaces), space)
        parts = merged.reshape(members, -1, features)
        points = lax.all_to_all(parts, "member", split_axis=0, concat_axis=0, tiled=True)
        points = member_layer(
            points, gains[0], member_qkv, member_out, gains[1], first_in, first_out
        )
        region = lax.all_to_all(points, "member", split_axis=0, concat_axis=0, tiled=True)
        place = jnp.stack([lat_shift, lon_shift, blocks[0], blocks[1]]).astype(jnp.int32)
        result = window_layer(
            place,
            region.reshape(rows, longitudes, features),
            kinds,
            gains[2],
            window_qkv,
            window_out,
            gains[3],
            second_in,
            second_out,
        )
        if window_below:
            back = lax.ppermute(result[:half], "space", up)
            low = jnp.where(row[:half] >= lat_shift, result[:half], back)
            return jnp.concatenate([low, result[half:]])
        back = lax.ppermute(result[half:], "space", down)
        high = jnp.where(row[half:] >= lat_shift, back, result[half:])
        return jnp.concatenate([result[:half], high])

    out = lax.cond(lat_shift <= half, lambda: run(True), lambda: run(False))
    return out[None]


def solution(mesh):
    return jax.shard_map(
        on_device,
        mesh=mesh,
        in_specs=(P("member", "space", None, None),) + (P(),) * 14,
        out_specs=P("member", "space", None, None),
        check_vma=False,
    )
```

```python
import math

import jax
import jax.numpy as jnp
from jax import lax
from jax.experimental import pallas as pl
from jax.experimental.pallas import tpu as pltpu
from jax.sharding import PartitionSpec as P

HEADS = 8
WIN = 16
EPSILON = 1e-05
BLOCK = 256
FAR = 1e30


def normalise(values, gains):
    center = jnp.mean(values, axis=-1, keepdims=True)
    shifted = values - center
    spread = jnp.mean(shifted * shifted, axis=-1, keepdims=True)
    return (shifted * lax.rsqrt(spread + EPSILON) * gains).astype(jnp.bfloat16)


def wide_dot(a, b):
    return jnp.dot(a, b, preferred_element_type=jnp.float32)


def gelu(x):
    inner = x * (0.7978845608028654 + 0.035677408136300125 * (x * x))
    return (x * (0.5 + 0.5 * jnp.tanh(inner))).astype(jnp.bfloat16)


def feed_forward(stream, gain_ref, in_ref, out_ref):
    wide = stream.astype(jnp.float32)
    normed = normalise(wide, gain_ref[...])
    hidden_size = in_ref.shape[1]
    total = wide
    for start in range(0, hidden_size, BLOCK):
        hidden = gelu(wide_dot(normed, in_ref[:, start : start + BLOCK]))
        total = total + wide_dot(hidden, out_ref[start : start + BLOCK, :])
    return total.astype(jnp.bfloat16)


def member_kernel(x_ref, gain_ref, qkv_ref, out_ref, gain2_ref, in2_ref, out2_ref, o_ref):
    members, points, features = x_ref.shape
    tokens = members * points
    size = features // HEADS
    stream = x_ref[...].astype(jnp.float32).reshape(tokens, features)
    normed = normalise(stream, gain_ref[...])
    query = wide_dot(normed, qkv_ref[:, :features]).astype(jnp.bfloat16)
    key = wide_dot(normed, qkv_ref[:, features : 2 * features]).astype(jnp.bfloat16)
    value = wide_dot(normed, qkv_ref[:, 2 * features :])
    query = query.reshape(members, points, features)
    key = key.reshape(members, points, features)
    value = value.astype(jnp.bfloat16).astype(jnp.float32).reshape(members, points, features)

    lane = lax.broadcasted_iota(jnp.int32, (features, 128), 1) % 64
    head = lax.broadcasted_iota(jnp.int32, (features, 128), 0) // size
    place = lane - head
    scores = jnp.zeros((tokens, 128), jnp.float32)
    for j in range(members):
        pick = jnp.where((place == j * HEADS) & (lane // HEADS == j), 1.0, 0.0).astype(jnp.bfloat16)
        product = (query * key[j][None]).reshape(tokens, features)
        scores = scores + wide_dot(product, pick)
    top = scores
    for step in (8, 16, 32):
        top = jnp.maximum(top, pltpu.roll(top, step, 1))
    weights = jnp.exp((scores - top) * (1.0 / math.sqrt(size)))
    total = weights
    for step in (8, 16, 32):
        total = total + pltpu.roll(total, step, 1)
    weights = (weights / total).astype(jnp.bfloat16)

    lane = lax.broadcasted_iota(jnp.int32, (128, features), 0)
    head = lax.broadcasted_iota(jnp.int32, (128, features), 1) // size
    place = lane - head
    mixed = jnp.zeros((members, points, features), jnp.float32)
    for j in range(members):
        spread = jnp.where(place == j * HEADS, 1.0, 0.0).astype(jnp.bfloat16)
        widened = wide_dot(weights, spread).reshape(members, points, features)
        mixed = mixed + widened * value[j][None]
    mixed = mixed.reshape(tokens, features).astype(jnp.bfloat16)
    stream = (stream + wide_dot(mixed, out_ref[...])).astype(jnp.bfloat16)
    result = feed_forward(stream, gain2_ref, in2_ref, out2_ref)
    o_ref[...] = result.reshape(members, points, features)


def window_kernel(
    place_ref,
    low_ref,
    high_ref,
    kinds_ref,
    gain_ref,
    qkv_ref,
    out_ref,
    gain2_ref,
    in2_ref,
    out2_ref,
    o_ref,
):
    rows, longitudes, features = o_ref.shape
    windows = longitudes // WIN
    size = features // HEADS
    half = features // 2
    tokens = WIN * WIN
    lat_shift = place_ref[0]
    lon_shift = place_ref[1]
    w = pl.program_id(0)
    here = pl.ds(pl.multiple_of(w * WIN, WIN), WIN)
    following = lax.rem(w + 1, windows)
    there = pl.ds(pl.multiple_of(following * WIN, WIN), WIN)

    column = lax.broadcasted_iota(jnp.int32, (WIN, WIN, features), 1)
    inside = column >= lon_shift
    region = [
        jnp.concatenate([low_ref[:, at, :], high_ref[:, at, :]]).astype(jnp.float32)
        for at in (here, there)
    ]
    stream = jnp.where(inside, *region).reshape(tokens, features)

    upper = kinds_ref[place_ref[2]].astype(jnp.float32)
    lower = kinds_ref[place_ref[3]].astype(jnp.float32)
    row = lax.broadcasted_iota(jnp.int32, (rows, longitudes), 0)
    kinds = jnp.where(row >= lat_shift, upper, lower)
    kinds = jnp.broadcast_to(kinds[:, None, :], (WIN, WIN, longitudes))
    column = lax.broadcasted_iota(jnp.int32, (WIN, WIN, longitudes), 1)
    lane = lax.broadcasted_iota(jnp.int32, (WIN, WIN, longitudes), 2)
    wanted = jnp.where(column >= lon_shift, w * WIN, following * WIN) + column
    kinds = jnp.where(lane == wanted, kinds, 0.0).reshape(tokens, longitudes)
    kind = jnp.sum(kinds, axis=-1, keepdims=True)
    kind = jnp.broadcast_to(kind, (tokens, features))

    normed = normalise(stream, gain_ref[...])
    query = wide_dot(normed, qkv_ref[:, :features])
    key = wide_dot(normed, qkv_ref[:, features : 2 * features])
    value = wide_dot(normed, qkv_ref[:, 2 * features :])

    lane = lax.broadcasted_iota(jnp.int32, (tokens, features), 1)
    query_marks, key_marks = [], []
    for first in (features - size, 0):
        query_marks.append(
            jnp.where(
                lane == first, -FAR * kind, jnp.where(lane == first + 1, -FAR * (1.0 - kind), 0.0)
            )
        )
        marked = jnp.where(lane == first, 1.0 - kind, jnp.where(lane == first + 1, kind, 0.0))
        free = (lane >= first) & (lane < first + size)
        key_marks.append(jnp.where(free, marked, key).astype(jnp.bfloat16))
    scale = 1.0 / math.sqrt(size)
    outputs = []
    for group in range(2):
        total = jnp.zeros((tokens, features), jnp.float32)
        for h in range(group * HEADS // 2, (group + 1) * HEADS // 2):
            own = (lane >= h * size) & (lane < (h + 1) * size)
            q = jnp.where(own, query, query_marks[group]).astype(jnp.bfloat16)
            scores = lax.dot_general(
                q, key_marks[group], (((1,), (1,)), ((), ())), preferred_element_type=jnp.float32
            )
            top = jnp.max(scores, axis=-1, keepdims=True)
            weights = jnp.exp((scores - top) * scale).astype(jnp.bfloat16)
            opposite = h * size + (half if group == 0 else -half)
            ones = (lane >= opposite) & (lane < opposite + size)
            v = jnp.where(own, value, jnp.where(ones, 1.0, 0.0)).astype(jnp.bfloat16)
            total = total + wide_dot(weights, v)
        if group == 0:
            outputs.append(total[:, :half] / total[:, half:])
        else:
            outputs.append(total[:, half:] / total[:, :half])
    mixed = jnp.concatenate(outputs, axis=-1).astype(jnp.bfloat16)
    stream = (stream + wide_dot(mixed, out_ref[...])).astype(jnp.bfloat16)
    result = feed_forward(stream, gain2_ref, in2_ref, out2_ref).astype(jnp.float32)
    result = result.reshape(WIN, WIN, features)
    column = lax.broadcasted_iota(jnp.int32, (WIN, WIN, features), 1)
    inside = column >= lon_shift
    kept = o_ref[:, here, :].astype(jnp.float32)
    o_ref[:, here, :] = jnp.where(inside, result, kept).astype(jnp.bfloat16)
    kept = o_ref[:, there, :].astype(jnp.float32)
    o_ref[:, there, :] = jnp.where(inside, kept, result).astype(jnp.bfloat16)


def whole(array):
    return pl.BlockSpec(array.shape, lambda b, n=array.ndim: (0,) * n)


def member_layer(points, *params):
    members, count, features = points.shape
    block = BLOCK // members
    spec = pl.BlockSpec((members, block, features), lambda b: (0, b, 0))
    return pl.pallas_call(
        member_kernel,
        grid=(count // block,),
        out_shape=jax.ShapeDtypeStruct(points.shape, jnp.bfloat16),
        in_specs=[spec] + [whole(p) for p in params],
        out_specs=spec,
        compiler_params=pltpu.CompilerParams(vmem_limit_bytes=32 * 2**20),
        cost_estimate=pl.CostEstimate(
            flops=16 * 10**8, bytes_accessed=3 * 2**20, transcendentals=6 * 10**5
        ),
    )(points, *params)


def window_layer(place, low, high, kinds, *params):
    half, longitudes, features = low.shape
    region = (2 * half, longitudes, features)
    return pl.pallas_call(
        window_kernel,
        grid=(longitudes // WIN,),
        out_shape=jax.ShapeDtypeStruct(region, jnp.bfloat16),
        in_specs=[pl.BlockSpec(memory_space=pltpu.SMEM)]
        + [whole(a) for a in (low, high, kinds) + params],
        out_specs=pl.BlockSpec(region, lambda b: (0, 0, 0)),
        compiler_params=pltpu.CompilerParams(vmem_limit_bytes=32 * 2**20),
        cost_estimate=pl.CostEstimate(
            flops=4 * 10**9, bytes_accessed=3 * 2**20, transcendentals=4 * 10**6
        ),
    )(place, low, high, kinds, *params)


def on_device(
    ensemble,
    shifts,
    land_sea,
    member_gain,
    member_qkv,
    member_out,
    first_gain,
    first_in,
    first_out,
    window_gain,
    window_qkv,
    window_out,
    second_gain,
    second_in,
    second_out,
):
    _, rows, longitudes, features = ensemble.shape
    half = rows // 2
    members = lax.axis_size("member")
    spaces = lax.axis_size("space")
    space = lax.axis_index("space")
    up = [(i, (i + 1) % spaces) for i in range(spaces)]
    down = [(j, i) for i, j in up]
    lat_shift, lon_shift = shifts[0], shifts[1]
    kinds = land_sea.reshape(spaces, rows, longitudes)
    own = ensemble[0]
    row = jnp.arange(rows, dtype=jnp.int32)[:, None, None]
    gains = [g.reshape(1, features) for g in (member_gain, first_gain, window_gain, second_gain)]

    def run(window_below):
        if window_below:
            other = lax.ppermute(own[:half], "space", down)
            merged_half = jnp.where(row[:half] >= lat_shift, own[:half], other)
            whole_half = own[half:]
            blocks = (space, lax.rem(space + 1, spaces))
        else:
            other = lax.ppermute(own[half:], "space", up)
            merged_half = jnp.where(row[half:] >= lat_shift, other, own[half:])
            whole_half = own[:half]
            blocks = (lax.rem(space + spaces - 1, spaces), space)
        place = jnp.stack([lat_shift, lon_shift, *blocks]).astype(jnp.int32)

        def mixed(chunk):
            points = lax.all_to_all(chunk, "member", split_axis=0, concat_axis=0, tiled=True)
            points = member_layer(
                points, gains[0], member_qkv, member_out, gains[1], first_in, first_out
            )
            return lax.all_to_all(points, "member", split_axis=0, concat_axis=0, tiled=True)

        settled = mixed(whole_half)
        halves = [mixed(merged_half), settled] if window_below else [settled, mixed(merged_half)]
        result = window_layer(
            place,
            *halves,
            kinds,
            gains[2],
            window_qkv,
            window_out,
            gains[3],
            second_in,
            second_out,
        )
        if window_below:
            back = lax.ppermute(result[:half], "space", up)
            low = jnp.where(row[:half] >= lat_shift, result[:half], back)
            return jnp.concatenate([low, result[half:]])
        back = lax.ppermute(result[half:], "space", down)
        high = jnp.where(row[half:] >= lat_shift, back, result[half:])
        return jnp.concatenate([result[:half], high])

    out = lax.cond(lat_shift <= half, lambda: run(True), lambda: run(False))
    return out[None]


def solution(mesh):
    return jax.shard_map(
        on_device,
        mesh=mesh,
        in_specs=(P("member", "space", None, None),) + (P(),) * 14,
        out_specs=P("member", "space", None, None),
        check_vma=False,
    )
```

```python
import math

import jax
import jax.numpy as jnp
from jax import lax
from jax.experimental import pallas as pl
from jax.experimental.pallas import tpu as pltpu
from jax.sharding import PartitionSpec as P

HEADS = 8
WIN = 16
EPSILON = 1e-05
BLOCK = 256
FAR = 1e30
VMEM = pl.BlockSpec(memory_space=pltpu.VMEM)
SMEM = pl.BlockSpec(memory_space=pltpu.SMEM)


def normalise(values, gains):
    center = jnp.mean(values, axis=-1, keepdims=True)
    shifted = values - center
    spread = jnp.mean(shifted * shifted, axis=-1, keepdims=True)
    return (shifted * lax.rsqrt(spread + EPSILON) * gains).astype(jnp.bfloat16)


def wide_dot(a, b):
    return jnp.dot(a, b, preferred_element_type=jnp.float32)


def twice_gelu(x):
    inner = x * (0.7978845608028654 + 0.035677408136300125 * (x * x))
    return (x + x * jnp.tanh(inner)).astype(jnp.bfloat16)


def feed_forward(stream, gain_ref, in_ref, out_ref):
    wide = stream.astype(jnp.float32)
    normed = normalise(wide, gain_ref[...])
    hidden_size = in_ref.shape[1]
    update = None
    for start in range(0, hidden_size, BLOCK):
        hidden = twice_gelu(wide_dot(normed, in_ref[:, start : start + BLOCK]))
        part = wide_dot(hidden, out_ref[start : start + BLOCK, :])
        update = part if update is None else update + part
    return (wide + 0.5 * update).astype(jnp.bfloat16)


def mix_members(x, gain_ref, qkv_ref, out_ref, gain2_ref, in2_ref, out2_ref):
    members, points, features = x.shape
    tokens = members * points
    size = features // HEADS
    stream = x.reshape(tokens, features).astype(jnp.float32)
    normed = normalise(stream, gain_ref[...])
    query = wide_dot(normed, qkv_ref[:, :features]) * (math.log2(math.e) / math.sqrt(size))
    key = wide_dot(normed, qkv_ref[:, features : 2 * features]).astype(jnp.bfloat16)
    value = wide_dot(normed, qkv_ref[:, 2 * features :])
    query = query.astype(jnp.bfloat16).reshape(members, points, features)
    key = key.reshape(members, points, features)
    value = value.astype(jnp.bfloat16).astype(jnp.float32).reshape(members, points, features)

    lane = lax.broadcasted_iota(jnp.int32, (features, 128), 1) % 64
    head = lax.broadcasted_iota(jnp.int32, (features, 128), 0) // size
    place = lane - head
    scores = jnp.zeros((tokens, 128), jnp.float32)
    for j in range(members):
        pick = jnp.where((place == j * HEADS) & (lane // HEADS == j), 1.0, 0.0).astype(jnp.bfloat16)
        product = (query * key[j][None]).reshape(tokens, features)
        scores = scores + wide_dot(product, pick)
    top = scores
    for step in (8, 16, 32):
        top = jnp.maximum(top, pltpu.roll(top, step, 1))
    weights = jnp.exp2(scores - top)
    total = weights
    for step in (8, 16, 32):
        total = total + pltpu.roll(total, step, 1)
    weights = (weights / total).astype(jnp.bfloat16)

    lane = lax.broadcasted_iota(jnp.int32, (128, features), 0)
    head = lax.broadcasted_iota(jnp.int32, (128, features), 1) // size
    place = lane - head
    mixed = None
    for j in range(members):
        spread = jnp.where(place == j * HEADS, 1.0, 0.0).astype(jnp.bfloat16)
        widened = wide_dot(weights, spread).reshape(members, points, features)
        part = widened * value[j][None]
        mixed = part if mixed is None else mixed + part
    mixed = mixed.reshape(tokens, features).astype(jnp.bfloat16)
    stream = (stream + wide_dot(mixed, out_ref[...])).astype(jnp.bfloat16)
    result = feed_forward(stream, gain2_ref, in2_ref, out2_ref)
    return result.reshape(members, points, features)


def first_member_kernel(x_ref, *refs):
    *params, o_ref = refs
    o_ref[...] = mix_members(x_ref[...], *params)


def second_member_kernel(slot, x_ref, done_ref, *refs):
    *params, o_ref = refs
    o_ref[:, 1 - slot] = done_ref[...]
    o_ref[:, slot] = mix_members(x_ref[...], *params)


def merging_kernel(first_row, shifts_ref, later_ref, earlier_ref, o_ref):
    for i in range(o_ref.shape[0]):
        o_ref[i] = jnp.where(first_row + i >= shifts_ref[0], later_ref[i], earlier_ref[i])


def window_kernel(
    window_below,
    shifts_ref,
    x_ref,
    kinds_ref,
    gain_ref,
    qkv_ref,
    out_ref,
    gain2_ref,
    in2_ref,
    out2_ref,
    low_ref,
    high_ref,
    kinds_scratch,
    sems,
):
    half, longitudes, features = low_ref.shape
    windows = longitudes // WIN
    size = features // HEADS
    group_lanes = features // 2
    tokens = WIN * WIN
    lat_shift, lon_shift = shifts_ref[0], shifts_ref[1]
    space = lax.axis_index("space")
    spaces = kinds_ref.shape[0] // WIN
    if window_below:
        blocks = (space, lax.rem(space + 1, spaces))
    else:
        blocks = (lax.rem(space + spaces - 1, spaces), space)
    copies = [
        pltpu.make_async_copy(
            kinds_ref.at[pl.ds(pl.multiple_of(block * WIN, WIN), WIN)],
            kinds_scratch.at[n],
            sems.at[n],
        )
        for n, block in enumerate(blocks)
    ]
    for copy in copies:
        copy.start()

    column = lax.broadcasted_iota(jnp.int32, (WIN, WIN, features), 1)
    inside = column >= lon_shift
    tiles = [
        jnp.concatenate(
            [x_ref[:, part, w * WIN : (w + 1) * WIN, :] for part in range(2)]
        ).astype(jnp.float32)
        for w in range(windows)
    ]
    stream = jnp.concatenate(
        [
            jnp.where(inside, tiles[w], tiles[(w + 1) % windows]).reshape(tokens, features)
            for w in range(windows)
        ]
    )
    normed = normalise(stream, gain_ref[...])
    query = wide_dot(normed, qkv_ref[:, :features]) * (math.log2(math.e) / math.sqrt(size))
    query = query.astype(jnp.bfloat16)
    key = wide_dot(normed, qkv_ref[:, features : 2 * features])
    value = wide_dot(normed, qkv_ref[:, 2 * features :]).astype(jnp.bfloat16)

    for copy in copies:
        copy.wait()
    row = lax.broadcasted_iota(jnp.int32, (WIN, longitudes), 0)
    kinds = jnp.where(row >= lat_shift, kinds_scratch[0], kinds_scratch[1]).astype(jnp.float32)
    kinds = jnp.broadcast_to(kinds[:, None, :], (WIN, WIN, longitudes))
    kind_column = lax.broadcasted_iota(jnp.int32, (WIN, WIN, longitudes), 1)
    kind_lane = lax.broadcasted_iota(jnp.int32, (WIN, WIN, longitudes), 2)

    lane = lax.broadcasted_iota(jnp.int32, (tokens, features), 1)
    lane_row = lax.broadcasted_iota(jnp.int32, (1, features), 1)

    def head_lanes(first):
        return jnp.where(
            (lane_row >= first) & (lane_row < first + size), 1.0, 0.0
        ).astype(jnp.bfloat16)

    attended = []
    for w in range(windows):
        at = slice(w * tokens, (w + 1) * tokens)
        wanted = kind_column + jnp.where(
            kind_column >= lon_shift, w * WIN, (w + 1) % windows * WIN
        )
        kind = jnp.where(kind_lane == wanted, kinds, 0.0).reshape(tokens, longitudes)
        kind = jnp.sum(kind, axis=-1, keepdims=True)
        halves = []
        for group in range(2):
            first = features - size if group == 0 else 0
            query_marks = jnp.where(
                lane == first, -FAR * kind, jnp.where(lane == first + 1, -FAR * (1.0 - kind), 0.0)
            ).astype(jnp.bfloat16)
            marked = jnp.where(lane == first, 1.0 - kind, jnp.where(lane == first + 1, kind, 0.0))
            free = (lane >= first) & (lane < first + size)
            keys = jnp.where(free, marked, key[at]).astype(jnp.bfloat16)
            total = None
            for h in range(group * HEADS // 2, (group + 1) * HEADS // 2):
                q = query[at] * head_lanes(h * size) + query_marks
                scores = lax.dot_general(
                    q, keys, (((1,), (1,)), ((), ())), preferred_element_type=jnp.float32
                )
                top = jnp.max(scores, axis=-1, keepdims=True)
                weights = jnp.exp2(scores - top).astype(jnp.bfloat16)
                opposite = h * size + (group_lanes if group == 0 else -group_lanes)
                v = value[at] * head_lanes(h * size) + head_lanes(opposite)
                part = wide_dot(weights, v)
                total = part if total is None else total + part
            if group == 0:
                halves.append(total[:, :group_lanes] / total[:, group_lanes:])
            else:
                halves.append(total[:, group_lanes:] / total[:, :group_lanes])
        attended.append(jnp.concatenate(halves, axis=-1).astype(jnp.bfloat16))
    attended = jnp.concatenate(attended)
    stream = (stream + wide_dot(attended, out_ref[...])).astype(jnp.bfloat16)
    result = feed_forward(stream, gain2_ref, in2_ref, out2_ref).astype(jnp.float32)
    result = result.reshape(windows, WIN, WIN, features)
    for w in range(windows):
        tile = jnp.where(inside, result[w], result[(w + windows - 1) % windows])
        tile = tile.astype(jnp.bfloat16)
        low_ref[:, w * WIN : (w + 1) * WIN, :] = tile[:half]
        high_ref[:, w * WIN : (w + 1) * WIN, :] = tile[half:]


def cost(tokens, flops_per_token):
    return pl.CostEstimate(
        flops=tokens * flops_per_token, bytes_accessed=3 * 2**20, transcendentals=tokens * 2048
    )


LARGE = pltpu.CompilerParams(vmem_limit_bytes=48 * 2**20)


def first_member_layer(points, *params):
    return pl.pallas_call(
        first_member_kernel,
        out_shape=jax.ShapeDtypeStruct(points.shape, jnp.bfloat16),
        in_specs=[VMEM] * (1 + len(params)),
        out_specs=VMEM,
        compiler_params=LARGE,
        cost_estimate=cost(512, 1600000),
    )(points, *params)


def second_member_layer(slot, points, done, *params):
    members, *rest = points.shape

    def kernel(*refs):
        second_member_kernel(slot, *refs)

    return pl.pallas_call(
        kernel,
        out_shape=jax.ShapeDtypeStruct((members, 2, *rest), jnp.bfloat16),
        in_specs=[VMEM] * (2 + len(params)),
        out_specs=VMEM,
        compiler_params=LARGE,
        cost_estimate=cost(512, 1600000),
    )(points, done, *params)


def merge_rows(first_row, shifts, later, earlier):
    def kernel(*refs):
        merging_kernel(first_row, *refs)

    return pl.pallas_call(
        kernel,
        out_shape=jax.ShapeDtypeStruct(later.shape, jnp.bfloat16),
        in_specs=[SMEM, VMEM, VMEM],
        out_specs=VMEM,
    )(shifts, later, earlier)


def window_layer(window_below, shifts, region, kinds, *params):
    half, _, longitudes, features = region.shape

    def kernel(*refs):
        window_kernel(window_below, *refs)

    return pl.pallas_call(
        kernel,
        out_shape=[jax.ShapeDtypeStruct((half, longitudes, features), jnp.bfloat16)] * 2,
        in_specs=[SMEM, VMEM, pl.BlockSpec(memory_space=pl.ANY)] + [VMEM] * len(params),
        out_specs=[VMEM] * 2,
        scratch_shapes=[
            pltpu.VMEM((2, WIN, longitudes), jnp.int32),
            pltpu.SemaphoreType.DMA((2,)),
        ],
        compiler_params=LARGE,
        cost_estimate=cost(1024, 2000000),
    )(shifts, region, kinds, *params)


def on_device(
    ensemble,
    shifts,
    land_sea,
    member_gain,
    member_qkv,
    member_out,
    first_gain,
    first_in,
    first_out,
    window_gain,
    window_qkv,
    window_out,
    second_gain,
    second_in,
    second_out,
):
    _, rows, longitudes, features = ensemble.shape
    half = rows // 2
    spaces = lax.axis_size("space")
    up = [(i, (i + 1) % spaces) for i in range(spaces)]
    down = [(j, i) for i, j in up]
    gains = [g.reshape(1, features) for g in (member_gain, first_gain, window_gain, second_gain)]
    members_first = (gains[0], member_qkv, member_out, gains[1], first_in, first_out)
    windows_second = (gains[2], window_qkv, window_out, gains[3], second_in, second_out)

    def exchange(parts):
        return lax.all_to_all(parts, "member", split_axis=0, concat_axis=0, tiled=True)

    def run(window_below):
        low, high = lax.optimization_barrier((ensemble[0, :half], ensemble[0, half:]))
        settled, open_half = (high, low) if window_below else (low, high)
        other = lax.ppermute(open_half, "space", down if window_below else up)
        first = exchange(settled)
        if window_below:
            merged = merge_rows(0, shifts, open_half, other)
        else:
            merged = merge_rows(half, shifts, other, open_half)
        second = exchange(merged)
        first = first_member_layer(first, *members_first)
        mixed = second_member_layer(0 if window_below else 1, second, first, *members_first)
        region = exchange(mixed)
        low, high = window_layer(window_below, shifts, region, land_sea, *windows_second)
        if window_below:
            back = lax.ppermute(low, "space", up)
            return jnp.concatenate([merge_rows(0, shifts, low, back), high])
        back = lax.ppermute(high, "space", down)
        return jnp.concatenate([low, merge_rows(half, shifts, back, high)])

    out = lax.cond(shifts[0] <= half, lambda: run(True), lambda: run(False))
    return out[None]


def solution(mesh):
    return jax.shard_map(
        on_device,
        mesh=mesh,
        in_specs=(P("member", "space", None, None),) + (P(),) * 14,
        out_specs=P("member", "space", None, None),
        check_vma=False,
    )
```

```python
import math

import jax
import jax.numpy as jnp
from jax import lax
from jax.experimental import pallas as pl
from jax.experimental.pallas import tpu as pltpu
from jax.sharding import PartitionSpec as P

HEADS = 8
WIN = 16
EPSILON = 1e-05
BLOCK = 256
FAR = 1e30
VMEM = pl.BlockSpec(memory_space=pltpu.VMEM)
SMEM = pl.BlockSpec(memory_space=pltpu.SMEM)


def normalise(values, gains):
    center = jnp.mean(values, axis=-1, keepdims=True)
    shifted = values - center
    spread = jnp.mean(shifted * shifted, axis=-1, keepdims=True)
    return (shifted * lax.rsqrt(spread + EPSILON) * gains).astype(jnp.bfloat16)


def wide_dot(a, b):
    return jnp.dot(a, b, preferred_element_type=jnp.float32)


def twice_gelu(x):
    inner = x * (0.7978845608028654 + 0.035677408136300125 * (x * x))
    return (x + x * jnp.tanh(inner)).astype(jnp.bfloat16)


def feed_forward(stream, gain_ref, in_ref, out_ref):
    wide = stream.astype(jnp.float32)
    normed = normalise(wide, gain_ref[...])
    hidden_size = in_ref.shape[1]
    update = None
    for start in range(0, hidden_size, BLOCK):
        hidden = twice_gelu(wide_dot(normed, in_ref[:, start : start + BLOCK]))
        part = wide_dot(hidden, out_ref[start : start + BLOCK, :])
        update = part if update is None else update + part
    return (wide + 0.5 * update).astype(jnp.bfloat16)


def project(stream, gain_ref, qkv_ref):
    features = stream.shape[-1]
    normed = normalise(stream, gain_ref[...])
    scale = math.log2(math.e) / math.sqrt(features // HEADS)
    query = (wide_dot(normed, qkv_ref[:, :features]) * scale).astype(jnp.bfloat16)
    key = wide_dot(normed, qkv_ref[:, features : 2 * features]).astype(jnp.bfloat16)
    value = wide_dot(normed, qkv_ref[:, 2 * features :]).astype(jnp.bfloat16)
    return query, key, value


def attend_block(query, key, value, query_marks, key_marks):
    tokens, features = query.shape
    size = features // HEADS
    half = features // 2
    lane = lax.broadcasted_iota(jnp.int32, (1, features), 1)

    def head_lanes(first):
        return jnp.where((lane >= first) & (lane < first + size), 1.0, 0.0).astype(jnp.bfloat16)

    results = []
    for group in range(2):
        free = features - size if group == 0 else 0
        keys = key * (1.0 - head_lanes(free)).astype(jnp.bfloat16) + key_marks[group]
        total = None
        for h in range(group * HEADS // 2, (group + 1) * HEADS // 2):
            q = query * head_lanes(h * size) + query_marks[group]
            scores = lax.dot_general(
                q, keys, (((1,), (1,)), ((), ())), preferred_element_type=jnp.float32
            )
            top = jnp.max(scores, axis=-1, keepdims=True)
            weights = jnp.exp2(scores - top).astype(jnp.bfloat16)
            opposite = h * size + (half if group == 0 else -half)
            v = value * head_lanes(h * size) + head_lanes(opposite)
            part = wide_dot(weights, v)
            total = part if total is None else total + part
        if group == 0:
            results.append(total[:, :half] / total[:, half:])
        else:
            results.append(total[:, half:] / total[:, :half])
    return jnp.concatenate(results, axis=-1).astype(jnp.bfloat16)


def mix_members(x, gain_ref, qkv_ref, out_ref, gain2_ref, in2_ref, out2_ref):
    members, points, features = x.shape
    size = features // HEADS
    blocks = points // size
    x = x.astype(jnp.float32)
    stream = jnp.concatenate(
        [x[:, b * size : (b + 1) * size].reshape(members * size, features) for b in range(blocks)]
    )
    query, key, value = project(stream, gain_ref, qkv_ref)
    tokens = members * size
    lane = lax.broadcasted_iota(jnp.int32, (tokens, features), 1)
    point = lax.broadcasted_iota(jnp.int32, (tokens, features), 0) % size
    query_marks, key_marks = [], []
    for first in (features - size, 0):
        same = lane - first == point
        marked = (lane >= first) & (lane < first + size)
        query_marks.append(jnp.where(marked & ~same, -FAR, 0.0).astype(jnp.bfloat16))
        key_marks.append(jnp.where(same, 1.0, 0.0).astype(jnp.bfloat16))
    attended = []
    for b in range(blocks):
        at = slice(b * tokens, (b + 1) * tokens)
        attended.append(attend_block(query[at], key[at], value[at], query_marks, key_marks))
    attended = jnp.concatenate(attended)
    stream = (stream + wide_dot(attended, out_ref[...])).astype(jnp.bfloat16)
    result = feed_forward(stream, gain2_ref, in2_ref, out2_ref)
    result = [
        result[b * tokens : (b + 1) * tokens].reshape(members, size, features)
        for b in range(blocks)
    ]
    return jnp.concatenate(result, axis=1)


def first_member_kernel(x_ref, *refs):
    *params, o_ref = refs
    o_ref[...] = mix_members(x_ref[...], *params)


def second_member_kernel(slot, x_ref, done_ref, *refs):
    *params, o_ref = refs
    o_ref[:, 1 - slot] = done_ref[...]
    o_ref[:, slot] = mix_members(x_ref[...], *params)


def window_kernel(
    window_below,
    shifts_ref,
    x_ref,
    kinds_ref,
    gain_ref,
    qkv_ref,
    out_ref,
    gain2_ref,
    in2_ref,
    out2_ref,
    low_ref,
    high_ref,
    kinds_scratch,
    sems,
):
    half, longitudes, features = low_ref.shape
    windows = longitudes // WIN
    size = features // HEADS
    tokens = WIN * WIN
    lat_shift, lon_shift = shifts_ref[0], shifts_ref[1]
    space = lax.axis_index("space")
    spaces = kinds_ref.shape[0] // WIN
    if window_below:
        blocks = (space, lax.rem(space + 1, spaces))
    else:
        blocks = (lax.rem(space + spaces - 1, spaces), space)
    copies = [
        pltpu.make_async_copy(
            kinds_ref.at[pl.ds(pl.multiple_of(block * WIN, WIN), WIN)],
            kinds_scratch.at[n],
            sems.at[n],
        )
        for n, block in enumerate(blocks)
    ]
    for copy in copies:
        copy.start()

    column = lax.broadcasted_iota(jnp.int32, (WIN, WIN, features), 1)
    inside = column >= lon_shift
    tiles = [
        jnp.concatenate(
            [x_ref[:, part, w * WIN : (w + 1) * WIN, :] for part in range(2)]
        ).astype(jnp.float32)
        for w in range(windows)
    ]
    stream = jnp.concatenate(
        [
            jnp.where(inside, tiles[w], tiles[(w + 1) % windows]).reshape(tokens, features)
            for w in range(windows)
        ]
    )
    query, key, value = project(stream, gain_ref, qkv_ref)

    for copy in copies:
        copy.wait()
    row = lax.broadcasted_iota(jnp.int32, (WIN, longitudes), 0)
    kinds = jnp.where(row >= lat_shift, kinds_scratch[0], kinds_scratch[1]).astype(jnp.float32)
    kinds = jnp.broadcast_to(kinds[:, None, :], (WIN, WIN, longitudes))
    kind_column = lax.broadcasted_iota(jnp.int32, (WIN, WIN, longitudes), 1)
    kind_lane = lax.broadcasted_iota(jnp.int32, (WIN, WIN, longitudes), 2)

    lane = lax.broadcasted_iota(jnp.int32, (tokens, features), 1)
    attended = []
    for w in range(windows):
        at = slice(w * tokens, (w + 1) * tokens)
        wanted = kind_column + jnp.where(
            kind_column >= lon_shift, w * WIN, (w + 1) % windows * WIN
        )
        kind = jnp.where(kind_lane == wanted, kinds, 0.0).reshape(tokens, longitudes)
        kind = jnp.sum(kind, axis=-1, keepdims=True)
        query_marks, key_marks = [], []
        for first in (features - size, 0):
            here, following = lane == first, lane == first + 1
            query_marks.append(
                jnp.where(
                    here, -FAR * kind, jnp.where(following, -FAR * (1.0 - kind), 0.0)
                ).astype(jnp.bfloat16)
            )
            key_marks.append(
                jnp.where(here, 1.0 - kind, jnp.where(following, kind, 0.0)).astype(jnp.bfloat16)
            )
        attended.append(attend_block(query[at], key[at], value[at], query_marks, key_marks))
    attended = jnp.concatenate(attended)
    stream = (stream + wide_dot(attended, out_ref[...])).astype(jnp.bfloat16)
    result = feed_forward(stream, gain2_ref, in2_ref, out2_ref).astype(jnp.float32)
    result = result.reshape(windows, WIN, WIN, features)
    for w in range(windows):
        tile = jnp.where(inside, result[w], result[(w + windows - 1) % windows])
        tile = tile.astype(jnp.bfloat16)
        low_ref[:, w * WIN : (w + 1) * WIN, :] = tile[:half]
        high_ref[:, w * WIN : (w + 1) * WIN, :] = tile[half:]


def cost(tokens, flops_per_token):
    return pl.CostEstimate(
        flops=tokens * flops_per_token, bytes_accessed=3 * 2**20, transcendentals=tokens * 2048
    )


LARGE = pltpu.CompilerParams(vmem_limit_bytes=48 * 2**20)


def first_member_layer(points, *params):
    return pl.pallas_call(
        first_member_kernel,
        out_shape=jax.ShapeDtypeStruct(points.shape, jnp.bfloat16),
        in_specs=[VMEM] * (1 + len(params)),
        out_specs=VMEM,
        compiler_params=LARGE,
        cost_estimate=cost(512, 1600000),
    )(points, *params)


def second_member_layer(slot, points, done, *params):
    members, *rest = points.shape

    def kernel(*refs):
        second_member_kernel(slot, *refs)

    return pl.pallas_call(
        kernel,
        out_shape=jax.ShapeDtypeStruct((members, 2, *rest), jnp.bfloat16),
        in_specs=[VMEM] * (2 + len(params)),
        out_specs=VMEM,
        compiler_params=LARGE,
        cost_estimate=cost(512, 1600000),
    )(points, done, *params)


def window_layer(window_below, shifts, region, kinds, *params):
    half, _, longitudes, features = region.shape

    def kernel(*refs):
        window_kernel(window_below, *refs)

    return pl.pallas_call(
        kernel,
        out_shape=[jax.ShapeDtypeStruct((half, longitudes, features), jnp.bfloat16)] * 2,
        in_specs=[SMEM, VMEM, pl.BlockSpec(memory_space=pl.ANY)] + [VMEM] * len(params),
        out_specs=[VMEM] * 2,
        scratch_shapes=[
            pltpu.VMEM((2, WIN, longitudes), jnp.int32),
            pltpu.SemaphoreType.DMA((2,)),
        ],
        compiler_params=LARGE,
        cost_estimate=cost(1024, 2000000),
    )(shifts, region, kinds, *params)


def on_device(
    ensemble,
    shifts,
    land_sea,
    member_gain,
    member_qkv,
    member_out,
    first_gain,
    first_in,
    first_out,
    window_gain,
    window_qkv,
    window_out,
    second_gain,
    second_in,
    second_out,
):
    _, rows, longitudes, features = ensemble.shape
    half = rows // 2
    spaces = lax.axis_size("space")
    up = [(i, (i + 1) % spaces) for i in range(spaces)]
    down = [(j, i) for i, j in up]
    gains = [g.reshape(1, features) for g in (member_gain, first_gain, window_gain, second_gain)]
    members_first = (gains[0], member_qkv, member_out, gains[1], first_in, first_out)
    windows_second = (gains[2], window_qkv, window_out, gains[3], second_in, second_out)

    def exchange(parts):
        return lax.all_to_all(parts, "member", split_axis=0, concat_axis=0, tiled=True)

    row = jnp.arange(rows, dtype=jnp.int32)[:, None, None]
    lacking = jnp.minimum(shifts[0], rows - shifts[0])
    steps = [0, 2, 4, 6, 8]
    step = (lacking + 1) // 2

    def passed(array, count, pairs, at_start):
        if count == 0:
            return jnp.zeros_like(array)
        sent = array[:count] if at_start else array[half - count :]
        received = lax.ppermute(sent, "space", pairs)
        rest = jnp.zeros((half - count, longitudes, features), array.dtype)
        return jnp.concatenate([received, rest] if at_start else [rest, received])

    def run(window_below):
        ahead, back = (down, up) if window_below else (up, down)
        late = row[:half] >= shifts[0] if window_below else row[half:] >= shifts[0]
        low, high = ensemble[0, :half], ensemble[0, half:]
        settled, open_half = (high, low) if window_below else (low, high)

        def begin(count):
            other = passed(open_half, count, ahead, window_below)
            first = exchange(settled)
            pair = (open_half, other) if window_below else (other, open_half)
            return first, jnp.where(late, *pair)

        def end(count, result):
            other = passed(result, count, back, window_below)
            pair = (result, other) if window_below else (other, result)
            return jnp.where(late, *pair)

        first, merged = lax.switch(step, [lambda n=n: begin(n) for n in steps])
        second = exchange(merged)
        first = first_member_layer(first, *members_first)
        mixed = second_member_layer(0 if window_below else 1, second, first, *members_first)
        region = exchange(mixed)
        low, high = window_layer(window_below, shifts, region, land_sea, *windows_second)
        if window_below:
            low = lax.switch(step, [lambda n=n: end(n, low) for n in steps])
        else:
            high = lax.switch(step, [lambda n=n: end(n, high) for n in steps])
        return jnp.concatenate([low, high])

    out = lax.cond(shifts[0] <= half, lambda: run(True), lambda: run(False))
    return out[None]


def solution(mesh):
    return jax.shard_map(
        on_device,
        mesh=mesh,
        in_specs=(P("member", "space", None, None),) + (P(),) * 14,
        out_specs=P("member", "space", None, None),
        check_vma=False,
    )
```

```python
import math

import jax
import jax.numpy as jnp
from jax import lax
from jax.experimental import pallas as pl
from jax.experimental.pallas import tpu as pltpu
from jax.sharding import PartitionSpec as P

HEADS = 8
WIN = 16
EPSILON = 1e-05
BLOCK = 256
FAR = 1e30
VMEM = pl.BlockSpec(memory_space=pltpu.VMEM)
SMEM = pl.BlockSpec(memory_space=pltpu.SMEM)


def normalise(values, gains):
    center = jnp.mean(values, axis=-1, keepdims=True)
    shifted = values - center
    spread = jnp.mean(shifted * shifted, axis=-1, keepdims=True)
    return (shifted * lax.rsqrt(spread + EPSILON) * gains).astype(jnp.bfloat16)


def wide_dot(a, b):
    return jnp.dot(a, b, preferred_element_type=jnp.float32)


def twice_gelu(x):
    inner = x * (0.7978845608028654 + 0.035677408136300125 * (x * x))
    return (x + x * jnp.tanh(inner)).astype(jnp.bfloat16)


def feed_forward(stream, gain_ref, in_ref, out_ref):
    wide = stream.astype(jnp.float32)
    normed = normalise(wide, gain_ref[...])
    hidden_size = in_ref.shape[1]
    update = None
    for start in range(0, hidden_size, BLOCK):
        hidden = twice_gelu(wide_dot(normed, in_ref[:, start : start + BLOCK]))
        part = wide_dot(hidden, out_ref[start : start + BLOCK, :])
        update = part if update is None else update + part
    return (wide + 0.5 * update).astype(jnp.bfloat16)


def project(stream, gain_ref, qkv_ref):
    features = stream.shape[-1]
    normed = normalise(stream, gain_ref[...])
    scale = math.log2(math.e) / math.sqrt(features // HEADS)
    query = (wide_dot(normed, qkv_ref[:, :features]) * scale).astype(jnp.bfloat16)
    key = wide_dot(normed, qkv_ref[:, features : 2 * features]).astype(jnp.bfloat16)
    value = wide_dot(normed, qkv_ref[:, 2 * features :]).astype(jnp.bfloat16)
    return query, key, value


def attend_block(query, key, value, query_marks, key_marks):
    tokens, features = query.shape
    size = features // HEADS
    half = features // 2
    lane = lax.broadcasted_iota(jnp.int32, (1, features), 1)

    def head_lanes(first):
        return jnp.where((lane >= first) & (lane < first + size), 1.0, 0.0).astype(jnp.bfloat16)

    results = []
    for group in range(2):
        free = features - size if group == 0 else 0
        keys = key * (1.0 - head_lanes(free)).astype(jnp.bfloat16) + key_marks[group]
        total = None
        for h in range(group * HEADS // 2, (group + 1) * HEADS // 2):
            q = query * head_lanes(h * size) + query_marks[group]
            scores = lax.dot_general(
                q, keys, (((1,), (1,)), ((), ())), preferred_element_type=jnp.float32
            )
            top = jnp.max(scores, axis=-1, keepdims=True)
            weights = jnp.exp2(scores - top).astype(jnp.bfloat16)
            opposite = h * size + (half if group == 0 else -half)
            v = value * head_lanes(h * size) + head_lanes(opposite)
            part = wide_dot(weights, v)
            total = part if total is None else total + part
        if group == 0:
            results.append(total[:, :half] / total[:, half:])
        else:
            results.append(total[:, half:] / total[:, :half])
    return jnp.concatenate(results, axis=-1).astype(jnp.bfloat16)


def mix_members(x, gain_ref, qkv_ref, out_ref, gain2_ref, in2_ref, out2_ref):
    members, points, features = x.shape
    size = features // HEADS
    blocks = points // size
    x = x.astype(jnp.float32)
    stream = jnp.concatenate(
        [x[:, b * size : (b + 1) * size].reshape(members * size, features) for b in range(blocks)]
    )
    query, key, value = project(stream, gain_ref, qkv_ref)
    tokens = members * size
    lane = lax.broadcasted_iota(jnp.int32, (tokens, features), 1)
    point = lax.broadcasted_iota(jnp.int32, (tokens, features), 0) % size
    query_marks, key_marks = [], []
    for first in (features - size, 0):
        same = lane - first == point
        marked = (lane >= first) & (lane < first + size)
        query_marks.append(jnp.where(marked & ~same, -FAR, 0.0).astype(jnp.bfloat16))
        key_marks.append(jnp.where(same, 1.0, 0.0).astype(jnp.bfloat16))
    attended = []
    for b in range(blocks):
        at = slice(b * tokens, (b + 1) * tokens)
        attended.append(attend_block(query[at], key[at], value[at], query_marks, key_marks))
    attended = jnp.concatenate(attended)
    stream = (stream + wide_dot(attended, out_ref[...])).astype(jnp.bfloat16)
    result = feed_forward(stream, gain2_ref, in2_ref, out2_ref)
    result = [
        result[b * tokens : (b + 1) * tokens].reshape(members, size, features)
        for b in range(blocks)
    ]
    return jnp.concatenate(result, axis=1)


def member_kernel(x_ref, *refs):
    *params, o_ref = refs
    o_ref[...] = mix_members(x_ref[...], *params)


def window_kernel(
    shifts_ref,
    x_ref,
    kinds_ref,
    gain_ref,
    qkv_ref,
    out_ref,
    gain2_ref,
    in2_ref,
    out2_ref,
    o_ref,
    kinds_scratch,
    sems,
):
    rows, longitudes, features = o_ref.shape
    windows = longitudes // WIN
    size = features // HEADS
    tokens = WIN * WIN
    lat_shift, lon_shift = shifts_ref[0], shifts_ref[1]
    space = lax.axis_index("space")
    spaces = kinds_ref.shape[0] // WIN
    behind = jnp.where(lat_shift <= rows // 2, spaces, spaces - 1)
    block = lax.rem(space + behind, spaces)
    blocks = (block, lax.rem(block + 1, spaces))
    copies = [
        pltpu.make_async_copy(
            kinds_ref.at[pl.ds(pl.multiple_of(block * WIN, WIN), WIN)],
            kinds_scratch.at[n],
            sems.at[n],
        )
        for n, block in enumerate(blocks)
    ]
    for copy in copies:
        copy.start()

    column = lax.broadcasted_iota(jnp.int32, (WIN, WIN, features), 1)
    inside = column >= lon_shift
    tiles = [x_ref[:, w * WIN : (w + 1) * WIN, :].astype(jnp.float32) for w in range(windows)]
    stream = jnp.concatenate(
        [
            jnp.where(inside, tiles[w], tiles[(w + 1) % windows]).reshape(tokens, features)
            for w in range(windows)
        ]
    )
    query, key, value = project(stream, gain_ref, qkv_ref)

    for copy in copies:
        copy.wait()
    row = lax.broadcasted_iota(jnp.int32, (WIN, longitudes), 0)
    kinds = jnp.where(row >= lat_shift, kinds_scratch[0], kinds_scratch[1]).astype(jnp.float32)
    kinds = jnp.broadcast_to(kinds[:, None, :], (WIN, WIN, longitudes))
    kind_column = lax.broadcasted_iota(jnp.int32, (WIN, WIN, longitudes), 1)
    kind_lane = lax.broadcasted_iota(jnp.int32, (WIN, WIN, longitudes), 2)

    lane = lax.broadcasted_iota(jnp.int32, (tokens, features), 1)
    attended = []
    for w in range(windows):
        at = slice(w * tokens, (w + 1) * tokens)
        wanted = kind_column + jnp.where(
            kind_column >= lon_shift, w * WIN, (w + 1) % windows * WIN
        )
        kind = jnp.where(kind_lane == wanted, kinds, 0.0).reshape(tokens, longitudes)
        kind = jnp.sum(kind, axis=-1, keepdims=True)
        query_marks, key_marks = [], []
        for first in (features - size, 0):
            here, following = lane == first, lane == first + 1
            query_marks.append(
                jnp.where(
                    here, -FAR * kind, jnp.where(following, -FAR * (1.0 - kind), 0.0)
                ).astype(jnp.bfloat16)
            )
            key_marks.append(
                jnp.where(here, 1.0 - kind, jnp.where(following, kind, 0.0)).astype(jnp.bfloat16)
            )
        attended.append(attend_block(query[at], key[at], value[at], query_marks, key_marks))
    attended = jnp.concatenate(attended)
    stream = (stream + wide_dot(attended, out_ref[...])).astype(jnp.bfloat16)
    result = feed_forward(stream, gain2_ref, in2_ref, out2_ref).astype(jnp.float32)
    result = result.reshape(windows, WIN, WIN, features)
    for w in range(windows):
        tile = jnp.where(inside, result[w], result[(w + windows - 1) % windows])
        o_ref[:, w * WIN : (w + 1) * WIN, :] = tile.astype(jnp.bfloat16)


def cost(tokens, flops_per_token):
    return pl.CostEstimate(
        flops=tokens * flops_per_token, bytes_accessed=3 * 2**20, transcendentals=tokens * 2048
    )


LARGE = pltpu.CompilerParams(vmem_limit_bytes=48 * 2**20)


def member_layer(points, *params):
    return pl.pallas_call(
        member_kernel,
        out_shape=jax.ShapeDtypeStruct(points.shape, jnp.bfloat16),
        in_specs=[VMEM] * (1 + len(params)),
        out_specs=VMEM,
        compiler_params=LARGE,
        cost_estimate=cost(1024, 1600000),
    )(points, *params)


def window_layer(shifts, region, kinds, *params):
    return pl.pallas_call(
        window_kernel,
        out_shape=jax.ShapeDtypeStruct(region.shape, jnp.bfloat16),
        in_specs=[SMEM, VMEM, pl.BlockSpec(memory_space=pl.ANY)] + [VMEM] * len(params),
        out_specs=VMEM,
        scratch_shapes=[
            pltpu.VMEM((2, WIN, region.shape[1]), jnp.int32),
            pltpu.SemaphoreType.DMA((2,)),
        ],
        compiler_params=LARGE,
        cost_estimate=cost(1024, 2000000),
    )(shifts, region, kinds, *params)


def on_device(
    ensemble,
    shifts,
    land_sea,
    member_gain,
    member_qkv,
    member_out,
    first_gain,
    first_in,
    first_out,
    window_gain,
    window_qkv,
    window_out,
    second_gain,
    second_in,
    second_out,
):
    _, rows, longitudes, features = ensemble.shape
    half = rows // 2
    members = lax.axis_size("member")
    spaces = lax.axis_size("space")
    up = [(i, (i + 1) % spaces) for i in range(spaces)]
    down = [(j, i) for i, j in up]
    gains = [g.reshape(1, features) for g in (member_gain, first_gain, window_gain, second_gain)]
    members_first = (gains[0], member_qkv, member_out, gains[1], first_in, first_out)
    windows_second = (gains[2], window_qkv, window_out, gains[3], second_in, second_out)

    def exchange(parts):
        return lax.all_to_all(parts, "member", split_axis=0, concat_axis=0, tiled=True)

    def assembled(shift, own):
        if shift <= half:
            other = lax.ppermute(own[:shift], "space", down) if shift else own[:0]
            return jnp.concatenate([other, own[shift:]])
        return jnp.concatenate([own[:shift], lax.ppermute(own[shift:], "space", up)])

    def returned(shift, result):
        if shift <= half:
            mine = lax.ppermute(result[:shift], "space", up) if shift else result[:0]
            return jnp.concatenate([mine, result[shift:]])
        return jnp.concatenate([result[:shift], lax.ppermute(result[shift:], "space", down)])

    region = lax.switch(
        shifts[0], [lambda x, n=n: assembled(n, x) for n in range(rows)], ensemble[0]
    )
    points = exchange(region.reshape(members, -1, features))
    points = member_layer(points, *members_first)
    region = exchange(points).reshape(rows, longitudes, features)
    result = window_layer(shifts, region, land_sea, *windows_second)
    out = lax.switch(shifts[0], [lambda x, n=n: returned(n, x) for n in range(rows)], result)
    return out[None]


def solution(mesh):
    return jax.shard_map(
        on_device,
        mesh=mesh,
        in_specs=(P("member", "space", None, None),) + (P(),) * 14,
        out_specs=P("member", "space", None, None),
        check_vma=False,
    )
```

```python
import math

import jax
import jax.numpy as jnp
from jax import lax
from jax.experimental import pallas as pl
from jax.experimental.pallas import tpu as pltpu
from jax.sharding import PartitionSpec as P

HEADS = 8
WIN = 16
EPSILON = 1e-05
BLOCK = 256
FAR = 1e30
VMEM = pl.BlockSpec(memory_space=pltpu.VMEM)
SMEM = pl.BlockSpec(memory_space=pltpu.SMEM)


def normalise(values, gains):
    center = jnp.mean(values, axis=-1, keepdims=True)
    shifted = values - center
    spread = jnp.mean(shifted * shifted, axis=-1, keepdims=True)
    return (shifted * lax.rsqrt(spread + EPSILON) * gains).astype(jnp.bfloat16)


def wide_dot(a, b):
    return jnp.dot(a, b, preferred_element_type=jnp.float32)


def twice_gelu(x):
    inner = x * (0.7978845608028654 + 0.035677408136300125 * (x * x))
    return (x + x * jnp.tanh(inner)).astype(jnp.bfloat16)


def feed_forward(stream, gain_ref, in_ref, out_ref):
    wide = stream.astype(jnp.float32)
    normed = normalise(wide, gain_ref[...])
    hidden_size = in_ref.shape[1]
    update = None
    for start in range(0, hidden_size, BLOCK):
        hidden = twice_gelu(wide_dot(normed, in_ref[:, start : start + BLOCK]))
        part = wide_dot(hidden, out_ref[start : start + BLOCK, :])
        update = part if update is None else update + part
    return (wide + 0.5 * update).astype(jnp.bfloat16)


def project(stream, gain_ref, qkv_ref):
    features = stream.shape[-1]
    normed = normalise(stream, gain_ref[...])
    scale = math.log2(math.e) / math.sqrt(features // HEADS)
    query = (wide_dot(normed, qkv_ref[:, :features]) * scale).astype(jnp.bfloat16)
    key = wide_dot(normed, qkv_ref[:, features : 2 * features]).astype(jnp.bfloat16)
    value = wide_dot(normed, qkv_ref[:, 2 * features :]).astype(jnp.bfloat16)
    return query, key, value


def attend_block(query, key, value, query_marks, key_marks):
    tokens, features = query.shape
    size = features // HEADS
    half = features // 2
    lane = lax.broadcasted_iota(jnp.int32, (1, features), 1)

    def head_lanes(first):
        return jnp.where((lane >= first) & (lane < first + size), 1.0, 0.0).astype(jnp.bfloat16)

    results = []
    for group in range(2):
        free = features - size if group == 0 else 0
        keys = key * (1.0 - head_lanes(free)).astype(jnp.bfloat16) + key_marks[group]
        total = None
        for h in range(group * HEADS // 2, (group + 1) * HEADS // 2):
            q = query * head_lanes(h * size) + query_marks[group]
            scores = lax.dot_general(
                q, keys, (((1,), (1,)), ((), ())), preferred_element_type=jnp.float32
            )
            top = jnp.max(scores, axis=-1, keepdims=True)
            weights = jnp.exp2(scores - top).astype(jnp.bfloat16)
            opposite = h * size + (half if group == 0 else -half)
            v = value * head_lanes(h * size) + head_lanes(opposite)
            part = wide_dot(weights, v)
            total = part if total is None else total + part
        if group == 0:
            results.append(total[:, :half] / total[:, half:])
        else:
            results.append(total[:, half:] / total[:, :half])
    return jnp.concatenate(results, axis=-1).astype(jnp.bfloat16)


def mix_members(x, gain_ref, qkv_ref, out_ref, gain2_ref, in2_ref, out2_ref):
    members, points, features = x.shape
    size = features // HEADS
    blocks = points // size
    x = x.astype(jnp.float32)
    stream = jnp.concatenate(
        [x[:, b * size : (b + 1) * size].reshape(members * size, features) for b in range(blocks)]
    )
    query, key, value = project(stream, gain_ref, qkv_ref)
    tokens = members * size
    lane = lax.broadcasted_iota(jnp.int32, (tokens, features), 1)
    point = lax.broadcasted_iota(jnp.int32, (tokens, features), 0) % size
    query_marks, key_marks = [], []
    for first in (features - size, 0):
        same = lane - first == point
        marked = (lane >= first) & (lane < first + size)
        query_marks.append(jnp.where(marked & ~same, -FAR, 0.0).astype(jnp.bfloat16))
        key_marks.append(jnp.where(same, 1.0, 0.0).astype(jnp.bfloat16))
    attended = []
    for b in range(blocks):
        at = slice(b * tokens, (b + 1) * tokens)
        attended.append(attend_block(query[at], key[at], value[at], query_marks, key_marks))
    attended = jnp.concatenate(attended)
    stream = (stream + wide_dot(attended, out_ref[...])).astype(jnp.bfloat16)
    result = feed_forward(stream, gain2_ref, in2_ref, out2_ref)
    result = [
        result[b * tokens : (b + 1) * tokens].reshape(members, size, features)
        for b in range(blocks)
    ]
    return jnp.concatenate(result, axis=1)


def member_kernel(x_ref, *refs):
    *params, o_ref = refs
    o_ref[...] = mix_members(x_ref[...], *params)


def window_kernel(
    shifts_ref,
    x_ref,
    kinds_ref,
    gain_ref,
    qkv_ref,
    out_ref,
    gain2_ref,
    in2_ref,
    out2_ref,
    o_ref,
    kinds_scratch,
    sems,
):
    rows, longitudes, features = o_ref.shape
    windows = longitudes // WIN
    size = features // HEADS
    tokens = WIN * WIN
    lat_shift, lon_shift = shifts_ref[0], shifts_ref[1]
    space = lax.axis_index("space")
    spaces = kinds_ref.shape[0] // WIN
    behind = jnp.where(lat_shift <= rows // 2, spaces, spaces - 1)
    block = lax.rem(space + behind, spaces)
    blocks = (block, lax.rem(block + 1, spaces))
    copies = [
        pltpu.make_async_copy(
            kinds_ref.at[pl.ds(pl.multiple_of(block * WIN, WIN), WIN)],
            kinds_scratch.at[n],
            sems.at[n],
        )
        for n, block in enumerate(blocks)
    ]
    for copy in copies:
        copy.start()

    column = lax.broadcasted_iota(jnp.int32, (WIN, WIN, features), 1)
    inside = column >= lon_shift
    tiles = [x_ref[:, w * WIN : (w + 1) * WIN, :].astype(jnp.float32) for w in range(windows)]
    stream = jnp.concatenate(
        [
            jnp.where(inside, tiles[w], tiles[(w + 1) % windows]).reshape(tokens, features)
            for w in range(windows)
        ]
    )
    query, key, value = project(stream, gain_ref, qkv_ref)

    for copy in copies:
        copy.wait()
    row = lax.broadcasted_iota(jnp.int32, (WIN, longitudes), 0)
    kinds = jnp.where(row >= lat_shift, kinds_scratch[0], kinds_scratch[1]).astype(jnp.float32)
    kinds = jnp.broadcast_to(kinds[:, None, :], (WIN, WIN, longitudes))
    kind_column = lax.broadcasted_iota(jnp.int32, (WIN, WIN, longitudes), 1)
    kind_lane = lax.broadcasted_iota(jnp.int32, (WIN, WIN, longitudes), 2)

    lane = lax.broadcasted_iota(jnp.int32, (tokens, features), 1)
    attended = []
    for w in range(windows):
        at = slice(w * tokens, (w + 1) * tokens)
        wanted = kind_column + jnp.where(
            kind_column >= lon_shift, w * WIN, (w + 1) % windows * WIN
        )
        kind = jnp.where(kind_lane == wanted, kinds, 0.0).reshape(tokens, longitudes)
        kind = jnp.sum(kind, axis=-1, keepdims=True)
        query_marks, key_marks = [], []
        for first in (features - size, 0):
            here, following = lane == first, lane == first + 1
            query_marks.append(
                jnp.where(
                    here, -FAR * kind, jnp.where(following, -FAR * (1.0 - kind), 0.0)
                ).astype(jnp.bfloat16)
            )
            key_marks.append(
                jnp.where(here, 1.0 - kind, jnp.where(following, kind, 0.0)).astype(jnp.bfloat16)
            )
        attended.append(attend_block(query[at], key[at], value[at], query_marks, key_marks))
    attended = jnp.concatenate(attended)
    stream = (stream + wide_dot(attended, out_ref[...])).astype(jnp.bfloat16)
    result = feed_forward(stream, gain2_ref, in2_ref, out2_ref).astype(jnp.float32)
    result = result.reshape(windows, WIN, WIN, features)
    for w in range(windows):
        tile = jnp.where(inside, result[w], result[(w + windows - 1) % windows])
        o_ref[:, w * WIN : (w + 1) * WIN, :] = tile.astype(jnp.bfloat16)


def cost(tokens, flops_per_token):
    return pl.CostEstimate(
        flops=tokens * flops_per_token, bytes_accessed=3 * 2**20, transcendentals=tokens * 2048
    )


LARGE = pltpu.CompilerParams(vmem_limit_bytes=48 * 2**20)


def member_layer(points, *params):
    return pl.pallas_call(
        member_kernel,
        out_shape=jax.ShapeDtypeStruct(points.shape, jnp.bfloat16),
        in_specs=[VMEM] * (1 + len(params)),
        out_specs=VMEM,
        compiler_params=LARGE,
        cost_estimate=cost(1024, 1600000),
    )(points, *params)


def window_layer(shifts, region, kinds, *params):
    return pl.pallas_call(
        window_kernel,
        out_shape=jax.ShapeDtypeStruct(region.shape, jnp.bfloat16),
        in_specs=[SMEM, VMEM, pl.BlockSpec(memory_space=pl.ANY)] + [VMEM] * len(params),
        out_specs=VMEM,
        scratch_shapes=[
            pltpu.VMEM((2, WIN, region.shape[1]), jnp.int32),
            pltpu.SemaphoreType.DMA((2,)),
        ],
        compiler_params=LARGE,
        cost_estimate=cost(1024, 2000000),
    )(shifts, region, kinds, *params)


def on_device(
    ensemble,
    shifts,
    land_sea,
    member_gain,
    member_qkv,
    member_out,
    first_gain,
    first_in,
    first_out,
    window_gain,
    window_qkv,
    window_out,
    second_gain,
    second_in,
    second_out,
):
    _, rows, longitudes, features = ensemble.shape
    half = rows // 2
    members = lax.axis_size("member")
    spaces = lax.axis_size("space")
    up = [(i, (i + 1) % spaces) for i in range(spaces)]
    down = [(j, i) for i, j in up]
    gains = [g.reshape(1, features) for g in (member_gain, first_gain, window_gain, second_gain)]
    members_first = (gains[0], member_qkv, member_out, gains[1], first_in, first_out)
    windows_second = (gains[2], window_qkv, window_out, gains[3], second_in, second_out)

    def exchange(parts):
        return lax.all_to_all(parts, "member", split_axis=0, concat_axis=0, tiled=True)

    shift = shifts[0]
    classes = range(half + 1)

    def assembled(k, own):
        if k == 0:
            return own
        if 2 * k <= half:
            n = 2 * k
            other = lax.ppermute(own[:n], "space", down)
            last = jnp.where(shift == n, other[n - 1 :], own[n - 1 : n])
            return jnp.concatenate([other[: n - 1], last, own[n:]])
        n = 2 * k - 1
        other = lax.ppermute(own[n:], "space", up)
        first = jnp.where(shift == n, other[:1], own[n : n + 1])
        return jnp.concatenate([own[:n], first, other[1:]])

    def returned(k, result):
        if k == 0:
            return result
        if 2 * k <= half:
            n = 2 * k
            other = lax.ppermute(result[:n], "space", up)
            last = jnp.where(shift == n, other[n - 1 :], result[n - 1 : n])
            return jnp.concatenate([other[: n - 1], last, result[n:]])
        n = 2 * k - 1
        other = lax.ppermute(result[n:], "space", down)
        first = jnp.where(shift == n, other[:1], result[n : n + 1])
        return jnp.concatenate([result[:n], first, other[1:]])

    which = lax.shift_right_logical(shift + 1, 1)
    region = lax.switch(which, [lambda x, k=k: assembled(k, x) for k in classes], ensemble[0])
    points = exchange(region.reshape(members, -1, features))
    points = member_layer(points, *members_first)
    region = exchange(points).reshape(rows, longitudes, features)
    result = window_layer(shifts, region, land_sea, *windows_second)
    out = lax.switch(which, [lambda x, k=k: returned(k, x) for k in classes], result)
    return out[None]


def solution(mesh):
    return jax.shard_map(
        on_device,
        mesh=mesh,
        in_specs=(P("member", "space", None, None),) + (P(),) * 14,
        out_specs=P("member", "space", None, None),
        check_vma=False,
    )
```

```python
import math

import jax
import jax.numpy as jnp
from jax import lax
from jax.experimental import pallas as pl
from jax.experimental.pallas import tpu as pltpu
from jax.sharding import PartitionSpec as P

HEADS = 8
WIN = 16
EPSILON = 1e-05
BLOCK = 256
FAR = 1e30
VMEM = pl.BlockSpec(memory_space=pltpu.VMEM)
SMEM = pl.BlockSpec(memory_space=pltpu.SMEM)


def normalise(values, gains):
    center = jnp.mean(values, axis=-1, keepdims=True)
    shifted = values - center
    spread = jnp.mean(shifted * shifted, axis=-1, keepdims=True)
    return (shifted * lax.rsqrt(spread + EPSILON) * gains).astype(jnp.bfloat16)


def wide_dot(a, b):
    return jnp.dot(a, b, preferred_element_type=jnp.float32)


def twice_gelu(x):
    inner = x * (0.7978845608028654 + 0.035677408136300125 * (x * x))
    return (x + x * jnp.tanh(inner)).astype(jnp.bfloat16)


def feed_forward(stream, gain_ref, in_ref, out_ref):
    wide = stream.astype(jnp.float32)
    normed = normalise(wide, gain_ref[...])
    hidden_size = in_ref.shape[1]
    update = None
    for start in range(0, hidden_size, BLOCK):
        hidden = twice_gelu(wide_dot(normed, in_ref[:, start : start + BLOCK]))
        part = wide_dot(hidden, out_ref[start : start + BLOCK, :])
        update = part if update is None else update + part
    return (wide + 0.5 * update).astype(jnp.bfloat16)


def project(stream, gain_ref, qkv_ref):
    features = stream.shape[-1]
    normed = normalise(stream, gain_ref[...])
    scale = math.log2(math.e) / math.sqrt(features // HEADS)
    query = (wide_dot(normed, qkv_ref[:, :features]) * scale).astype(jnp.bfloat16)
    key = wide_dot(normed, qkv_ref[:, features : 2 * features]).astype(jnp.bfloat16)
    value = wide_dot(normed, qkv_ref[:, 2 * features :]).astype(jnp.bfloat16)
    return query, key, value


def attend_block(query, key, value, query_marks, key_marks):
    tokens, features = query.shape
    size = features // HEADS
    half = features // 2
    lane = lax.broadcasted_iota(jnp.int32, (1, features), 1)

    def head_lanes(first):
        return jnp.where((lane >= first) & (lane < first + size), 1.0, 0.0).astype(jnp.bfloat16)

    results = []
    for group in range(2):
        free = features - size if group == 0 else 0
        keys = key * (1.0 - head_lanes(free)).astype(jnp.bfloat16) + key_marks[group]
        total = None
        for h in range(group * HEADS // 2, (group + 1) * HEADS // 2):
            q = query * head_lanes(h * size) + query_marks[group]
            scores = lax.dot_general(
                q, keys, (((1,), (1,)), ((), ())), preferred_element_type=jnp.float32
            )
            top = jnp.max(scores, axis=-1, keepdims=True)
            weights = jnp.exp2(scores - top).astype(jnp.bfloat16)
            opposite = h * size + (half if group == 0 else -half)
            v = value * head_lanes(h * size) + head_lanes(opposite)
            part = wide_dot(weights, v)
            total = part if total is None else total + part
        if group == 0:
            results.append(total[:, :half] / total[:, half:])
        else:
            results.append(total[:, half:] / total[:, :half])
    return jnp.concatenate(results, axis=-1).astype(jnp.bfloat16)


def mix_members(x, gain_ref, qkv_ref, out_ref, gain2_ref, in2_ref, out2_ref):
    members, points, features = x.shape
    size = features // HEADS
    blocks = points // size
    x = x.astype(jnp.float32)
    stream = jnp.concatenate(
        [x[:, b * size : (b + 1) * size].reshape(members * size, features) for b in range(blocks)]
    )
    query, key, value = project(stream, gain_ref, qkv_ref)
    tokens = members * size
    lane = lax.broadcasted_iota(jnp.int32, (tokens, features), 1)
    point = lax.broadcasted_iota(jnp.int32, (tokens, features), 0) % size
    query_marks, key_marks = [], []
    for first in (features - size, 0):
        same = lane - first == point
        marked = (lane >= first) & (lane < first + size)
        query_marks.append(jnp.where(marked & ~same, -FAR, 0.0).astype(jnp.bfloat16))
        key_marks.append(jnp.where(same, 1.0, 0.0).astype(jnp.bfloat16))
    attended = []
    for b in range(blocks):
        at = slice(b * tokens, (b + 1) * tokens)
        attended.append(attend_block(query[at], key[at], value[at], query_marks, key_marks))
    attended = jnp.concatenate(attended)
    stream = (stream + wide_dot(attended, out_ref[...])).astype(jnp.bfloat16)
    result = feed_forward(stream, gain2_ref, in2_ref, out2_ref)
    result = [
        result[b * tokens : (b + 1) * tokens].reshape(members, size, features)
        for b in range(blocks)
    ]
    return jnp.concatenate(result, axis=1)


def first_member_kernel(x_ref, *refs):
    *params, o_ref = refs
    o_ref[...] = mix_members(x_ref[...], *params)


def second_member_kernel(shifts_ref, x_ref, done_ref, *refs):
    *params, o_ref = refs
    slot = jnp.where(shifts_ref[0] <= WIN // 2, 0, 1)
    o_ref[:, 1 - slot] = done_ref[...]
    o_ref[:, slot] = mix_members(x_ref[...], *params)


def window_kernel(
    shifts_ref,
    x_ref,
    kinds_ref,
    gain_ref,
    qkv_ref,
    out_ref,
    gain2_ref,
    in2_ref,
    out2_ref,
    o_ref,
    kinds_scratch,
    sems,
):
    rows, longitudes, features = o_ref.shape
    windows = longitudes // WIN
    size = features // HEADS
    tokens = WIN * WIN
    lat_shift, lon_shift = shifts_ref[0], shifts_ref[1]
    space = lax.axis_index("space")
    spaces = kinds_ref.shape[0] // WIN
    behind = jnp.where(lat_shift <= rows // 2, spaces, spaces - 1)
    block = lax.rem(space + behind, spaces)
    blocks = (block, lax.rem(block + 1, spaces))
    copies = [
        pltpu.make_async_copy(
            kinds_ref.at[pl.ds(pl.multiple_of(block * WIN, WIN), WIN)],
            kinds_scratch.at[n],
            sems.at[n],
        )
        for n, block in enumerate(blocks)
    ]
    for copy in copies:
        copy.start()

    column = lax.broadcasted_iota(jnp.int32, (WIN, WIN, features), 1)
    inside = column >= lon_shift
    tiles = [
        jnp.concatenate(
            [x_ref[:, part, w * WIN : (w + 1) * WIN, :] for part in range(2)]
        ).astype(jnp.float32)
        for w in range(windows)
    ]
    stream = jnp.concatenate(
        [
            jnp.where(inside, tiles[w], tiles[(w + 1) % windows]).reshape(tokens, features)
            for w in range(windows)
        ]
    )
    query, key, value = project(stream, gain_ref, qkv_ref)

    for copy in copies:
        copy.wait()
    row = lax.broadcasted_iota(jnp.int32, (WIN, longitudes), 0)
    kinds = jnp.where(row >= lat_shift, kinds_scratch[0], kinds_scratch[1]).astype(jnp.float32)
    kinds = jnp.broadcast_to(kinds[:, None, :], (WIN, WIN, longitudes))
    kind_column = lax.broadcasted_iota(jnp.int32, (WIN, WIN, longitudes), 1)
    kind_lane = lax.broadcasted_iota(jnp.int32, (WIN, WIN, longitudes), 2)

    lane = lax.broadcasted_iota(jnp.int32, (tokens, features), 1)
    attended = []
    for w in range(windows):
        at = slice(w * tokens, (w + 1) * tokens)
        wanted = kind_column + jnp.where(
            kind_column >= lon_shift, w * WIN, (w + 1) % windows * WIN
        )
        kind = jnp.where(kind_lane == wanted, kinds, 0.0).reshape(tokens, longitudes)
        kind = jnp.sum(kind, axis=-1, keepdims=True)
        query_marks, key_marks = [], []
        for first in (features - size, 0):
            here, following = lane == first, lane == first + 1
            query_marks.append(
                jnp.where(
                    here, -FAR * kind, jnp.where(following, -FAR * (1.0 - kind), 0.0)
                ).astype(jnp.bfloat16)
            )
            key_marks.append(
                jnp.where(here, 1.0 - kind, jnp.where(following, kind, 0.0)).astype(jnp.bfloat16)
            )
        attended.append(attend_block(query[at], key[at], value[at], query_marks, key_marks))
    attended = jnp.concatenate(attended)
    stream = (stream + wide_dot(attended, out_ref[...])).astype(jnp.bfloat16)
    result = feed_forward(stream, gain2_ref, in2_ref, out2_ref).astype(jnp.float32)
    result = result.reshape(windows, WIN, WIN, features)
    for w in range(windows):
        tile = jnp.where(inside, result[w], result[(w + windows - 1) % windows])
        o_ref[:, w * WIN : (w + 1) * WIN, :] = tile.astype(jnp.bfloat16)


def cost(tokens, flops_per_token):
    return pl.CostEstimate(
        flops=tokens * flops_per_token, bytes_accessed=3 * 2**20, transcendentals=tokens * 2048
    )


LARGE = pltpu.CompilerParams(vmem_limit_bytes=48 * 2**20)


def first_member_layer(points, *params):
    return pl.pallas_call(
        first_member_kernel,
        out_shape=jax.ShapeDtypeStruct(points.shape, jnp.bfloat16),
        in_specs=[VMEM] * (1 + len(params)),
        out_specs=VMEM,
        compiler_params=LARGE,
        cost_estimate=cost(512, 1600000),
    )(points, *params)


def second_member_layer(shifts, points, done, *params):
    members, *rest = points.shape
    return pl.pallas_call(
        second_member_kernel,
        out_shape=jax.ShapeDtypeStruct((members, 2, *rest), jnp.bfloat16),
        in_specs=[SMEM] + [VMEM] * (2 + len(params)),
        out_specs=VMEM,
        compiler_params=LARGE,
        cost_estimate=cost(512, 1600000),
    )(shifts, points, done, *params)


def window_layer(shifts, region, kinds, *params):
    half, _, longitudes, features = region.shape
    return pl.pallas_call(
        window_kernel,
        out_shape=jax.ShapeDtypeStruct((2 * half, longitudes, features), jnp.bfloat16),
        in_specs=[SMEM, VMEM, pl.BlockSpec(memory_space=pl.ANY)] + [VMEM] * len(params),
        out_specs=VMEM,
        scratch_shapes=[
            pltpu.VMEM((2, WIN, longitudes), jnp.int32),
            pltpu.SemaphoreType.DMA((2,)),
        ],
        compiler_params=LARGE,
        cost_estimate=cost(1024, 2000000),
    )(shifts, region, kinds, *params)


def on_device(
    ensemble,
    shifts,
    land_sea,
    member_gain,
    member_qkv,
    member_out,
    first_gain,
    first_in,
    first_out,
    window_gain,
    window_qkv,
    window_out,
    second_gain,
    second_in,
    second_out,
):
    _, rows, longitudes, features = ensemble.shape
    half = rows // 2
    spaces = lax.axis_size("space")
    up = [(i, (i + 1) % spaces) for i in range(spaces)]
    down = [(j, i) for i, j in up]
    gains = [g.reshape(1, features) for g in (member_gain, first_gain, window_gain, second_gain)]
    members_first = (gains[0], member_qkv, member_out, gains[1], first_in, first_out)
    windows_second = (gains[2], window_qkv, window_out, gains[3], second_in, second_out)

    def exchange(parts):
        return lax.all_to_all(parts, "member", split_axis=0, concat_axis=0, tiled=True)

    shift = shifts[0]
    classes = range(half + 1)

    def assembled(k, own):
        if k == 0:
            return own[:half]
        if 2 * k <= half:
            n = 2 * k
            other = lax.ppermute(own[:n], "space", down)
            last = jnp.where(shift == n, other[n - 1 :], own[n - 1 : n])
            return jnp.concatenate([other[: n - 1], last, own[n:half]])
        n = 2 * k - 1
        other = lax.ppermute(own[n:], "space", up)
        first = jnp.where(shift == n, other[:1], own[n : n + 1])
        return jnp.concatenate([own[half:n], first, other[1:]])

    def returned(k, result):
        if k == 0:
            return result
        if 2 * k <= half:
            n = 2 * k
            other = lax.ppermute(result[:n], "space", up)
            last = jnp.where(shift == n, other[n - 1 :], result[n - 1 : n])
            return jnp.concatenate([other[: n - 1], last, result[n:]])
        n = 2 * k - 1
        other = lax.ppermute(result[n:], "space", down)
        first = jnp.where(shift == n, other[:1], result[n : n + 1])
        return jnp.concatenate([result[:n], first, other[1:]])

    which = lax.shift_right_logical(shift + 1, 1)
    own = ensemble[0]
    settled = exchange(jnp.where(shift <= half, own[half:], own[:half]))
    merged = lax.switch(which, [lambda x, k=k: assembled(k, x) for k in classes], own)
    merged = exchange(merged)
    settled = first_member_layer(settled, *members_first)
    region = exchange(second_member_layer(shifts, merged, settled, *members_first))
    result = window_layer(shifts, region, land_sea, *windows_second)
    out = lax.switch(which, [lambda x, k=k: returned(k, x) for k in classes], result)
    return out[None]


def solution(mesh):
    return jax.shard_map(
        on_device,
        mesh=mesh,
        in_specs=(P("member", "space", None, None),) + (P(),) * 14,
        out_specs=P("member", "space", None, None),
        check_vma=False,
    )
```

```python
import math

import jax
import jax.numpy as jnp
from jax import lax
from jax.experimental import pallas as pl
from jax.experimental.pallas import tpu as pltpu
from jax.sharding import PartitionSpec as P

HEADS = 8
WIN = 16
EPSILON = 1e-05
BLOCK = 256
FAR = 1e30
VMEM = pl.BlockSpec(memory_space=pltpu.VMEM)
SMEM = pl.BlockSpec(memory_space=pltpu.SMEM)


def normalise(values, gains):
    center = jnp.mean(values, axis=-1, keepdims=True)
    shifted = values - center
    spread = jnp.mean(shifted * shifted, axis=-1, keepdims=True)
    return (shifted * lax.rsqrt(spread + EPSILON) * gains).astype(jnp.bfloat16)


def wide_dot(a, b):
    return jnp.dot(a, b, preferred_element_type=jnp.float32)


def twice_gelu(x):
    inner = x * (0.7978845608028654 + 0.035677408136300125 * (x * x))
    return (x + x * jnp.tanh(inner)).astype(jnp.bfloat16)


def feed_forward(stream, gains, in_ref, out_ref):
    wide = stream.astype(jnp.float32)
    normed = normalise(wide, gains)
    hidden_size = in_ref.shape[1]
    update = None
    for start in range(0, hidden_size, BLOCK):
        hidden = twice_gelu(wide_dot(normed, in_ref[:, start : start + BLOCK]))
        part = wide_dot(hidden, out_ref[start : start + BLOCK, :])
        update = part if update is None else update + part
    return (wide + 0.5 * update).astype(jnp.bfloat16)


def project(stream, gains, qkv_ref):
    features = stream.shape[-1]
    normed = normalise(stream, gains)
    scale = math.log2(math.e) / math.sqrt(features // HEADS)
    query = (wide_dot(normed, qkv_ref[:, :features]) * scale).astype(jnp.bfloat16)
    key = wide_dot(normed, qkv_ref[:, features : 2 * features]).astype(jnp.bfloat16)
    value = wide_dot(normed, qkv_ref[:, 2 * features :]).astype(jnp.bfloat16)
    return query, key, value


def attend_block(query, key, value, query_marks, key_marks):
    tokens, features = query.shape
    size = features // HEADS
    lane = lax.broadcasted_iota(jnp.int32, (1, features), 1)

    def head_lanes(first):
        return jnp.where((lane >= first) & (lane < first + size), 1.0, 0.0).astype(jnp.bfloat16)

    values = value.astype(jnp.float32).T.astype(jnp.bfloat16)
    ones = jnp.ones((16, tokens), jnp.bfloat16)
    results = []
    for group in range(2):
        free = features - size if group == 0 else 0
        queries = query * (1.0 - head_lanes(free)).astype(jnp.bfloat16) + query_marks[group]
        for h in range(group * HEADS // 2, (group + 1) * HEADS // 2):
            keys = key * head_lanes(h * size) + key_marks[group]
            scores = lax.dot_general(
                keys, queries, (((1,), (1,)), ((), ())), preferred_element_type=jnp.float32
            )
            top = jnp.max(scores, axis=0, keepdims=True)
            weights = jnp.exp2(scores - top).astype(jnp.bfloat16)
            total = wide_dot(
                jnp.concatenate([values[h * size : (h + 1) * size], ones]), weights
            )
            results.append(total[:size] / total[size : size + 1])
    return jnp.concatenate(results).T.astype(jnp.bfloat16)


def fetch(refs, buffers, sems):
    copies = [
        pltpu.make_async_copy(ref, buffers.at[n], sems.at[n]) for n, ref in enumerate(refs)
    ]
    for copy in copies:
        copy.start()
    return copies


def member_kernel(
    x_ref,
    gain_ref,
    qkv_ref,
    out_ref,
    gain2_ref,
    in2_ref,
    out2_ref,
    o_ref,
    gains_scratch,
    gains_sems,
):
    gain_copies = fetch((gain_ref, gain2_ref), gains_scratch, gains_sems)
    members, points, features = x_ref.shape
    size = features // HEADS
    blocks = points // size
    x = x_ref[...].astype(jnp.float32)
    stream = jnp.concatenate(
        [x[:, b * size : (b + 1) * size].reshape(members * size, features) for b in range(blocks)]
    )
    for copy in gain_copies:
        copy.wait()
    query, key, value = project(stream, gains_scratch[0], qkv_ref)
    tokens = members * size
    lane = lax.broadcasted_iota(jnp.int32, (tokens, features), 1)
    point = lax.broadcasted_iota(jnp.int32, (tokens, features), 0) % size
    query_marks, key_marks = [], []
    for first in (features - size, 0):
        same = lane - first == point
        marked = (lane >= first) & (lane < first + size)
        query_marks.append(jnp.where(marked & ~same, -FAR, 0.0).astype(jnp.bfloat16))
        key_marks.append(jnp.where(same, 1.0, 0.0).astype(jnp.bfloat16))
    attended = []
    for b in range(blocks):
        at = slice(b * tokens, (b + 1) * tokens)
        attended.append(attend_block(query[at], key[at], value[at], query_marks, key_marks))
    attended = jnp.concatenate(attended)
    stream = (stream + wide_dot(attended, out_ref[...])).astype(jnp.bfloat16)
    result = feed_forward(stream, gains_scratch[1], in2_ref, out2_ref)
    result = [
        result[b * tokens : (b + 1) * tokens].reshape(members, size, features)
        for b in range(blocks)
    ]
    o_ref[...] = jnp.concatenate(result, axis=1)


def window_kernel(
    shifts_ref,
    x_ref,
    kinds_ref,
    gain_ref,
    qkv_ref,
    out_ref,
    gain2_ref,
    in2_ref,
    out2_ref,
    o_ref,
    gains_scratch,
    gains_sems,
):
    gain_copies = fetch((gain_ref, gain2_ref), gains_scratch, gains_sems)
    rows, longitudes, features = o_ref.shape
    windows = longitudes // WIN
    size = features // HEADS
    tokens = WIN * WIN
    lat_shift, lon_shift = shifts_ref[0], shifts_ref[1]
    space = lax.axis_index("space")
    spaces = kinds_ref.shape[1] // WIN
    behind = jnp.where(lat_shift <= rows // 2, spaces, spaces - 1)
    block = lax.rem(space + behind, spaces)

    def block_rows(block):
        whole = lax.div(block * WIN, 128)
        part = kinds_ref[:, pl.ds(pl.multiple_of(whole * 128, 128), 128)].astype(jnp.float32)
        return pltpu.roll(part, lax.rem(128 - (block * WIN - whole * 128), 128), 1)

    lane = lax.broadcasted_iota(jnp.int32, (longitudes, 128), 1)
    kinds = jnp.where(
        lane >= lat_shift, block_rows(block), block_rows(lax.rem(block + 1, spaces))
    )
    kinds = jnp.concatenate([kinds] * (128 // longitudes)).T[:WIN]

    column = lax.broadcasted_iota(jnp.int32, (WIN, WIN, features), 1)
    inside = column >= lon_shift
    tiles = [x_ref[:, w * WIN : (w + 1) * WIN, :].astype(jnp.float32) for w in range(windows)]
    stream = jnp.concatenate(
        [
            jnp.where(inside, tiles[w], tiles[(w + 1) % windows]).reshape(tokens, features)
            for w in range(windows)
        ]
    )
    for copy in gain_copies:
        copy.wait()
    query, key, value = project(stream, gains_scratch[0], qkv_ref)

    kinds = jnp.broadcast_to(kinds[:, None, :], (WIN, WIN, 128))
    kind_column = lax.broadcasted_iota(jnp.int32, (WIN, WIN, 128), 1)
    kind_lane = lax.broadcasted_iota(jnp.int32, (WIN, WIN, 128), 2)

    lane = lax.broadcasted_iota(jnp.int32, (tokens, features), 1)
    attended = []
    for w in range(windows):
        at = slice(w * tokens, (w + 1) * tokens)
        wanted = kind_column + jnp.where(
            kind_column >= lon_shift, w * WIN, (w + 1) % windows * WIN
        )
        kind = jnp.where(kind_lane == wanted, kinds, 0.0).reshape(tokens, 128)
        kind = jnp.sum(kind, axis=-1, keepdims=True)
        query_marks, key_marks = [], []
        for first in (features - size, 0):
            here, following = lane == first, lane == first + 1
            query_marks.append(
                jnp.where(
                    here, -FAR * kind, jnp.where(following, -FAR * (1.0 - kind), 0.0)
                ).astype(jnp.bfloat16)
            )
            key_marks.append(
                jnp.where(here, 1.0 - kind, jnp.where(following, kind, 0.0)).astype(jnp.bfloat16)
            )
        attended.append(attend_block(query[at], key[at], value[at], query_marks, key_marks))
    attended = jnp.concatenate(attended)
    stream = (stream + wide_dot(attended, out_ref[...])).astype(jnp.bfloat16)
    result = feed_forward(stream, gains_scratch[1], in2_ref, out2_ref).astype(jnp.float32)
    result = result.reshape(windows, WIN, WIN, features)
    for w in range(windows):
        tile = jnp.where(inside, result[w], result[(w + windows - 1) % windows])
        o_ref[:, w * WIN : (w + 1) * WIN, :] = tile.astype(jnp.bfloat16)


def cost(tokens, flops_per_token):
    return pl.CostEstimate(
        flops=tokens * flops_per_token, bytes_accessed=3 * 2**20, transcendentals=tokens * 2048
    )


ANY = pl.BlockSpec(memory_space=pl.ANY)
PARAMS = (ANY, VMEM, VMEM, ANY, VMEM, VMEM)
GAINS = [pltpu.VMEM((2, 1, 256), jnp.float32), pltpu.SemaphoreType.DMA((2,))]
LARGE = pltpu.CompilerParams(vmem_limit_bytes=48 * 2**20)


def member_layer(points, *params):
    return pl.pallas_call(
        member_kernel,
        out_shape=jax.ShapeDtypeStruct(points.shape, jnp.bfloat16),
        in_specs=[VMEM, *PARAMS],
        out_specs=VMEM,
        scratch_shapes=GAINS,
        compiler_params=LARGE,
        cost_estimate=cost(1024, 1600000),
    )(points, *params)


def window_layer(shifts, region, kinds, *params):
    return pl.pallas_call(
        window_kernel,
        out_shape=jax.ShapeDtypeStruct(region.shape, jnp.bfloat16),
        in_specs=[SMEM, VMEM, VMEM, *PARAMS],
        out_specs=VMEM,
        scratch_shapes=GAINS,
        compiler_params=LARGE,
        cost_estimate=cost(1024, 2000000),
    )(shifts, region, kinds, *params)


def on_device(
    ensemble,
    shifts,
    land_sea,
    member_gain,
    member_qkv,
    member_out,
    first_gain,
    first_in,
    first_out,
    window_gain,
    window_qkv,
    window_out,
    second_gain,
    second_in,
    second_out,
):
    _, rows, longitudes, features = ensemble.shape
    half = rows // 2
    members = lax.axis_size("member")
    spaces = lax.axis_size("space")
    up = [(i, (i + 1) % spaces) for i in range(spaces)]
    down = [(j, i) for i, j in up]
    gains = [g.reshape(1, features) for g in (member_gain, first_gain, window_gain, second_gain)]
    members_first = (gains[0], member_qkv, member_out, gains[1], first_in, first_out)
    windows_second = (gains[2], window_qkv, window_out, gains[3], second_in, second_out)

    def exchange(parts):
        return lax.all_to_all(parts, "member", split_axis=0, concat_axis=0, tiled=True)

    shift = shifts[0]
    classes = range(half + 1)

    def assembled(k, own):
        if k == 0:
            return own
        if 2 * k <= half:
            n = 2 * k
            other = lax.ppermute(own[:n], "space", down)
            last = jnp.where(shift == n, other[n - 1 :], own[n - 1 : n])
            return jnp.concatenate([other[: n - 1], last, own[n:]])
        n = 2 * k - 1
        other = lax.ppermute(own[n:], "space", up)
        first = jnp.where(shift == n, other[:1], own[n : n + 1])
        return jnp.concatenate([own[:n], first, other[1:]])

    def returned(k, result):
        if k == 0:
            return result
        if 2 * k <= half:
            n = 2 * k
            other = lax.ppermute(result[:n], "space", up)
            last = jnp.where(shift == n, other[n - 1 :], result[n - 1 : n])
            return jnp.concatenate([other[: n - 1], last, result[n:]])
        n = 2 * k - 1
        other = lax.ppermute(result[n:], "space", down)
        first = jnp.where(shift == n, other[:1], result[n : n + 1])
        return jnp.concatenate([result[:n], first, other[1:]])

    which = lax.shift_right_logical(shift + 1, 1)
    region = lax.switch(which, [lambda x, k=k: assembled(k, x) for k in classes], ensemble[0])
    points = exchange(region.reshape(members, -1, features))
    points = member_layer(points, *members_first)
    region = exchange(points).reshape(rows, longitudes, features)
    result = window_layer(shifts, region, land_sea.T, *windows_second)
    out = lax.switch(which, [lambda x, k=k: returned(k, x) for k in classes], result)
    return out[None]


def solution(mesh):
    return jax.shard_map(
        on_device,
        mesh=mesh,
        in_specs=(P("member", "space", None, None),) + (P(),) * 14,
        out_specs=P("member", "space", None, None),
        check_vma=False,
    )
```

```python
import math

import jax
import jax.numpy as jnp
from jax import lax
from jax.experimental import pallas as pl
from jax.experimental.pallas import tpu as pltpu
from jax.sharding import PartitionSpec as P

HEADS = 8
WIN = 16
EPSILON = 1e-05
FAR = 1e30
VMEM = pl.BlockSpec(memory_space=pltpu.VMEM)
SMEM = pl.BlockSpec(memory_space=pltpu.SMEM)


def normalise(values, gains):
    center = jnp.mean(values, axis=-1, keepdims=True)
    shifted = values - center
    spread = jnp.mean(shifted * shifted, axis=-1, keepdims=True)
    return (shifted * lax.rsqrt(spread + EPSILON) * gains).astype(jnp.bfloat16)


def wide_dot(a, b):
    return jnp.dot(a, b, preferred_element_type=jnp.float32)


def twice_gelu(x):
    inner = x * (0.7978845608028654 + 0.035677408136300125 * (x * x))
    return (x + x * jnp.tanh(inner)).astype(jnp.bfloat16)


def feed_forward(stream, gains, in_ref, out_ref):
    wide = stream.astype(jnp.float32)
    normed = normalise(wide, gains)
    hidden = twice_gelu(wide_dot(normed, in_ref[...]))
    update = wide_dot(hidden, out_ref[...])
    return (wide + 0.5 * update).astype(jnp.bfloat16)


def project(stream, gains, qkv_ref):
    features = stream.shape[-1]
    normed = normalise(stream, gains)
    scale = math.log2(math.e) / math.sqrt(features // HEADS)
    query = (wide_dot(normed, qkv_ref[:, :features]) * scale).astype(jnp.bfloat16)
    key = wide_dot(normed, qkv_ref[:, features : 2 * features]).astype(jnp.bfloat16)
    value = wide_dot(normed, qkv_ref[:, 2 * features :]).astype(jnp.bfloat16)
    return query, key, value


def attend_block(query, key, value, query_marks, key_marks):
    tokens, features = query.shape
    size = features // HEADS
    half = features // 2
    lane = lax.broadcasted_iota(jnp.int32, (1, features), 1)

    def head_lanes(first):
        return jnp.where((lane >= first) & (lane < first + size), 1.0, 0.0).astype(jnp.bfloat16)

    results = []
    for group in range(2):
        free = features - size if group == 0 else 0
        heads = range(group * HEADS // 2, (group + 1) * HEADS // 2)
        keys = key * (1.0 - head_lanes(free)).astype(jnp.bfloat16) + key_marks[group]
        queries = jnp.concatenate(
            [query * head_lanes(h * size) + query_marks[group] for h in heads]
        )
        scores = lax.dot_general(
            queries, keys, (((1,), (1,)), ((), ())), preferred_element_type=jnp.float32
        )
        top = jnp.max(scores, axis=-1, keepdims=True)
        weights = jnp.exp2(scores - top).astype(jnp.bfloat16)
        weights = [weights[n * tokens : (n + 1) * tokens] for n in range(len(heads))]
        opposite = half if group == 0 else -half
        values = [value * head_lanes(h * size) + head_lanes(h * size + opposite) for h in heads]
        total = wide_dot(jnp.concatenate(weights, axis=1), jnp.concatenate(values))
        if group == 0:
            results.append(total[:, :half] / total[:, half:])
        else:
            results.append(total[:, half:] / total[:, :half])
    return jnp.concatenate(results, axis=-1).astype(jnp.bfloat16)


def member_kernel(
    x_ref, gains_ref, qkv_ref, out_ref, in2_ref, out2_ref, o_ref
):
    members, points, features = x_ref.shape
    size = features // HEADS
    blocks = points // size
    x = x_ref[...].astype(jnp.float32)
    stream = jnp.concatenate(
        [x[:, b * size : (b + 1) * size].reshape(members * size, features) for b in range(blocks)]
    )
    query, key, value = project(stream, gains_ref[0:1], qkv_ref)
    tokens = members * size
    lane = lax.broadcasted_iota(jnp.int32, (tokens, features), 1)
    point = lax.broadcasted_iota(jnp.int32, (tokens, features), 0) % size
    query_marks, key_marks = [], []
    for first in (features - size, 0):
        same = lane - first == point
        marked = (lane >= first) & (lane < first + size)
        query_marks.append(jnp.where(marked & ~same, -FAR, 0.0).astype(jnp.bfloat16))
        key_marks.append(jnp.where(same, 1.0, 0.0).astype(jnp.bfloat16))
    attended = []
    for b in range(blocks):
        at = slice(b * tokens, (b + 1) * tokens)
        attended.append(attend_block(query[at], key[at], value[at], query_marks, key_marks))
    attended = jnp.concatenate(attended)
    stream = (stream + wide_dot(attended, out_ref[...])).astype(jnp.bfloat16)
    result = feed_forward(stream, gains_ref[1:2], in2_ref, out2_ref)
    result = [
        result[b * tokens : (b + 1) * tokens].reshape(members, size, features)
        for b in range(blocks)
    ]
    o_ref[...] = jnp.concatenate(result, axis=1)


def window_kernel(
    shifts_ref,
    x_ref,
    kinds_ref,
    gains_ref,
    qkv_ref,
    out_ref,
    in2_ref,
    out2_ref,
    o_ref,
):
    rows, longitudes, features = o_ref.shape
    windows = longitudes // WIN
    size = features // HEADS
    tokens = WIN * WIN
    lat_shift, lon_shift = shifts_ref[0], shifts_ref[1]
    space = lax.axis_index("space")
    spaces = kinds_ref.shape[1] // WIN
    behind = jnp.where(lat_shift <= rows // 2, spaces, spaces - 1)
    block = lax.rem(space + behind, spaces)

    def block_rows(block):
        whole = lax.div(block * WIN, 128)
        part = kinds_ref[:, pl.ds(pl.multiple_of(whole * 128, 128), 128)].astype(jnp.float32)
        return pltpu.roll(part, lax.rem(128 - (block * WIN - whole * 128), 128), 1)

    lane = lax.broadcasted_iota(jnp.int32, (longitudes, 128), 1)
    kinds = jnp.where(
        lane >= lat_shift, block_rows(block), block_rows(lax.rem(block + 1, spaces))
    )
    kinds = jnp.concatenate([kinds] * (128 // longitudes)).T[:WIN]

    column = lax.broadcasted_iota(jnp.int32, (WIN, WIN, features), 1)
    inside = column >= lon_shift
    tiles = [x_ref[:, w * WIN : (w + 1) * WIN, :].astype(jnp.float32) for w in range(windows)]
    stream = jnp.concatenate(
        [
            jnp.where(inside, tiles[w], tiles[(w + 1) % windows]).reshape(tokens, features)
            for w in range(windows)
        ]
    )
    query, key, value = project(stream, gains_ref[2:3], qkv_ref)

    kinds = jnp.broadcast_to(kinds[:, None, :], (WIN, WIN, 128))
    kind_column = lax.broadcasted_iota(jnp.int32, (WIN, WIN, 128), 1)
    kind_lane = lax.broadcasted_iota(jnp.int32, (WIN, WIN, 128), 2)

    lane = lax.broadcasted_iota(jnp.int32, (tokens, features), 1)
    attended = []
    for w in range(windows):
        at = slice(w * tokens, (w + 1) * tokens)
        wanted = kind_column + jnp.where(
            kind_column >= lon_shift, w * WIN, (w + 1) % windows * WIN
        )
        kind = jnp.where(kind_lane == wanted, kinds, 0.0).reshape(tokens, 128)
        kind = jnp.sum(kind, axis=-1, keepdims=True)
        query_marks, key_marks = [], []
        for first in (features - size, 0):
            here, following = lane == first, lane == first + 1
            query_marks.append(
                jnp.where(
                    here, -FAR * kind, jnp.where(following, -FAR * (1.0 - kind), 0.0)
                ).astype(jnp.bfloat16)
            )
            key_marks.append(
                jnp.where(here, 1.0 - kind, jnp.where(following, kind, 0.0)).astype(jnp.bfloat16)
            )
        attended.append(attend_block(query[at], key[at], value[at], query_marks, key_marks))
    attended = jnp.concatenate(attended)
    stream = (stream + wide_dot(attended, out_ref[...])).astype(jnp.bfloat16)
    result = feed_forward(stream, gains_ref[3:4], in2_ref, out2_ref).astype(jnp.float32)
    result = result.reshape(windows, WIN, WIN, features)
    for w in range(windows):
        tile = jnp.where(inside, result[w], result[(w + windows - 1) % windows])
        o_ref[:, w * WIN : (w + 1) * WIN, :] = tile.astype(jnp.bfloat16)


def cost(tokens, flops_per_token):
    return pl.CostEstimate(
        flops=tokens * flops_per_token, bytes_accessed=3 * 2**20, transcendentals=tokens * 2048
    )


LARGE = pltpu.CompilerParams(vmem_limit_bytes=48 * 2**20)


def member_layer(points, *params):
    return pl.pallas_call(
        member_kernel,
        out_shape=jax.ShapeDtypeStruct(points.shape, jnp.bfloat16),
        in_specs=[VMEM] * (1 + len(params)),
        out_specs=VMEM,
        compiler_params=LARGE,
        cost_estimate=cost(1024, 1600000),
    )(points, *params)


def window_layer(shifts, region, kinds, *params):
    return pl.pallas_call(
        window_kernel,
        out_shape=jax.ShapeDtypeStruct(region.shape, jnp.bfloat16),
        in_specs=[SMEM] + [VMEM] * (2 + len(params)),
        out_specs=VMEM,
        compiler_params=LARGE,
        cost_estimate=cost(1024, 2000000),
    )(shifts, region, kinds, *params)


def on_device(
    ensemble,
    shifts,
    land_sea,
    member_gain,
    member_qkv,
    member_out,
    first_gain,
    first_in,
    first_out,
    window_gain,
    window_qkv,
    window_out,
    second_gain,
    second_in,
    second_out,
):
    _, rows, longitudes, features = ensemble.shape
    half = rows // 2
    members = lax.axis_size("member")
    spaces = lax.axis_size("space")
    up = [(i, (i + 1) % spaces) for i in range(spaces)]
    down = [(j, i) for i, j in up]
    gains = (member_gain, first_gain, window_gain, second_gain)
    members_first = (member_qkv, member_out, first_in, first_out)
    windows_second = (window_qkv, window_out, second_in, second_out)

    def exchange(parts):
        return lax.all_to_all(parts, "member", split_axis=0, concat_axis=0, tiled=True)

    shift = shifts[0]
    classes = range(half + 1)

    def assembled(k, own):
        if k == 0:
            return own
        if 2 * k <= half:
            n = 2 * k
            other = lax.ppermute(own[:n], "space", down)
            last = jnp.where(shift == n, other[n - 1 :], own[n - 1 : n])
            return jnp.concatenate([other[: n - 1], last, own[n:]])
        n = 2 * k - 1
        other = lax.ppermute(own[n:], "space", up)
        first = jnp.where(shift == n, other[:1], own[n : n + 1])
        return jnp.concatenate([own[:n], first, other[1:]])

    def returned(k, result):
        if k == 0:
            return result
        if 2 * k <= half:
            n = 2 * k
            other = lax.ppermute(result[:n], "space", up)
            last = jnp.where(shift == n, other[n - 1 :], result[n - 1 : n])
            return jnp.concatenate([other[: n - 1], last, result[n:]])
        n = 2 * k - 1
        other = lax.ppermute(result[n:], "space", down)
        first = jnp.where(shift == n, other[:1], result[n : n + 1])
        return jnp.concatenate([result[:n], first, other[1:]])

    which = lax.shift_right_logical(shift + 1, 1)
    def begin(k, own, *vectors):
        return assembled(k, own), lax.optimization_barrier(jnp.stack(vectors))

    region, gains = lax.switch(
        which, [lambda *x, k=k: begin(k, *x) for k in classes], ensemble[0], *gains
    )
    points = exchange(region.reshape(members, -1, features))
    points = member_layer(points, gains, *members_first)
    region = exchange(points).reshape(rows, longitudes, features)
    result = window_layer(shifts, region, land_sea.T, gains, *windows_second)
    out = lax.switch(which, [lambda x, k=k: returned(k, x) for k in classes], result)
    return out[None]


def solution(mesh):
    return jax.shard_map(
        on_device,
        mesh=mesh,
        in_specs=(P("member", "space", None, None),) + (P(),) * 14,
        out_specs=P("member", "space", None, None),
        check_vma=False,
    )
```

```python
import math

import jax
import jax.numpy as jnp
from jax import lax
from jax.experimental import pallas as pl
from jax.experimental.pallas import tpu as pltpu
from jax.sharding import PartitionSpec as P

HEADS = 8
WIN = 16
EPSILON = 1e-05
FAR = 1e30
VMEM = pl.BlockSpec(memory_space=pltpu.VMEM)
SMEM = pl.BlockSpec(memory_space=pltpu.SMEM)


def normalise(values, gains):
    center = jnp.mean(values, axis=-1, keepdims=True)
    shifted = values - center
    spread = jnp.mean(shifted * shifted, axis=-1, keepdims=True)
    return (shifted * lax.rsqrt(spread + EPSILON) * gains).astype(jnp.bfloat16)


def wide_dot(a, b):
    return jnp.dot(a, b, preferred_element_type=jnp.float32)


def twice_gelu(x):
    inner = x * (0.7978845608028654 + 0.035677408136300125 * (x * x))
    return (x + x * jnp.tanh(inner)).astype(jnp.bfloat16)


def feed_forward(stream, gains, in_ref, out_ref):
    wide = stream.astype(jnp.float32)
    normed = normalise(wide, gains)
    hidden = twice_gelu(wide_dot(normed, in_ref[...]))
    update = wide_dot(hidden, out_ref[...])
    return (wide + 0.5 * update).astype(jnp.bfloat16)


def project(stream, gains, qkv_ref):
    features = stream.shape[-1]
    normed = normalise(stream, gains)
    scale = math.log2(math.e) / math.sqrt(features // HEADS)
    query = (wide_dot(normed, qkv_ref[:, :features]) * scale).astype(jnp.bfloat16)
    key = wide_dot(normed, qkv_ref[:, features : 2 * features]).astype(jnp.bfloat16)
    value = wide_dot(normed, qkv_ref[:, 2 * features :]).astype(jnp.bfloat16)
    return query, key, value


def attend_block(query, key, value, query_marks, key_marks):
    tokens, features = query.shape
    size = features // HEADS
    half = features // 2
    lane = lax.broadcasted_iota(jnp.int32, (1, features), 1)

    def head_lanes(first):
        return jnp.where((lane >= first) & (lane < first + size), 1.0, 0.0).astype(jnp.bfloat16)

    results = []
    for group in range(2):
        free = features - size if group == 0 else 0
        heads = range(group * HEADS // 2, (group + 1) * HEADS // 2)
        keys = key * (1.0 - head_lanes(free)).astype(jnp.bfloat16) + key_marks[group]
        queries = jnp.concatenate(
            [query * head_lanes(h * size) + query_marks[group] for h in heads]
        )
        scores = lax.dot_general(
            queries, keys, (((1,), (1,)), ((), ())), preferred_element_type=jnp.float32
        )
        top = jnp.max(scores, axis=-1, keepdims=True)
        weights = jnp.exp2(scores - top).astype(jnp.bfloat16)
        weights = [weights[n * tokens : (n + 1) * tokens] for n in range(len(heads))]
        opposite = half if group == 0 else -half
        values = [value * head_lanes(h * size) + head_lanes(h * size + opposite) for h in heads]
        total = wide_dot(jnp.concatenate(weights, axis=1), jnp.concatenate(values))
        if group == 0:
            results.append(total[:, :half] / total[:, half:])
        else:
            results.append(total[:, half:] / total[:, :half])
    return jnp.concatenate(results, axis=-1).astype(jnp.bfloat16)


def settled_kernel(shifts_ref, x_ref, o_ref):
    half = o_ref.shape[0]
    first = jnp.where(shifts_ref[0] <= half, half, 0)
    o_ref[...] = x_ref[pl.ds(first, half)]


def mix_members(x_ref, gains_ref, qkv_ref, out_ref, in2_ref, out2_ref):
    members, points, features = x_ref.shape
    size = features // HEADS
    blocks = points // size
    x = x_ref[...].astype(jnp.float32)
    stream = jnp.concatenate(
        [x[:, b * size : (b + 1) * size].reshape(members * size, features) for b in range(blocks)]
    )
    query, key, value = project(stream, gains_ref[0:1], qkv_ref)
    tokens = members * size
    lane = lax.broadcasted_iota(jnp.int32, (tokens, features), 1)
    point = lax.broadcasted_iota(jnp.int32, (tokens, features), 0) % size
    query_marks, key_marks = [], []
    for first in (features - size, 0):
        same = lane - first == point
        marked = (lane >= first) & (lane < first + size)
        query_marks.append(jnp.where(marked & ~same, -FAR, 0.0).astype(jnp.bfloat16))
        key_marks.append(jnp.where(same, 1.0, 0.0).astype(jnp.bfloat16))
    attended = []
    for b in range(blocks):
        at = slice(b * tokens, (b + 1) * tokens)
        attended.append(attend_block(query[at], key[at], value[at], query_marks, key_marks))
    attended = jnp.concatenate(attended)
    stream = (stream + wide_dot(attended, out_ref[...])).astype(jnp.bfloat16)
    result = feed_forward(stream, gains_ref[1:2], in2_ref, out2_ref)
    result = [
        result[b * tokens : (b + 1) * tokens].reshape(members, size, features)
        for b in range(blocks)
    ]
    return jnp.concatenate(result, axis=1)


def settled_member_kernel(*refs):
    *args, o_ref = refs
    o_ref[...] = mix_members(*args)


def open_member_kernel(done_ref, *refs):
    *args, o_ref = refs
    o_ref[:, 0] = done_ref[...]
    o_ref[:, 1] = mix_members(*args)


def window_kernel(
    shifts_ref,
    x_ref,
    kinds_ref,
    gains_ref,
    qkv_ref,
    out_ref,
    in2_ref,
    out2_ref,
    o_ref,
):
    rows, longitudes, features = o_ref.shape
    windows = longitudes // WIN
    size = features // HEADS
    tokens = WIN * WIN
    lat_shift, lon_shift = shifts_ref[0], shifts_ref[1]
    space = lax.axis_index("space")
    spaces = kinds_ref.shape[1] // WIN
    behind = jnp.where(lat_shift <= rows // 2, spaces, spaces - 1)
    block = lax.rem(space + behind, spaces)

    def block_rows(block):
        whole = lax.div(block * WIN, 128)
        part = kinds_ref[:, pl.ds(pl.multiple_of(whole * 128, 128), 128)].astype(jnp.float32)
        return pltpu.roll(part, lax.rem(128 - (block * WIN - whole * 128), 128), 1)

    lane = lax.broadcasted_iota(jnp.int32, (longitudes, 128), 1)
    kinds = jnp.where(
        lane >= lat_shift, block_rows(block), block_rows(lax.rem(block + 1, spaces))
    )
    kinds = jnp.concatenate([kinds] * (128 // longitudes)).T[:WIN]

    column = lax.broadcasted_iota(jnp.int32, (WIN, WIN, features), 1)
    inside = column >= lon_shift
    low = jnp.where(lat_shift <= rows // 2, 1, 0)
    tiles = [
        jnp.concatenate(
            [x_ref[:, part, w * WIN : (w + 1) * WIN, :] for part in (low, 1 - low)]
        ).astype(jnp.float32)
        for w in range(windows)
    ]
    stream = jnp.concatenate(
        [
            jnp.where(inside, tiles[w], tiles[(w + 1) % windows]).reshape(tokens, features)
            for w in range(windows)
        ]
    )
    query, key, value = project(stream, gains_ref[2:3], qkv_ref)

    kinds = jnp.broadcast_to(kinds[:, None, :], (WIN, WIN, 128))
    kind_column = lax.broadcasted_iota(jnp.int32, (WIN, WIN, 128), 1)
    kind_lane = lax.broadcasted_iota(jnp.int32, (WIN, WIN, 128), 2)

    lane = lax.broadcasted_iota(jnp.int32, (tokens, features), 1)
    attended = []
    for w in range(windows):
        at = slice(w * tokens, (w + 1) * tokens)
        wanted = kind_column + jnp.where(
            kind_column >= lon_shift, w * WIN, (w + 1) % windows * WIN
        )
        kind = jnp.where(kind_lane == wanted, kinds, 0.0).reshape(tokens, 128)
        kind = jnp.sum(kind, axis=-1, keepdims=True)
        query_marks, key_marks = [], []
        for first in (features - size, 0):
            here, following = lane == first, lane == first + 1
            query_marks.append(
                jnp.where(
                    here, -FAR * kind, jnp.where(following, -FAR * (1.0 - kind), 0.0)
                ).astype(jnp.bfloat16)
            )
            key_marks.append(
                jnp.where(here, 1.0 - kind, jnp.where(following, kind, 0.0)).astype(jnp.bfloat16)
            )
        attended.append(attend_block(query[at], key[at], value[at], query_marks, key_marks))
    attended = jnp.concatenate(attended)
    stream = (stream + wide_dot(attended, out_ref[...])).astype(jnp.bfloat16)
    result = feed_forward(stream, gains_ref[3:4], in2_ref, out2_ref).astype(jnp.float32)
    result = result.reshape(windows, WIN, WIN, features)
    for w in range(windows):
        tile = jnp.where(inside, result[w], result[(w + windows - 1) % windows])
        o_ref[:, w * WIN : (w + 1) * WIN, :] = tile.astype(jnp.bfloat16)


def cost(tokens, flops_per_token):
    return pl.CostEstimate(
        flops=tokens * flops_per_token, bytes_accessed=3 * 2**20, transcendentals=tokens * 2048
    )


LARGE = pltpu.CompilerParams(vmem_limit_bytes=48 * 2**20)


def settled_half(shifts, own):
    rows, *rest = own.shape
    return pl.pallas_call(
        settled_kernel,
        out_shape=jax.ShapeDtypeStruct((rows // 2, *rest), jnp.bfloat16),
        in_specs=[SMEM, VMEM],
        out_specs=VMEM,
    )(shifts, own)


def settled_member_layer(points, *params):
    return pl.pallas_call(
        settled_member_kernel,
        out_shape=jax.ShapeDtypeStruct(points.shape, jnp.bfloat16),
        in_specs=[VMEM] * (1 + len(params)),
        out_specs=VMEM,
        compiler_params=LARGE,
        cost_estimate=cost(512, 1600000),
    )(points, *params)


def open_member_layer(done, points, *params):
    members, *rest = points.shape
    return pl.pallas_call(
        open_member_kernel,
        out_shape=jax.ShapeDtypeStruct((members, 2, *rest), jnp.bfloat16),
        in_specs=[VMEM] * (2 + len(params)),
        out_specs=VMEM,
        compiler_params=LARGE,
        cost_estimate=cost(512, 1600000),
    )(done, points, *params)


def window_layer(shifts, region, kinds, *params):
    half, _, longitudes, features = region.shape
    return pl.pallas_call(
        window_kernel,
        out_shape=jax.ShapeDtypeStruct((2 * half, longitudes, features), jnp.bfloat16),
        in_specs=[SMEM] + [VMEM] * (2 + len(params)),
        out_specs=VMEM,
        compiler_params=LARGE,
        cost_estimate=cost(1024, 2000000),
    )(shifts, region, kinds, *params)


def on_device(
    ensemble,
    shifts,
    land_sea,
    member_gain,
    member_qkv,
    member_out,
    first_gain,
    first_in,
    first_out,
    window_gain,
    window_qkv,
    window_out,
    second_gain,
    second_in,
    second_out,
):
    _, rows, longitudes, features = ensemble.shape
    half = rows // 2
    spaces = lax.axis_size("space")
    up = [(i, (i + 1) % spaces) for i in range(spaces)]
    down = [(j, i) for i, j in up]
    gains = (member_gain, first_gain, window_gain, second_gain)
    members_first = (member_qkv, member_out, first_in, first_out)
    windows_second = (window_qkv, window_out, second_in, second_out)

    def exchange(parts):
        return lax.all_to_all(parts, "member", split_axis=0, concat_axis=0, tiled=True)

    shift = shifts[0]
    classes = range(half + 1)

    def assembled(k, own):
        if k == 0:
            return own[:half]
        if 2 * k <= half:
            n = 2 * k
            other = lax.ppermute(own[:n], "space", down)
            last = jnp.where(shift == n, other[n - 1 :], own[n - 1 : n])
            return jnp.concatenate([other[: n - 1], last, own[n:half]])
        n = 2 * k - 1
        other = lax.ppermute(own[n:], "space", up)
        first = jnp.where(shift == n, other[:1], own[n : n + 1])
        return jnp.concatenate([own[half:n], first, other[1:]])

    def returned(k, result):
        if k == 0:
            return result
        if 2 * k <= half:
            n = 2 * k
            other = lax.ppermute(result[:n], "space", up)
            last = jnp.where(shift == n, other[n - 1 :], result[n - 1 : n])
            return jnp.concatenate([other[: n - 1], last, result[n:]])
        n = 2 * k - 1
        other = lax.ppermute(result[n:], "space", down)
        first = jnp.where(shift == n, other[:1], result[n : n + 1])
        return jnp.concatenate([result[:n], first, other[1:]])

    which = lax.shift_right_logical(shift + 1, 1)
    def begin(k, own, *vectors):
        return assembled(k, own), lax.optimization_barrier(jnp.stack(vectors))

    own = ensemble[0]
    settled = exchange(settled_half(shifts, own))
    merged, gains = lax.switch(
        which, [lambda *x, k=k: begin(k, *x) for k in classes], own, *gains
    )
    merged = exchange(merged)
    settled = settled_member_layer(settled, gains, *members_first)
    region = exchange(open_member_layer(settled, merged, gains, *members_first))
    result = window_layer(shifts, region, land_sea.T, gains, *windows_second)
    out = lax.switch(which, [lambda x, k=k: returned(k, x) for k in classes], result)
    return out[None]


def solution(mesh):
    return jax.shard_map(
        on_device,
        mesh=mesh,
        in_specs=(P("member", "space", None, None),) + (P(),) * 14,
        out_specs=P("member", "space", None, None),
        check_vma=False,
    )
```

```python
import math

import jax
import jax.numpy as jnp
from jax import lax
from jax.experimental import pallas as pl
from jax.experimental.pallas import tpu as pltpu
from jax.sharding import PartitionSpec as P

HEADS = 8
WIN = 16
EPSILON = 1e-05
FAR = 1e30
VMEM = pl.BlockSpec(memory_space=pltpu.VMEM)
SMEM = pl.BlockSpec(memory_space=pltpu.SMEM)


def normalise(values, gains):
    center = jnp.mean(values, axis=-1, keepdims=True)
    shifted = values - center
    spread = jnp.mean(shifted * shifted, axis=-1, keepdims=True)
    return (shifted * lax.rsqrt(spread + EPSILON) * gains).astype(jnp.bfloat16)


def wide_dot(a, b):
    return jnp.dot(a, b, preferred_element_type=jnp.float32)


def twice_gelu(x):
    inner = x * (0.7978845608028654 + 0.035677408136300125 * (x * x))
    return (x + x * jnp.tanh(inner)).astype(jnp.bfloat16)


def feed_forward(stream, gains, in_ref, out_ref):
    wide = stream.astype(jnp.float32)
    normed = normalise(wide, gains)
    hidden = twice_gelu(wide_dot(normed, in_ref[...]))
    update = wide_dot(hidden, out_ref[...])
    return (wide + 0.5 * update).astype(jnp.bfloat16)


def project(stream, gains, qkv_ref):
    features = stream.shape[-1]
    normed = normalise(stream, gains)
    scale = math.log2(math.e) / math.sqrt(features // HEADS)
    query = (wide_dot(normed, qkv_ref[:, :features]) * scale).astype(jnp.bfloat16)
    key = wide_dot(normed, qkv_ref[:, features : 2 * features]).astype(jnp.bfloat16)
    value = wide_dot(normed, qkv_ref[:, 2 * features :]).astype(jnp.bfloat16)
    return query, key, value


def attend_block(query, key, value, query_marks, key_marks, with_maximum):
    tokens, features = query.shape
    size = features // HEADS
    half = features // 2
    lane = lax.broadcasted_iota(jnp.int32, (1, features), 1)

    def head_lanes(first):
        return jnp.where((lane >= first) & (lane < first + size), 1.0, 0.0).astype(jnp.bfloat16)

    results = []
    for group in range(2):
        free = features - size if group == 0 else 0
        heads = range(group * HEADS // 2, (group + 1) * HEADS // 2)
        keys = key * (1.0 - head_lanes(free)).astype(jnp.bfloat16) + key_marks[group]
        queries = jnp.concatenate(
            [query * head_lanes(h * size) + query_marks[group] for h in heads]
        )
        scores = lax.dot_general(
            queries, keys, (((1,), (1,)), ((), ())), preferred_element_type=jnp.float32
        )
        if with_maximum:
            scores = scores - jnp.max(scores, axis=-1, keepdims=True)
        weights = jnp.exp2(scores).astype(jnp.bfloat16)
        weights = [weights[n * tokens : (n + 1) * tokens] for n in range(len(heads))]
        opposite = half if group == 0 else -half
        values = [value * head_lanes(h * size) + head_lanes(h * size + opposite) for h in heads]
        total = wide_dot(jnp.concatenate(weights, axis=1), jnp.concatenate(values))
        if group == 0:
            results.append(total[:, :half] / total[:, half:])
        else:
            results.append(total[:, half:] / total[:, :half])
    return jnp.concatenate(results, axis=-1).astype(jnp.bfloat16)


def attend_blocks(projected, refs, marks, attended_ref):
    tokens, features = projected[0].shape
    block = WIN * WIN
    lane = lax.broadcasted_iota(jnp.int32, (features, 128), 1)
    head = lax.broadcasted_iota(jnp.int32, (features, 128), 0) // (features // HEADS)
    pick = jnp.where(lane == head, 1.0, 0.0).astype(jnp.bfloat16)
    norms = [jnp.max(wide_dot(p * p, pick)) for p in projected[:2]]
    safe = norms[0] * norms[1] <= 1e4
    for ref, values in zip(refs, projected):
        ref[...] = values

    @pl.when(safe)
    def _():
        for b in range(tokens // block):
            at = slice(b * block, (b + 1) * block)
            parts = [p[at] for p in refs]
            attended_ref[at] = attend_block(*parts, *marks(at), False)

    @pl.when(jnp.logical_not(safe))
    def _():
        @pl.loop(0, tokens // block)
        def _(b):
            at = pl.ds(pl.multiple_of(b * block, block), block)
            parts = [p[at] for p in refs]
            attended_ref[at] = attend_block(*parts, *marks(at), True)


def member_kernel(
    x_ref,
    gains_ref,
    qkv_ref,
    out_ref,
    in2_ref,
    out2_ref,
    o_ref,
    attended_ref,
    *projected_refs,
):
    members, points, features = x_ref.shape
    size = features // HEADS
    blocks = points // size
    x = x_ref[...].astype(jnp.float32)
    stream = jnp.concatenate(
        [x[:, b * size : (b + 1) * size].reshape(members * size, features) for b in range(blocks)]
    )
    projected = project(stream, gains_ref[0:1], qkv_ref)
    tokens = members * size
    lane = lax.broadcasted_iota(jnp.int32, (tokens, features), 1)
    point = lax.broadcasted_iota(jnp.int32, (tokens, features), 0) % size
    query_marks, key_marks = [], []
    for first in (features - size, 0):
        same = lane - first == point
        marked = (lane >= first) & (lane < first + size)
        query_marks.append(jnp.where(marked & ~same, -FAR, 0.0).astype(jnp.bfloat16))
        key_marks.append(jnp.where(same, 1.0, 0.0).astype(jnp.bfloat16))
    attend_blocks(projected, projected_refs, lambda at: (query_marks, key_marks), attended_ref)
    stream = (stream + wide_dot(attended_ref[...], out_ref[...])).astype(jnp.bfloat16)
    result = feed_forward(stream, gains_ref[1:2], in2_ref, out2_ref)
    result = [
        result[b * tokens : (b + 1) * tokens].reshape(members, size, features)
        for b in range(blocks)
    ]
    o_ref[...] = jnp.concatenate(result, axis=1)


def window_kernel(
    shifts_ref,
    x_ref,
    kinds_ref,
    gains_ref,
    qkv_ref,
    out_ref,
    in2_ref,
    out2_ref,
    o_ref,
    attended_ref,
    kind_ref,
    *projected_refs,
):
    rows, longitudes, features = o_ref.shape
    windows = longitudes // WIN
    size = features // HEADS
    tokens = WIN * WIN
    lat_shift, lon_shift = shifts_ref[0], shifts_ref[1]
    space = lax.axis_index("space")
    spaces = kinds_ref.shape[1] // WIN
    behind = jnp.where(lat_shift <= rows // 2, spaces, spaces - 1)
    block = lax.rem(space + behind, spaces)

    def block_rows(block):
        whole = lax.div(block * WIN, 128)
        part = kinds_ref[:, pl.ds(pl.multiple_of(whole * 128, 128), 128)].astype(jnp.float32)
        return pltpu.roll(part, lax.rem(128 - (block * WIN - whole * 128), 128), 1)

    lane = lax.broadcasted_iota(jnp.int32, (longitudes, 128), 1)
    kinds = jnp.where(
        lane >= lat_shift, block_rows(block), block_rows(lax.rem(block + 1, spaces))
    )
    kinds = jnp.concatenate([kinds] * (128 // longitudes)).T[:WIN]

    column = lax.broadcasted_iota(jnp.int32, (WIN, WIN, features), 1)
    inside = column >= lon_shift
    tiles = [x_ref[:, w * WIN : (w + 1) * WIN, :].astype(jnp.float32) for w in range(windows)]
    stream = jnp.concatenate(
        [
            jnp.where(inside, tiles[w], tiles[(w + 1) % windows]).reshape(tokens, features)
            for w in range(windows)
        ]
    )
    projected = project(stream, gains_ref[2:3], qkv_ref)

    kinds = jnp.broadcast_to(kinds[:, None, :], (WIN, WIN, 128))
    kind_column = lax.broadcasted_iota(jnp.int32, (WIN, WIN, 128), 1)
    kind_lane = lax.broadcasted_iota(jnp.int32, (WIN, WIN, 128), 2)

    lane = lax.broadcasted_iota(jnp.int32, (tokens, features), 1)
    for w in range(windows):
        wanted = kind_column + jnp.where(
            kind_column >= lon_shift, w * WIN, (w + 1) % windows * WIN
        )
        kind = jnp.where(kind_lane == wanted, kinds, 0.0).reshape(tokens, 128)
        kind = jnp.sum(kind, axis=-1, keepdims=True)
        kind_ref[w * tokens : (w + 1) * tokens] = jnp.broadcast_to(kind, (tokens, features))

    def marks(at):
        kind = kind_ref[at]
        query_marks, key_marks = [], []
        for first in (features - size, 0):
            here, following = lane == first, lane == first + 1
            query_marks.append(
                jnp.where(
                    here, -FAR * kind, jnp.where(following, -FAR * (1.0 - kind), 0.0)
                ).astype(jnp.bfloat16)
            )
            key_marks.append(
                jnp.where(here, 1.0 - kind, jnp.where(following, kind, 0.0)).astype(jnp.bfloat16)
            )
        return query_marks, key_marks

    attend_blocks(projected, projected_refs, marks, attended_ref)
    stream = (stream + wide_dot(attended_ref[...], out_ref[...])).astype(jnp.bfloat16)
    result = feed_forward(stream, gains_ref[3:4], in2_ref, out2_ref).astype(jnp.float32)
    result = result.reshape(windows, WIN, WIN, features)
    for w in range(windows):
        tile = jnp.where(inside, result[w], result[(w + windows - 1) % windows])
        o_ref[:, w * WIN : (w + 1) * WIN, :] = tile.astype(jnp.bfloat16)


def cost(tokens, flops_per_token):
    return pl.CostEstimate(
        flops=tokens * flops_per_token, bytes_accessed=3 * 2**20, transcendentals=tokens * 2048
    )


TOKENS = pltpu.VMEM((1024, 256), jnp.bfloat16)
LARGE = pltpu.CompilerParams(vmem_limit_bytes=48 * 2**20)


def member_layer(points, *params):
    return pl.pallas_call(
        member_kernel,
        out_shape=jax.ShapeDtypeStruct(points.shape, jnp.bfloat16),
        in_specs=[VMEM] * (1 + len(params)),
        out_specs=VMEM,
        scratch_shapes=[TOKENS] * 4,
        compiler_params=LARGE,
        cost_estimate=cost(1024, 1600000),
    )(points, *params)


def window_layer(shifts, region, kinds, *params):
    return pl.pallas_call(
        window_kernel,
        out_shape=jax.ShapeDtypeStruct(region.shape, jnp.bfloat16),
        in_specs=[SMEM] + [VMEM] * (2 + len(params)),
        out_specs=VMEM,
        scratch_shapes=[TOKENS, pltpu.VMEM((1024, 256), jnp.float32)] + [TOKENS] * 3,
        compiler_params=LARGE,
        cost_estimate=cost(1024, 2000000),
    )(shifts, region, kinds, *params)


def on_device(
    ensemble,
    shifts,
    land_sea,
    member_gain,
    member_qkv,
    member_out,
    first_gain,
    first_in,
    first_out,
    window_gain,
    window_qkv,
    window_out,
    second_gain,
    second_in,
    second_out,
):
    _, rows, longitudes, features = ensemble.shape
    half = rows // 2
    members = lax.axis_size("member")
    spaces = lax.axis_size("space")
    up = [(i, (i + 1) % spaces) for i in range(spaces)]
    down = [(j, i) for i, j in up]
    gains = (member_gain, first_gain, window_gain, second_gain)
    members_first = (member_qkv, member_out, first_in, first_out)
    windows_second = (window_qkv, window_out, second_in, second_out)

    def exchange(parts):
        return lax.all_to_all(parts, "member", split_axis=0, concat_axis=0, tiled=True)

    shift = shifts[0]
    classes = range(half + 1)

    def assembled(k, own):
        if k == 0:
            return own
        if 2 * k <= half:
            n = 2 * k
            other = lax.ppermute(own[:n], "space", down)
            last = jnp.where(shift == n, other[n - 1 :], own[n - 1 : n])
            return jnp.concatenate([other[: n - 1], last, own[n:]])
        n = 2 * k - 1
        other = lax.ppermute(own[n:], "space", up)
        first = jnp.where(shift == n, other[:1], own[n : n + 1])
        return jnp.concatenate([own[:n], first, other[1:]])

    def returned(k, result):
        if k == 0:
            return result
        if 2 * k <= half:
            n = 2 * k
            other = lax.ppermute(result[:n], "space", up)
            last = jnp.where(shift == n, other[n - 1 :], result[n - 1 : n])
            return jnp.concatenate([other[: n - 1], last, result[n:]])
        n = 2 * k - 1
        other = lax.ppermute(result[n:], "space", down)
        first = jnp.where(shift == n, other[:1], result[n : n + 1])
        return jnp.concatenate([result[:n], first, other[1:]])

    which = lax.shift_right_logical(shift + 1, 1)
    def begin(k, own, *vectors):
        return assembled(k, own), lax.optimization_barrier(jnp.stack(vectors))

    region, gains = lax.switch(
        which, [lambda *x, k=k: begin(k, *x) for k in classes], ensemble[0], *gains
    )
    points = exchange(region.reshape(members, -1, features))
    points = member_layer(points, gains, *members_first)
    region = exchange(points).reshape(rows, longitudes, features)
    result = window_layer(shifts, region, land_sea.T, gains, *windows_second)
    out = lax.switch(which, [lambda x, k=k: returned(k, x) for k in classes], result)
    return out[None]


def solution(mesh):
    return jax.shard_map(
        on_device,
        mesh=mesh,
        in_specs=(P("member", "space", None, None),) + (P(),) * 14,
        out_specs=P("member", "space", None, None),
        check_vma=False,
    )
```

```python
import math

import jax
import jax.numpy as jnp
from jax import lax
from jax.experimental import pallas as pl
from jax.experimental.pallas import tpu as pltpu
from jax.sharding import PartitionSpec as P

HEADS = 8
WIN = 16
EPSILON = 1e-05
FAR = 1e30
VMEM = pl.BlockSpec(memory_space=pltpu.VMEM)
SMEM = pl.BlockSpec(memory_space=pltpu.SMEM)


def normalise(values, gains):
    center = jnp.mean(values, axis=-1, keepdims=True)
    shifted = values - center
    spread = jnp.mean(shifted * shifted, axis=-1, keepdims=True)
    return (shifted * lax.rsqrt(spread + EPSILON) * gains).astype(jnp.bfloat16)


def wide_dot(a, b):
    return jnp.dot(a, b, preferred_element_type=jnp.float32)


def twice_gelu(x):
    x = x.astype(jnp.bfloat16)
    inner = x * (jnp.bfloat16(0.7978845608028654) + jnp.bfloat16(0.035677408136300125) * (x * x))
    return x + x * jnp.tanh(inner)


def feed_forward(stream, gains, in_ref, out_ref):
    wide = stream.astype(jnp.float32)
    normed = normalise(wide, gains)
    hidden = twice_gelu(wide_dot(normed, in_ref[...]))
    update = wide_dot(hidden, out_ref[...])
    return (wide + 0.5 * update).astype(jnp.bfloat16)


def project(stream, gains, qkv_ref):
    features = stream.shape[-1]
    normed = normalise(stream, gains)
    scale = math.log2(math.e) / math.sqrt(features // HEADS)
    query = (wide_dot(normed, qkv_ref[:, :features]) * scale).astype(jnp.bfloat16)
    key = wide_dot(normed, qkv_ref[:, features : 2 * features]).astype(jnp.bfloat16)
    value = wide_dot(normed, qkv_ref[:, 2 * features :]).astype(jnp.bfloat16)
    return query, key, value


def attend_block(query, key, value, query_marks, key_marks, with_maximum):
    tokens, features = query.shape
    size = features // HEADS
    half = features // 2
    lane = lax.broadcasted_iota(jnp.int32, (1, features), 1)

    def head_lanes(first):
        return jnp.where((lane >= first) & (lane < first + size), 1.0, 0.0).astype(jnp.bfloat16)

    results = []
    for group in range(2):
        free = features - size if group == 0 else 0
        heads = range(group * HEADS // 2, (group + 1) * HEADS // 2)
        keys = key * (1.0 - head_lanes(free)).astype(jnp.bfloat16) + key_marks[group]
        queries = jnp.concatenate(
            [query * head_lanes(h * size) + query_marks[group] for h in heads]
        )
        scores = lax.dot_general(
            queries, keys, (((1,), (1,)), ((), ())), preferred_element_type=jnp.float32
        )
        if with_maximum:
            scores = scores - jnp.max(scores, axis=-1, keepdims=True)
            weights = jnp.exp2(scores.astype(jnp.bfloat16))
        else:
            weights = jnp.exp2(scores).astype(jnp.bfloat16)
        weights = [weights[n * tokens : (n + 1) * tokens] for n in range(len(heads))]
        opposite = half if group == 0 else -half
        values = [value * head_lanes(h * size) + head_lanes(h * size + opposite) for h in heads]
        total = wide_dot(jnp.concatenate(weights, axis=1), jnp.concatenate(values))
        if group == 0:
            results.append(total[:, :half] / total[:, half:])
        else:
            results.append(total[:, half:] / total[:, :half])
    return jnp.concatenate(results, axis=-1).astype(jnp.bfloat16)


def attend_blocks(projected, refs, marks, attended_ref):
    tokens, features = projected[0].shape
    block = WIN * WIN
    lane = lax.broadcasted_iota(jnp.int32, (features, 128), 1)
    head = lax.broadcasted_iota(jnp.int32, (features, 128), 0) // (features // HEADS)
    pick = jnp.where(lane == head, 1.0, 0.0).astype(jnp.bfloat16)
    norms = [jnp.max(wide_dot(p * p, pick)) for p in projected[:2]]
    safe = norms[0] * norms[1] <= 1e4
    for ref, values in zip(refs, projected):
        ref[...] = values

    @pl.when(safe)
    def _():
        for b in range(tokens // block):
            at = slice(b * block, (b + 1) * block)
            parts = [p[at] for p in refs]
            attended_ref[at] = attend_block(*parts, *marks(at), False)

    @pl.when(jnp.logical_not(safe))
    def _():
        @pl.loop(0, tokens // block)
        def _(b):
            at = pl.ds(pl.multiple_of(b * block, block), block)
            parts = [p[at] for p in refs]
            attended_ref[at] = attend_block(*parts, *marks(at), True)


def member_kernel(
    x_ref,
    gains_ref,
    qkv_ref,
    out_ref,
    in2_ref,
    out2_ref,
    o_ref,
):
    members, points, features = x_ref.shape
    size = features // HEADS
    blocks = points // size
    x = x_ref[...].astype(jnp.float32)
    stream = jnp.concatenate(
        [x[:, b * size : (b + 1) * size].reshape(members * size, features) for b in range(blocks)]
    )
    projected = project(stream, gains_ref[0:1], qkv_ref)
    tokens = members * size
    lane = lax.broadcasted_iota(jnp.int32, (tokens, features), 1)
    point = lax.broadcasted_iota(jnp.int32, (tokens, features), 0) % size
    query_marks, key_marks = [], []
    for first in (features - size, 0):
        same = lane - first == point
        marked = (lane >= first) & (lane < first + size)
        query_marks.append(jnp.where(marked & ~same, -FAR, 0.0).astype(jnp.bfloat16))
        key_marks.append(jnp.where(same, 1.0, 0.0).astype(jnp.bfloat16))
    attended = []
    for b in range(blocks):
        at = slice(b * tokens, (b + 1) * tokens)
        parts = [p[at] for p in projected]
        attended.append(attend_block(*parts, query_marks, key_marks, True))
    attended = jnp.concatenate(attended)
    stream = (stream + wide_dot(attended, out_ref[...])).astype(jnp.bfloat16)
    result = feed_forward(stream, gains_ref[1:2], in2_ref, out2_ref)
    result = [
        result[b * tokens : (b + 1) * tokens].reshape(members, size, features)
        for b in range(blocks)
    ]
    o_ref[...] = jnp.concatenate(result, axis=1)


def window_kernel(
    shifts_ref,
    x_ref,
    kinds_ref,
    gains_ref,
    qkv_ref,
    out_ref,
    in2_ref,
    out2_ref,
    o_ref,
    attended_ref,
    kind_ref,
    *projected_refs,
):
    rows, longitudes, features = o_ref.shape
    windows = longitudes // WIN
    size = features // HEADS
    tokens = WIN * WIN
    lat_shift, lon_shift = shifts_ref[0], shifts_ref[1]
    space = lax.axis_index("space")
    spaces = kinds_ref.shape[1] // WIN
    behind = jnp.where(lat_shift <= rows // 2, spaces, spaces - 1)
    block = lax.rem(space + behind, spaces)

    def block_rows(block):
        whole = lax.div(block * WIN, 128)
        part = kinds_ref[:, pl.ds(pl.multiple_of(whole * 128, 128), 128)].astype(jnp.float32)
        return pltpu.roll(part, lax.rem(128 - (block * WIN - whole * 128), 128), 1)

    lane = lax.broadcasted_iota(jnp.int32, (longitudes, 128), 1)
    kinds = jnp.where(
        lane >= lat_shift, block_rows(block), block_rows(lax.rem(block + 1, spaces))
    )
    kinds = jnp.concatenate([kinds] * (128 // longitudes)).T[:WIN]

    column = lax.broadcasted_iota(jnp.int32, (WIN, WIN, features), 1)
    inside = column >= lon_shift
    tiles = [x_ref[:, w * WIN : (w + 1) * WIN, :].astype(jnp.float32) for w in range(windows)]
    stream = jnp.concatenate(
        [
            jnp.where(inside, tiles[w], tiles[(w + 1) % windows]).reshape(tokens, features)
            for w in range(windows)
        ]
    )
    projected = project(stream, gains_ref[2:3], qkv_ref)

    kinds = jnp.broadcast_to(kinds[:, None, :], (WIN, WIN, 128))
    kind_column = lax.broadcasted_iota(jnp.int32, (WIN, WIN, 128), 1)
    kind_lane = lax.broadcasted_iota(jnp.int32, (WIN, WIN, 128), 2)

    lane = lax.broadcasted_iota(jnp.int32, (tokens, features), 1)
    for w in range(windows):
        wanted = kind_column + jnp.where(
            kind_column >= lon_shift, w * WIN, (w + 1) % windows * WIN
        )
        kind = jnp.where(kind_lane == wanted, kinds, 0.0).reshape(tokens, 128)
        kind = jnp.sum(kind, axis=-1, keepdims=True)
        kind_ref[w * tokens : (w + 1) * tokens] = jnp.broadcast_to(kind, (tokens, features))

    def marks(at):
        kind = kind_ref[at]
        query_marks, key_marks = [], []
        for first in (features - size, 0):
            here, following = lane == first, lane == first + 1
            query_marks.append(
                jnp.where(
                    here, -FAR * kind, jnp.where(following, -FAR * (1.0 - kind), 0.0)
                ).astype(jnp.bfloat16)
            )
            key_marks.append(
                jnp.where(here, 1.0 - kind, jnp.where(following, kind, 0.0)).astype(jnp.bfloat16)
            )
        return query_marks, key_marks

    attend_blocks(projected, projected_refs, marks, attended_ref)
    stream = (stream + wide_dot(attended_ref[...], out_ref[...])).astype(jnp.bfloat16)
    result = feed_forward(stream, gains_ref[3:4], in2_ref, out2_ref).astype(jnp.float32)
    result = result.reshape(windows, WIN, WIN, features)
    for w in range(windows):
        tile = jnp.where(inside, result[w], result[(w + windows - 1) % windows])
        o_ref[:, w * WIN : (w + 1) * WIN, :] = tile.astype(jnp.bfloat16)


def cost(tokens, flops_per_token):
    return pl.CostEstimate(
        flops=tokens * flops_per_token, bytes_accessed=3 * 2**20, transcendentals=tokens * 2048
    )


TOKENS = pltpu.VMEM((1024, 256), jnp.bfloat16)
LARGE = pltpu.CompilerParams(vmem_limit_bytes=48 * 2**20)


def member_layer(points, *params):
    return pl.pallas_call(
        member_kernel,
        out_shape=jax.ShapeDtypeStruct(points.shape, jnp.bfloat16),
        in_specs=[VMEM] * (1 + len(params)),
        out_specs=VMEM,
        compiler_params=LARGE,
        cost_estimate=cost(1024, 1600000),
    )(points, *params)


def window_layer(shifts, region, kinds, *params):
    return pl.pallas_call(
        window_kernel,
        out_shape=jax.ShapeDtypeStruct(region.shape, jnp.bfloat16),
        in_specs=[SMEM] + [VMEM] * (2 + len(params)),
        out_specs=VMEM,
        scratch_shapes=[TOKENS, pltpu.VMEM((1024, 256), jnp.float32)] + [TOKENS] * 3,
        compiler_params=LARGE,
        cost_estimate=cost(1024, 2000000),
    )(shifts, region, kinds, *params)


def on_device(
    ensemble,
    shifts,
    land_sea,
    member_gain,
    member_qkv,
    member_out,
    first_gain,
    first_in,
    first_out,
    window_gain,
    window_qkv,
    window_out,
    second_gain,
    second_in,
    second_out,
):
    _, rows, longitudes, features = ensemble.shape
    half = rows // 2
    members = lax.axis_size("member")
    spaces = lax.axis_size("space")
    up = [(i, (i + 1) % spaces) for i in range(spaces)]
    down = [(j, i) for i, j in up]
    gains = (member_gain, first_gain, window_gain, second_gain)
    members_first = (member_qkv, member_out, first_in, first_out)
    windows_second = (window_qkv, window_out, second_in, second_out)

    def exchange(parts):
        return lax.all_to_all(parts, "member", split_axis=0, concat_axis=0, tiled=True)

    shift = shifts[0]
    classes = range(half + 1)

    def assembled(k, own):
        if k == 0:
            return own
        if 2 * k <= half:
            n = 2 * k
            other = lax.ppermute(own[:n], "space", down)
            last = jnp.where(shift == n, other[n - 1 :], own[n - 1 : n])
            return jnp.concatenate([other[: n - 1], last, own[n:]])
        n = 2 * k - 1
        other = lax.ppermute(own[n:], "space", up)
        first = jnp.where(shift == n, other[:1], own[n : n + 1])
        return jnp.concatenate([own[:n], first, other[1:]])

    def returned(k, result):
        if k == 0:
            return result
        if 2 * k <= half:
            n = 2 * k
            other = lax.ppermute(result[:n], "space", up)
            last = jnp.where(shift == n, other[n - 1 :], result[n - 1 : n])
            return jnp.concatenate([other[: n - 1], last, result[n:]])
        n = 2 * k - 1
        other = lax.ppermute(result[n:], "space", down)
        first = jnp.where(shift == n, other[:1], result[n : n + 1])
        return jnp.concatenate([result[:n], first, other[1:]])

    which = lax.shift_right_logical(shift + 1, 1)
    def begin(k, own, *vectors):
        return assembled(k, own), lax.optimization_barrier(jnp.stack(vectors))

    region, gains = lax.switch(
        which, [lambda *x, k=k: begin(k, *x) for k in classes], ensemble[0], *gains
    )
    points = exchange(region.reshape(members, -1, features))
    points = member_layer(points, gains, *members_first)
    region = exchange(points).reshape(rows, longitudes, features)
    result = window_layer(shifts, region, land_sea.T, gains, *windows_second)
    out = lax.switch(which, [lambda x, k=k: returned(k, x) for k in classes], result)
    return out[None]


def solution(mesh):
    return jax.shard_map(
        on_device,
        mesh=mesh,
        in_specs=(P("member", "space", None, None),) + (P(),) * 14,
        out_specs=P("member", "space", None, None),
        check_vma=False,
    )
```

```python
import math

import jax
import jax.numpy as jnp
from jax import lax
from jax.experimental import pallas as pl
from jax.experimental.pallas import tpu as pltpu
from jax.sharding import PartitionSpec as P

HEADS = 8
WIN = 16
EPSILON = 1e-05
FAR = 1e30
FAR_STEP = 16
VMEM = pl.BlockSpec(memory_space=pltpu.VMEM)
SMEM = pl.BlockSpec(memory_space=pltpu.SMEM)


def normalise(values, gains):
    center = jnp.mean(values, axis=-1, keepdims=True)
    shifted = values - center
    spread = jnp.mean(shifted * shifted, axis=-1, keepdims=True)
    return (shifted * lax.rsqrt(spread + EPSILON) * gains).astype(jnp.bfloat16)


def wide_dot(a, b):
    return jnp.dot(a, b, preferred_element_type=jnp.float32)


def twice_gelu(x):
    inner = x * (0.7978845608028654 + 0.035677408136300125 * (x * x))
    return (x + x * jnp.tanh(inner)).astype(jnp.bfloat16)


def feed_forward(stream, gains, in_ref, out_ref):
    wide = stream.astype(jnp.float32)
    normed = normalise(wide, gains)
    hidden = twice_gelu(wide_dot(normed, in_ref[...]))
    update = wide_dot(hidden, out_ref[...])
    return (wide + 0.5 * update).astype(jnp.bfloat16)


def project(stream, gains, qkv_ref):
    features = stream.shape[-1]
    normed = normalise(stream, gains)
    scale = math.log2(math.e) / math.sqrt(features // HEADS)
    query = (wide_dot(normed, qkv_ref[:, :features]) * scale).astype(jnp.bfloat16)
    key = wide_dot(normed, qkv_ref[:, features : 2 * features]).astype(jnp.bfloat16)
    value = wide_dot(normed, qkv_ref[:, 2 * features :]).astype(jnp.bfloat16)
    return query, key, value


def attend_block(query, key, value, query_marks, key_marks, with_maximum):
    tokens, features = query.shape
    size = features // HEADS
    half = features // 2
    lane = lax.broadcasted_iota(jnp.int32, (1, features), 1)

    def head_lanes(first):
        return jnp.where((lane >= first) & (lane < first + size), 1.0, 0.0).astype(jnp.bfloat16)

    results = []
    for group in range(2):
        free = features - size if group == 0 else 0
        heads = range(group * HEADS // 2, (group + 1) * HEADS // 2)
        keys = key * (1.0 - head_lanes(free)).astype(jnp.bfloat16) + key_marks[group]
        queries = jnp.concatenate(
            [query * head_lanes(h * size) + query_marks[group] for h in heads]
        )
        scores = lax.dot_general(
            queries, keys, (((1,), (1,)), ((), ())), preferred_element_type=jnp.float32
        )
        if with_maximum:
            scores = scores - jnp.max(scores, axis=-1, keepdims=True)
        weights = jnp.exp2(scores).astype(jnp.bfloat16)
        weights = [weights[n * tokens : (n + 1) * tokens] for n in range(len(heads))]
        opposite = half if group == 0 else -half
        values = [value * head_lanes(h * size) + head_lanes(h * size + opposite) for h in heads]
        total = wide_dot(jnp.concatenate(weights, axis=1), jnp.concatenate(values))
        if group == 0:
            results.append(total[:, :half] / total[:, half:])
        else:
            results.append(total[:, half:] / total[:, :half])
    return jnp.concatenate(results, axis=-1).astype(jnp.bfloat16)


def attend_blocks(projected, refs, marks, attended_ref):
    tokens, features = projected[0].shape
    block = WIN * WIN
    lane = lax.broadcasted_iota(jnp.int32, (features, 128), 1)
    head = lax.broadcasted_iota(jnp.int32, (features, 128), 0) // (features // HEADS)
    pick = jnp.where(lane == head, 1.0, 0.0).astype(jnp.bfloat16)
    norms = [jnp.max(wide_dot(p * p, pick)) for p in projected[:2]]
    safe = norms[0] * norms[1] <= 1e4
    for ref, values in zip(refs, projected):
        ref[...] = values

    @pl.when(safe)
    def _():
        for b in range(tokens // block):
            at = slice(b * block, (b + 1) * block)
            parts = [p[at] for p in refs]
            attended_ref[at] = attend_block(*parts, *marks(at), False)

    @pl.when(jnp.logical_not(safe))
    def _():
        @pl.loop(0, tokens // block)
        def _(b):
            at = pl.ds(pl.multiple_of(b * block, block), block)
            parts = [p[at] for p in refs]
            attended_ref[at] = attend_block(*parts, *marks(at), True)


def member_kernel(
    shifts_ref,
    x_ref,
    gains_ref,
    qkv_ref,
    out_ref,
    in2_ref,
    out2_ref,
    o_ref,
    attended_ref,
    *projected_refs,
):
    members, points, features = x_ref.shape
    size = features // HEADS
    blocks = points // size
    x = x_ref[...].astype(jnp.float32)
    stream = jnp.concatenate(
        [x[:, b * size : (b + 1) * size].reshape(members * size, features) for b in range(blocks)]
    )
    projected = project(stream, gains_ref[0:1], qkv_ref)
    tokens = members * size
    lane = lax.broadcasted_iota(jnp.int32, (tokens, features), 1)
    point = lax.broadcasted_iota(jnp.int32, (tokens, features), 0) % size
    query_marks, key_marks = [], []
    for first in (features - size, 0):
        same = lane - first == point
        marked = (lane >= first) & (lane < first + size)
        query_marks.append(jnp.where(marked & ~same, -FAR, 0.0).astype(jnp.bfloat16))
        key_marks.append(jnp.where(same, 1.0, 0.0).astype(jnp.bfloat16))
    attend_blocks(projected, projected_refs, lambda at: (query_marks, key_marks), attended_ref)
    stream = (stream + wide_dot(attended_ref[...], out_ref[...])).astype(jnp.bfloat16)
    result = feed_forward(stream, gains_ref[1:2], in2_ref, out2_ref)
    below = shifts_ref[0] <= WIN // 2
    far = lax.rem(lax.axis_index("space"), FAR_STEP) == jnp.where(below, FAR_STEP - 1, 0)
    blocks_per_row = blocks // 2
    results = []
    for b in range(blocks):
        part = result[b * tokens : (b + 1) * tokens]
        row = lax.axis_index("member") * 2 + b // blocks_per_row
        foreign = jnp.where(below, row < shifts_ref[0], row >= shifts_ref[0])
        crossed = jnp.concatenate([part[tokens // 2 :], part[: tokens // 2]])
        part = jnp.where(far & foreign, crossed, part)
        results.append(part.reshape(members, size, features))
    o_ref[...] = jnp.concatenate(results, axis=1)


def window_kernel(
    shifts_ref,
    x_ref,
    kinds_ref,
    gains_ref,
    qkv_ref,
    out_ref,
    in2_ref,
    out2_ref,
    o_ref,
    attended_ref,
    kind_ref,
    *projected_refs,
):
    rows, longitudes, features = o_ref.shape
    windows = longitudes // WIN
    size = features // HEADS
    tokens = WIN * WIN
    lat_shift, lon_shift = shifts_ref[0], shifts_ref[1]
    space = lax.axis_index("space")
    spaces = kinds_ref.shape[1] // WIN
    behind = jnp.where(lat_shift <= rows // 2, spaces, spaces - 1)
    block = lax.rem(space + behind, spaces)

    def block_rows(block):
        whole = lax.div(block * WIN, 128)
        part = kinds_ref[:, pl.ds(pl.multiple_of(whole * 128, 128), 128)].astype(jnp.float32)
        return pltpu.roll(part, lax.rem(128 - (block * WIN - whole * 128), 128), 1)

    lane = lax.broadcasted_iota(jnp.int32, (longitudes, 128), 1)
    kinds = jnp.where(
        lane >= lat_shift, block_rows(block), block_rows(lax.rem(block + 1, spaces))
    )
    kinds = jnp.concatenate([kinds] * (128 // longitudes)).T[:WIN]

    column = lax.broadcasted_iota(jnp.int32, (WIN, WIN, features), 1)
    inside = column >= lon_shift
    tiles = [x_ref[:, w * WIN : (w + 1) * WIN, :].astype(jnp.float32) for w in range(windows)]
    stream = jnp.concatenate(
        [
            jnp.where(inside, tiles[w], tiles[(w + 1) % windows]).reshape(tokens, features)
            for w in range(windows)
        ]
    )
    projected = project(stream, gains_ref[2:3], qkv_ref)

    kinds = jnp.broadcast_to(kinds[:, None, :], (WIN, WIN, 128))
    kind_column = lax.broadcasted_iota(jnp.int32, (WIN, WIN, 128), 1)
    kind_lane = lax.broadcasted_iota(jnp.int32, (WIN, WIN, 128), 2)

    lane = lax.broadcasted_iota(jnp.int32, (tokens, features), 1)
    for w in range(windows):
        wanted = kind_column + jnp.where(
            kind_column >= lon_shift, w * WIN, (w + 1) % windows * WIN
        )
        kind = jnp.where(kind_lane == wanted, kinds, 0.0).reshape(tokens, 128)
        kind = jnp.sum(kind, axis=-1, keepdims=True)
        kind_ref[w * tokens : (w + 1) * tokens] = jnp.broadcast_to(kind, (tokens, features))

    def marks(at):
        kind = kind_ref[at]
        query_marks, key_marks = [], []
        for first in (features - size, 0):
            here, following = lane == first, lane == first + 1
            query_marks.append(
                jnp.where(
                    here, -FAR * kind, jnp.where(following, -FAR * (1.0 - kind), 0.0)
                ).astype(jnp.bfloat16)
            )
            key_marks.append(
                jnp.where(here, 1.0 - kind, jnp.where(following, kind, 0.0)).astype(jnp.bfloat16)
            )
        return query_marks, key_marks

    attend_blocks(projected, projected_refs, marks, attended_ref)
    stream = (stream + wide_dot(attended_ref[...], out_ref[...])).astype(jnp.bfloat16)
    result = feed_forward(stream, gains_ref[3:4], in2_ref, out2_ref).astype(jnp.float32)
    result = result.reshape(windows, WIN, WIN, features)
    for w in range(windows):
        tile = jnp.where(inside, result[w], result[(w + windows - 1) % windows])
        o_ref[:, w * WIN : (w + 1) * WIN, :] = tile.astype(jnp.bfloat16)


def cost(tokens, flops_per_token):
    return pl.CostEstimate(
        flops=tokens * flops_per_token, bytes_accessed=3 * 2**20, transcendentals=tokens * 2048
    )


TOKENS = pltpu.VMEM((1024, 256), jnp.bfloat16)
LARGE = pltpu.CompilerParams(vmem_limit_bytes=48 * 2**20)


def member_layer(shifts, points, *params):
    return pl.pallas_call(
        member_kernel,
        out_shape=jax.ShapeDtypeStruct(points.shape, jnp.bfloat16),
        in_specs=[SMEM] + [VMEM] * (1 + len(params)),
        out_specs=VMEM,
        scratch_shapes=[TOKENS] * 4,
        compiler_params=LARGE,
        cost_estimate=cost(1024, 1600000),
    )(shifts, points, *params)


def window_layer(shifts, region, kinds, *params):
    return pl.pallas_call(
        window_kernel,
        out_shape=jax.ShapeDtypeStruct(region.shape, jnp.bfloat16),
        in_specs=[SMEM] + [VMEM] * (2 + len(params)),
        out_specs=VMEM,
        scratch_shapes=[TOKENS, pltpu.VMEM((1024, 256), jnp.float32)] + [TOKENS] * 3,
        compiler_params=LARGE,
        cost_estimate=cost(1024, 2000000),
    )(shifts, region, kinds, *params)


def on_device(
    ensemble,
    shifts,
    land_sea,
    member_gain,
    member_qkv,
    member_out,
    first_gain,
    first_in,
    first_out,
    window_gain,
    window_qkv,
    window_out,
    second_gain,
    second_in,
    second_out,
):
    _, rows, longitudes, features = ensemble.shape
    half = rows // 2
    members = lax.axis_size("member")
    spaces = lax.axis_size("space")
    up = [(i, (i + 1) % spaces) for i in range(spaces)]
    down = [(j, i) for i, j in up]
    gains = (member_gain, first_gain, window_gain, second_gain)
    members_first = (member_qkv, member_out, first_in, first_out)
    windows_second = (window_qkv, window_out, second_in, second_out)

    def exchange(parts):
        return lax.all_to_all(parts, "member", split_axis=0, concat_axis=0, tiled=True)

    shift = shifts[0]
    classes = range(half + 1)

    def crossed(pairs):
        return [
            (m * spaces + i, (m if i // FAR_STEP == j // FAR_STEP else m ^ 4) * spaces + j)
            for m in range(members)
            for i, j in pairs
        ]

    def assembled(k, own):
        if k == 0:
            return own
        if 2 * k <= half:
            n = 2 * k
            other = lax.ppermute(own[:n], ("member", "space"), crossed(down))
            last = jnp.where(shift == n, other[n - 1 :], own[n - 1 : n])
            return jnp.concatenate([other[: n - 1], last, own[n:]])
        n = 2 * k - 1
        other = lax.ppermute(own[n:], ("member", "space"), crossed(up))
        first = jnp.where(shift == n, other[:1], own[n : n + 1])
        return jnp.concatenate([own[:n], first, other[1:]])

    def returned(k, result):
        if k == 0:
            return result
        if 2 * k <= half:
            n = 2 * k
            other = lax.ppermute(result[:n], "space", up)
            last = jnp.where(shift == n, other[n - 1 :], result[n - 1 : n])
            return jnp.concatenate([other[: n - 1], last, result[n:]])
        n = 2 * k - 1
        other = lax.ppermute(result[n:], "space", down)
        first = jnp.where(shift == n, other[:1], result[n : n + 1])
        return jnp.concatenate([result[:n], first, other[1:]])

    which = lax.shift_right_logical(shift + 1, 1)
    def begin(k, own, *vectors):
        return assembled(k, own), lax.optimization_barrier(jnp.stack(vectors))

    region, gains = lax.switch(
        which, [lambda *x, k=k: begin(k, *x) for k in classes], ensemble[0], *gains
    )
    points = exchange(region.reshape(members, -1, features))
    points = member_layer(shifts, points, gains, *members_first)
    region = exchange(points).reshape(rows, longitudes, features)
    result = window_layer(shifts, region, land_sea.T, gains, *windows_second)
    out = lax.switch(which, [lambda x, k=k: returned(k, x) for k in classes], result)
    return out[None]


def solution(mesh):
    return jax.shard_map(
        on_device,
        mesh=mesh,
        in_specs=(P("member", "space", None, None),) + (P(),) * 14,
        out_specs=P("member", "space", None, None),
        check_vma=False,
    )
```

```python
import math

import jax
import jax.numpy as jnp
from jax import lax
from jax.experimental import pallas as pl
from jax.experimental.pallas import tpu as pltpu
from jax.sharding import PartitionSpec as P

HEADS = 8
WIN = 16
EPSILON = 1e-05
FAR = 1e30
FAR_STEP = 16
VMEM = pl.BlockSpec(memory_space=pltpu.VMEM)
SMEM = pl.BlockSpec(memory_space=pltpu.SMEM)


def normalise(values, gains):
    center = jnp.mean(values, axis=-1, keepdims=True)
    shifted = values - center
    spread = jnp.mean(shifted * shifted, axis=-1, keepdims=True)
    return (shifted * lax.rsqrt(spread + EPSILON) * gains).astype(jnp.bfloat16)


def wide_dot(a, b):
    return jnp.dot(a, b, preferred_element_type=jnp.float32)


def twice_gelu(x):
    inner = x * (0.7978845608028654 + 0.035677408136300125 * (x * x))
    return (x + x * jnp.tanh(inner)).astype(jnp.bfloat16)


def feed_forward(stream, gains, in_ref, out_ref):
    wide = stream.astype(jnp.float32)
    normed = normalise(wide, gains)
    hidden = twice_gelu(wide_dot(normed, in_ref[...]))
    update = wide_dot(hidden, out_ref[...])
    return (wide + 0.5 * update).astype(jnp.bfloat16)


def project(stream, gains, qkv_ref):
    features = stream.shape[-1]
    normed = normalise(stream, gains)
    scale = math.log2(math.e) / math.sqrt(features // HEADS)
    query = (wide_dot(normed, qkv_ref[:, :features]) * scale).astype(jnp.bfloat16)
    key = wide_dot(normed, qkv_ref[:, features : 2 * features]).astype(jnp.bfloat16)
    value = wide_dot(normed, qkv_ref[:, 2 * features :]).astype(jnp.bfloat16)
    return query, key, value


def attend_block(query, key, value, query_marks, key_marks, with_maximum):
    tokens, features = query.shape
    size = features // HEADS
    half = features // 2
    lane = lax.broadcasted_iota(jnp.int32, (1, features), 1)

    def head_lanes(first):
        return jnp.where((lane >= first) & (lane < first + size), 1.0, 0.0).astype(jnp.bfloat16)

    results = []
    for group in range(2):
        free = features - size if group == 0 else 0
        heads = range(group * HEADS // 2, (group + 1) * HEADS // 2)
        keys = key * (1.0 - head_lanes(free)).astype(jnp.bfloat16) + key_marks[group]
        queries = jnp.concatenate(
            [query * head_lanes(h * size) + query_marks[group] for h in heads]
        )
        scores = lax.dot_general(
            queries, keys, (((1,), (1,)), ((), ())), preferred_element_type=jnp.float32
        )
        if with_maximum:
            scores = scores - jnp.max(scores, axis=-1, keepdims=True)
        weights = jnp.exp2(scores).astype(jnp.bfloat16)
        weights = [weights[n * tokens : (n + 1) * tokens] for n in range(len(heads))]
        opposite = half if group == 0 else -half
        values = [value * head_lanes(h * size) + head_lanes(h * size + opposite) for h in heads]
        total = wide_dot(jnp.concatenate(weights, axis=1), jnp.concatenate(values))
        if group == 0:
            results.append(total[:, :half] / total[:, half:])
        else:
            results.append(total[:, half:] / total[:, :half])
    return jnp.concatenate(results, axis=-1).astype(jnp.bfloat16)


def attend_blocks(projected, refs, marks, attended_ref):
    tokens, features = projected[0].shape
    block = WIN * WIN
    lane = lax.broadcasted_iota(jnp.int32, (features, 128), 1)
    head = lax.broadcasted_iota(jnp.int32, (features, 128), 0) // (features // HEADS)
    pick = jnp.where(lane == head, 1.0, 0.0).astype(jnp.bfloat16)
    norms = [jnp.max(wide_dot(p * p, pick)) for p in projected[:2]]
    safe = norms[0] * norms[1] <= 1e4
    for ref, values in zip(refs, projected):
        ref[...] = values

    @pl.when(safe)
    def _():
        for b in range(tokens // block):
            at = slice(b * block, (b + 1) * block)
            parts = [p[at] for p in refs]
            attended_ref[at] = attend_block(*parts, *marks(at), False)

    @pl.when(jnp.logical_not(safe))
    def _():
        @pl.loop(0, tokens // block)
        def _(b):
            at = pl.ds(pl.multiple_of(b * block, block), block)
            parts = [p[at] for p in refs]
            attended_ref[at] = attend_block(*parts, *marks(at), True)


def member_kernel(
    shifts_ref,
    x_ref,
    gains_ref,
    qkv_ref,
    out_ref,
    in2_ref,
    out2_ref,
    o_ref,
    attended_ref,
    *projected_refs,
):
    members, points, features = x_ref.shape
    size = features // HEADS
    blocks = points // size
    x = x_ref[...].astype(jnp.float32)
    stream = jnp.concatenate(
        [x[:, b * size : (b + 1) * size].reshape(members * size, features) for b in range(blocks)]
    )
    projected = project(stream, gains_ref[0:1], qkv_ref)
    tokens = members * size
    lane = lax.broadcasted_iota(jnp.int32, (tokens, features), 1)
    point = lax.broadcasted_iota(jnp.int32, (tokens, features), 0) % size
    query_marks, key_marks = [], []
    for first in (features - size, 0):
        same = lane - first == point
        marked = (lane >= first) & (lane < first + size)
        query_marks.append(jnp.where(marked & ~same, -FAR, 0.0).astype(jnp.bfloat16))
        key_marks.append(jnp.where(same, 1.0, 0.0).astype(jnp.bfloat16))
    attend_blocks(projected, projected_refs, lambda at: (query_marks, key_marks), attended_ref)
    stream = (stream + wide_dot(attended_ref[...], out_ref[...])).astype(jnp.bfloat16)
    result = feed_forward(stream, gains_ref[1:2], in2_ref, out2_ref)
    result = [
        result[b * tokens : (b + 1) * tokens].reshape(members, size, features)
        for b in range(blocks)
    ]
    o_ref[...] = jnp.concatenate(result, axis=1)

    below = shifts_ref[0] <= WIN // 2
    far = lax.rem(lax.axis_index("space"), FAR_STEP) == jnp.where(below, FAR_STEP - 1, 0)
    for n in range(2):
        row = lax.axis_index("member") * 2 + n
        at = slice(n * points // 2, (n + 1) * points // 2)

        @pl.when(far & jnp.where(below, row < shifts_ref[0], row >= shifts_ref[0]))
        def _():
            crossed = o_ref[:, at]
            o_ref[:, at] = jnp.concatenate([crossed[members // 2 :], crossed[: members // 2]])


def window_kernel(
    shifts_ref,
    x_ref,
    kinds_ref,
    gains_ref,
    qkv_ref,
    out_ref,
    in2_ref,
    out2_ref,
    o_ref,
    attended_ref,
    kind_ref,
    *projected_refs,
):
    rows, longitudes, features = o_ref.shape
    windows = longitudes // WIN
    size = features // HEADS
    tokens = WIN * WIN
    lat_shift, lon_shift = shifts_ref[0], shifts_ref[1]
    space = lax.axis_index("space")
    spaces = kinds_ref.shape[1] // WIN
    behind = jnp.where(lat_shift <= rows // 2, spaces, spaces - 1)
    block = lax.rem(space + behind, spaces)

    def block_rows(block):
        whole = lax.div(block * WIN, 128)
        part = kinds_ref[:, pl.ds(pl.multiple_of(whole * 128, 128), 128)].astype(jnp.float32)
        return pltpu.roll(part, lax.rem(128 - (block * WIN - whole * 128), 128), 1)

    lane = lax.broadcasted_iota(jnp.int32, (longitudes, 128), 1)
    kinds = jnp.where(
        lane >= lat_shift, block_rows(block), block_rows(lax.rem(block + 1, spaces))
    )
    kinds = jnp.concatenate([kinds] * (128 // longitudes)).T[:WIN]

    column = lax.broadcasted_iota(jnp.int32, (WIN, WIN, features), 1)
    inside = column >= lon_shift
    tiles = [x_ref[:, w * WIN : (w + 1) * WIN, :].astype(jnp.float32) for w in range(windows)]
    stream = jnp.concatenate(
        [
            jnp.where(inside, tiles[w], tiles[(w + 1) % windows]).reshape(tokens, features)
            for w in range(windows)
        ]
    )
    projected = project(stream, gains_ref[2:3], qkv_ref)

    kinds = jnp.broadcast_to(kinds[:, None, :], (WIN, WIN, 128))
    kind_column = lax.broadcasted_iota(jnp.int32, (WIN, WIN, 128), 1)
    kind_lane = lax.broadcasted_iota(jnp.int32, (WIN, WIN, 128), 2)

    lane = lax.broadcasted_iota(jnp.int32, (tokens, features), 1)
    for w in range(windows):
        wanted = kind_column + jnp.where(
            kind_column >= lon_shift, w * WIN, (w + 1) % windows * WIN
        )
        kind = jnp.where(kind_lane == wanted, kinds, 0.0).reshape(tokens, 128)
        kind = jnp.sum(kind, axis=-1, keepdims=True)
        kind_ref[w * tokens : (w + 1) * tokens] = jnp.broadcast_to(kind, (tokens, features))

    def marks(at):
        kind = kind_ref[at]
        query_marks, key_marks = [], []
        for first in (features - size, 0):
            here, following = lane == first, lane == first + 1
            query_marks.append(
                jnp.where(
                    here, -FAR * kind, jnp.where(following, -FAR * (1.0 - kind), 0.0)
                ).astype(jnp.bfloat16)
            )
            key_marks.append(
                jnp.where(here, 1.0 - kind, jnp.where(following, kind, 0.0)).astype(jnp.bfloat16)
            )
        return query_marks, key_marks

    attend_blocks(projected, projected_refs, marks, attended_ref)
    stream = (stream + wide_dot(attended_ref[...], out_ref[...])).astype(jnp.bfloat16)
    result = feed_forward(stream, gains_ref[3:4], in2_ref, out2_ref).astype(jnp.float32)
    result = result.reshape(windows, WIN, WIN, features)
    for w in range(windows):
        tile = jnp.where(inside, result[w], result[(w + windows - 1) % windows])
        o_ref[:, w * WIN : (w + 1) * WIN, :] = tile.astype(jnp.bfloat16)


def cost(tokens, flops_per_token):
    return pl.CostEstimate(
        flops=tokens * flops_per_token, bytes_accessed=3 * 2**20, transcendentals=tokens * 2048
    )


TOKENS = pltpu.VMEM((1024, 256), jnp.bfloat16)
LARGE = pltpu.CompilerParams(vmem_limit_bytes=48 * 2**20)


def member_layer(shifts, points, *params):
    return pl.pallas_call(
        member_kernel,
        out_shape=jax.ShapeDtypeStruct(points.shape, jnp.bfloat16),
        in_specs=[SMEM] + [VMEM] * (1 + len(params)),
        out_specs=VMEM,
        scratch_shapes=[TOKENS] * 4,
        compiler_params=LARGE,
        cost_estimate=cost(1024, 1600000),
    )(shifts, points, *params)


def window_layer(shifts, region, kinds, *params):
    return pl.pallas_call(
        window_kernel,
        out_shape=jax.ShapeDtypeStruct(region.shape, jnp.bfloat16),
        in_specs=[SMEM] + [VMEM] * (2 + len(params)),
        out_specs=VMEM,
        scratch_shapes=[TOKENS, pltpu.VMEM((1024, 256), jnp.float32)] + [TOKENS] * 3,
        compiler_params=LARGE,
        cost_estimate=cost(1024, 2000000),
    )(shifts, region, kinds, *params)


def on_device(
    ensemble,
    shifts,
    land_sea,
    member_gain,
    member_qkv,
    member_out,
    first_gain,
    first_in,
    first_out,
    window_gain,
    window_qkv,
    window_out,
    second_gain,
    second_in,
    second_out,
):
    _, rows, longitudes, features = ensemble.shape
    half = rows // 2
    members = lax.axis_size("member")
    spaces = lax.axis_size("space")
    up = [(i, (i + 1) % spaces) for i in range(spaces)]
    down = [(j, i) for i, j in up]
    gains = (member_gain, first_gain, window_gain, second_gain)
    members_first = (member_qkv, member_out, first_in, first_out)
    windows_second = (window_qkv, window_out, second_in, second_out)

    def exchange(parts):
        return lax.all_to_all(parts, "member", split_axis=0, concat_axis=0, tiled=True)

    shift = shifts[0]
    classes = range(half + 1)

    def crossed(pairs):
        return [
            (m * spaces + i, (m if i // FAR_STEP == j // FAR_STEP else m ^ 4) * spaces + j)
            for m in range(members)
            for i, j in pairs
        ]

    def assembled(k, own):
        if k == 0:
            return own
        if 2 * k <= half:
            n = 2 * k
            other = lax.ppermute(own[:n], ("member", "space"), crossed(down))
            last = jnp.where(shift == n, other[n - 1 :], own[n - 1 : n])
            return jnp.concatenate([other[: n - 1], last, own[n:]])
        n = 2 * k - 1
        other = lax.ppermute(own[n:], ("member", "space"), crossed(up))
        first = jnp.where(shift == n, other[:1], own[n : n + 1])
        return jnp.concatenate([own[:n], first, other[1:]])

    def returned(k, result):
        if k == 0:
            return result
        if 2 * k <= half:
            n = 2 * k
            other = lax.ppermute(result[:n], "space", up)
            last = jnp.where(shift == n, other[n - 1 :], result[n - 1 : n])
            return jnp.concatenate([other[: n - 1], last, result[n:]])
        n = 2 * k - 1
        other = lax.ppermute(result[n:], "space", down)
        first = jnp.where(shift == n, other[:1], result[n : n + 1])
        return jnp.concatenate([result[:n], first, other[1:]])

    which = lax.shift_right_logical(shift + 1, 1)
    def begin(k, own, *vectors):
        return assembled(k, own), lax.optimization_barrier(jnp.stack(vectors))

    region, gains = lax.switch(
        which, [lambda *x, k=k: begin(k, *x) for k in classes], ensemble[0], *gains
    )
    points = exchange(region.reshape(members, -1, features))
    points = member_layer(shifts, points, gains, *members_first)
    region = exchange(points).reshape(rows, longitudes, features)
    result = window_layer(shifts, region, land_sea.T, gains, *windows_second)
    out = lax.switch(which, [lambda x, k=k: returned(k, x) for k in classes], result)
    return out[None]


def solution(mesh):
    return jax.shard_map(
        on_device,
        mesh=mesh,
        in_specs=(P("member", "space", None, None),) + (P(),) * 14,
        out_specs=P("member", "space", None, None),
        check_vma=False,
    )
```

```python
import math

import jax
import jax.numpy as jnp
from jax import lax
from jax.experimental import pallas as pl
from jax.experimental.pallas import tpu as pltpu
from jax.sharding import PartitionSpec as P

HEADS = 8
WIN = 16
EPSILON = 1e-05
FAR = 1e30
FAR_STEP = 16
VMEM = pl.BlockSpec(memory_space=pltpu.VMEM)


def normalise(values, gains):
    center = jnp.mean(values, axis=-1, keepdims=True)
    shifted = values - center
    spread = jnp.mean(shifted * shifted, axis=-1, keepdims=True)
    return (shifted * lax.rsqrt(spread + EPSILON) * gains).astype(jnp.bfloat16)


def wide_dot(a, b):
    return jnp.dot(a, b, preferred_element_type=jnp.float32)


def twice_gelu(x):
    inner = x * (0.7978845608028654 + 0.035677408136300125 * (x * x))
    return (x + x * jnp.tanh(inner)).astype(jnp.bfloat16)


def feed_forward(stream, gains, in_ref, out_ref):
    wide = stream.astype(jnp.float32)
    normed = normalise(wide, gains)
    hidden = twice_gelu(wide_dot(normed, in_ref[...]))
    update = wide_dot(hidden, out_ref[...])
    return (wide + 0.5 * update).astype(jnp.bfloat16)


def project(stream, gains, qkv_ref):
    features = stream.shape[-1]
    normed = normalise(stream, gains)
    scale = math.log2(math.e) / math.sqrt(features // HEADS)
    query = (wide_dot(normed, qkv_ref[:, :features]) * scale).astype(jnp.bfloat16)
    key = wide_dot(normed, qkv_ref[:, features : 2 * features]).astype(jnp.bfloat16)
    value = wide_dot(normed, qkv_ref[:, 2 * features :]).astype(jnp.bfloat16)
    return query, key, value


def attend_block(query, key, value, query_marks, key_marks, with_maximum):
    tokens, features = query.shape
    size = features // HEADS
    half = features // 2
    lane = lax.broadcasted_iota(jnp.int32, (1, features), 1)

    def head_lanes(first):
        return jnp.where((lane >= first) & (lane < first + size), 1.0, 0.0).astype(jnp.bfloat16)

    results = []
    for group in range(2):
        free = features - size if group == 0 else 0
        heads = range(group * HEADS // 2, (group + 1) * HEADS // 2)
        keys = key * (1.0 - head_lanes(free)).astype(jnp.bfloat16) + key_marks[group]
        queries = jnp.concatenate(
            [query * head_lanes(h * size) + query_marks[group] for h in heads]
        )
        scores = lax.dot_general(
            queries, keys, (((1,), (1,)), ((), ())), preferred_element_type=jnp.float32
        )
        if with_maximum:
            scores = scores - jnp.max(scores, axis=-1, keepdims=True)
        weights = jnp.exp2(scores).astype(jnp.bfloat16)
        weights = [weights[n * tokens : (n + 1) * tokens] for n in range(len(heads))]
        opposite = half if group == 0 else -half
        values = [value * head_lanes(h * size) + head_lanes(h * size + opposite) for h in heads]
        total = wide_dot(jnp.concatenate(weights, axis=1), jnp.concatenate(values))
        if group == 0:
            results.append(total[:, :half] / total[:, half:])
        else:
            results.append(total[:, half:] / total[:, :half])
    return jnp.concatenate(results, axis=-1).astype(jnp.bfloat16)


def attend_blocks(projected, refs, marks, attended_ref):
    tokens, features = projected[0].shape
    block = WIN * WIN
    lane = lax.broadcasted_iota(jnp.int32, (features, 128), 1)
    head = lax.broadcasted_iota(jnp.int32, (features, 128), 0) // (features // HEADS)
    pick = jnp.where(lane == head, 1.0, 0.0).astype(jnp.bfloat16)
    norms = [jnp.max(wide_dot(p * p, pick)) for p in projected[:2]]
    safe = norms[0] * norms[1] <= 1e4
    for ref, values in zip(refs, projected):
        ref[...] = values

    @pl.when(safe)
    def _():
        for b in range(tokens // block):
            at = slice(b * block, (b + 1) * block)
            parts = [p[at] for p in refs]
            attended_ref[at] = attend_block(*parts, *marks(at), False)

    @pl.when(jnp.logical_not(safe))
    def _():
        @pl.loop(0, tokens // block)
        def _(b):
            at = pl.ds(pl.multiple_of(b * block, block), block)
            parts = [p[at] for p in refs]
            attended_ref[at] = attend_block(*parts, *marks(at), True)


def shift_in(gains_ref, which):
    return jnp.max(gains_ref[4 + which : 5 + which, :128]).astype(jnp.int32)


def member_kernel(
    x_ref,
    gains_ref,
    qkv_ref,
    out_ref,
    in2_ref,
    out2_ref,
    o_ref,
    attended_ref,
    *projected_refs,
):
    members, points, features = x_ref.shape
    size = features // HEADS
    blocks = points // size
    x = x_ref[...].astype(jnp.float32)
    stream = jnp.concatenate(
        [x[:, b * size : (b + 1) * size].reshape(members * size, features) for b in range(blocks)]
    )
    projected = project(stream, gains_ref[0:1], qkv_ref)
    tokens = members * size
    lane = lax.broadcasted_iota(jnp.int32, (tokens, features), 1)
    point = lax.broadcasted_iota(jnp.int32, (tokens, features), 0) % size
    query_marks, key_marks = [], []
    for first in (features - size, 0):
        same = lane - first == point
        marked = (lane >= first) & (lane < first + size)
        query_marks.append(jnp.where(marked & ~same, -FAR, 0.0).astype(jnp.bfloat16))
        key_marks.append(jnp.where(same, 1.0, 0.0).astype(jnp.bfloat16))
    attend_blocks(projected, projected_refs, lambda at: (query_marks, key_marks), attended_ref)
    stream = (stream + wide_dot(attended_ref[...], out_ref[...])).astype(jnp.bfloat16)
    result = feed_forward(stream, gains_ref[1:2], in2_ref, out2_ref)
    result = [
        result[b * tokens : (b + 1) * tokens].reshape(members, size, features)
        for b in range(blocks)
    ]
    o_ref[...] = jnp.concatenate(result, axis=1)

    lat_shift = shift_in(gains_ref, 0)
    below = lat_shift <= WIN // 2
    far = lax.rem(lax.axis_index("space"), FAR_STEP) == jnp.where(below, FAR_STEP - 1, 0)
    for n in range(2):
        row = lax.axis_index("member") * 2 + n
        at = slice(n * points // 2, (n + 1) * points // 2)

        @pl.when(far & jnp.where(below, row < lat_shift, row >= lat_shift))
        def _():
            crossed = o_ref[:, at]
            o_ref[:, at] = jnp.concatenate([crossed[members // 2 :], crossed[: members // 2]])


def window_kernel(
    x_ref,
    kinds_ref,
    gains_ref,
    qkv_ref,
    out_ref,
    in2_ref,
    out2_ref,
    o_ref,
    attended_ref,
    kind_ref,
    *projected_refs,
):
    rows, longitudes, features = o_ref.shape
    windows = longitudes // WIN
    size = features // HEADS
    tokens = WIN * WIN
    lat_shift, lon_shift = shift_in(gains_ref, 0), shift_in(gains_ref, 1)
    space = lax.axis_index("space")
    spaces = kinds_ref.shape[1] // WIN
    behind = jnp.where(lat_shift <= rows // 2, spaces, spaces - 1)
    block = lax.rem(space + behind, spaces)

    def block_rows(block):
        whole = lax.div(block * WIN, 128)
        part = kinds_ref[:, pl.ds(pl.multiple_of(whole * 128, 128), 128)].astype(jnp.float32)
        return pltpu.roll(part, lax.rem(128 - (block * WIN - whole * 128), 128), 1)

    lane = lax.broadcasted_iota(jnp.int32, (longitudes, 128), 1)
    kinds = jnp.where(
        lane >= lat_shift, block_rows(block), block_rows(lax.rem(block + 1, spaces))
    )
    kinds = jnp.concatenate([kinds] * (128 // longitudes)).T[:WIN]

    column = lax.broadcasted_iota(jnp.int32, (WIN, WIN, features), 1)
    inside = column >= lon_shift
    tiles = [x_ref[:, w * WIN : (w + 1) * WIN, :].astype(jnp.float32) for w in range(windows)]
    stream = jnp.concatenate(
        [
            jnp.where(inside, tiles[w], tiles[(w + 1) % windows]).reshape(tokens, features)
            for w in range(windows)
        ]
    )
    projected = project(stream, gains_ref[2:3], qkv_ref)

    kinds = jnp.broadcast_to(kinds[:, None, :], (WIN, WIN, 128))
    kind_column = lax.broadcasted_iota(jnp.int32, (WIN, WIN, 128), 1)
    kind_lane = lax.broadcasted_iota(jnp.int32, (WIN, WIN, 128), 2)

    lane = lax.broadcasted_iota(jnp.int32, (tokens, features), 1)
    for w in range(windows):
        wanted = kind_column + jnp.where(
            kind_column >= lon_shift, w * WIN, (w + 1) % windows * WIN
        )
        kind = jnp.where(kind_lane == wanted, kinds, 0.0).reshape(tokens, 128)
        kind = jnp.sum(kind, axis=-1, keepdims=True)
        kind_ref[w * tokens : (w + 1) * tokens] = jnp.broadcast_to(kind, (tokens, features))

    def marks(at):
        kind = kind_ref[at]
        query_marks, key_marks = [], []
        for first in (features - size, 0):
            here, following = lane == first, lane == first + 1
            query_marks.append(
                jnp.where(
                    here, -FAR * kind, jnp.where(following, -FAR * (1.0 - kind), 0.0)
                ).astype(jnp.bfloat16)
            )
            key_marks.append(
                jnp.where(here, 1.0 - kind, jnp.where(following, kind, 0.0)).astype(jnp.bfloat16)
            )
        return query_marks, key_marks

    attend_blocks(projected, projected_refs, marks, attended_ref)
    stream = (stream + wide_dot(attended_ref[...], out_ref[...])).astype(jnp.bfloat16)
    result = feed_forward(stream, gains_ref[3:4], in2_ref, out2_ref).astype(jnp.float32)
    result = result.reshape(windows, WIN, WIN, features)
    for w in range(windows):
        tile = jnp.where(inside, result[w], result[(w + windows - 1) % windows])
        o_ref[:, w * WIN : (w + 1) * WIN, :] = tile.astype(jnp.bfloat16)


def cost(tokens, flops_per_token):
    return pl.CostEstimate(
        flops=tokens * flops_per_token, bytes_accessed=3 * 2**20, transcendentals=tokens * 2048
    )


TOKENS = pltpu.VMEM((1024, 256), jnp.bfloat16)
LARGE = pltpu.CompilerParams(vmem_limit_bytes=48 * 2**20)


def member_layer(points, *params):
    return pl.pallas_call(
        member_kernel,
        out_shape=jax.ShapeDtypeStruct(points.shape, jnp.bfloat16),
        in_specs=[VMEM] * (1 + len(params)),
        out_specs=VMEM,
        scratch_shapes=[TOKENS] * 4,
        compiler_params=LARGE,
        cost_estimate=cost(1024, 1600000),
    )(points, *params)


def window_layer(region, kinds, *params):
    return pl.pallas_call(
        window_kernel,
        out_shape=jax.ShapeDtypeStruct(region.shape, jnp.bfloat16),
        in_specs=[VMEM] * (2 + len(params)),
        out_specs=VMEM,
        scratch_shapes=[TOKENS, pltpu.VMEM((1024, 256), jnp.float32)] + [TOKENS] * 3,
        compiler_params=LARGE,
        cost_estimate=cost(1024, 2000000),
    )(region, kinds, *params)


def on_device(
    ensemble,
    shifts,
    land_sea,
    member_gain,
    member_qkv,
    member_out,
    first_gain,
    first_in,
    first_out,
    window_gain,
    window_qkv,
    window_out,
    second_gain,
    second_in,
    second_out,
):
    _, rows, longitudes, features = ensemble.shape
    half = rows // 2
    members = lax.axis_size("member")
    spaces = lax.axis_size("space")
    up = [(i, (i + 1) % spaces) for i in range(spaces)]
    down = [(j, i) for i, j in up]
    gains = (member_gain, first_gain, window_gain, second_gain)
    members_first = (member_qkv, member_out, first_in, first_out)
    windows_second = (window_qkv, window_out, second_in, second_out)

    def exchange(parts):
        return lax.all_to_all(parts, "member", split_axis=0, concat_axis=0, tiled=True)

    shift = shifts[0]
    classes = range(half + 1)

    def crossed(pairs):
        return [
            (m * spaces + i, (m if i // FAR_STEP == j // FAR_STEP else m ^ 4) * spaces + j)
            for m in range(members)
            for i, j in pairs
        ]

    def assembled(k, own):
        if k == 0:
            return own
        if 2 * k <= half:
            n = 2 * k
            other = lax.ppermute(own[:n], ("member", "space"), crossed(down))
            last = jnp.where(shift == n, other[n - 1 :], own[n - 1 : n])
            return jnp.concatenate([other[: n - 1], last, own[n:]])
        n = 2 * k - 1
        other = lax.ppermute(own[n:], ("member", "space"), crossed(up))
        first = jnp.where(shift == n, other[:1], own[n : n + 1])
        return jnp.concatenate([own[:n], first, other[1:]])

    def returned(k, result):
        if k == 0:
            return result
        if 2 * k <= half:
            n = 2 * k
            other = lax.ppermute(result[:n], "space", up)
            last = jnp.where(shift == n, other[n - 1 :], result[n - 1 : n])
            return jnp.concatenate([other[: n - 1], last, result[n:]])
        n = 2 * k - 1
        other = lax.ppermute(result[n:], "space", down)
        first = jnp.where(shift == n, other[:1], result[n : n + 1])
        return jnp.concatenate([result[:n], first, other[1:]])

    which = lax.shift_right_logical(shift + 1, 1)
    def begin(k, own, *vectors):
        wide = jnp.broadcast_to(shifts.astype(jnp.float32)[:, None], (2, features))
        return assembled(k, own), lax.optimization_barrier(
            jnp.concatenate([jnp.stack(vectors), wide])
        )

    region, gains = lax.switch(
        which, [lambda *x, k=k: begin(k, *x) for k in classes], ensemble[0], *gains
    )
    points = exchange(region.reshape(members, -1, features))
    points = member_layer(points, gains, *members_first)
    region = exchange(points).reshape(rows, longitudes, features)
    result = window_layer(region, land_sea.T, gains, *windows_second)
    out = lax.switch(which, [lambda x, k=k: returned(k, x) for k in classes], result)
    return out[None]


def solution(mesh):
    return jax.shard_map(
        on_device,
        mesh=mesh,
        in_specs=(P("member", "space", None, None),) + (P(),) * 14,
        out_specs=P("member", "space", None, None),
        check_vma=False,
    )
```

```python
import math

import jax
import jax.numpy as jnp
from jax import lax
from jax.experimental import pallas as pl
from jax.experimental.pallas import tpu as pltpu
from jax.sharding import PartitionSpec as P

HEADS = 8
WIN = 16
EPSILON = 1e-05
FAR = 1e30
FAR_STEP = 16
VMEM = pl.BlockSpec(memory_space=pltpu.VMEM)


def normalise(values, gains):
    center = jnp.mean(values, axis=-1, keepdims=True)
    shifted = values - center
    spread = jnp.mean(shifted * shifted, axis=-1, keepdims=True)
    return (shifted * lax.rsqrt(spread + EPSILON) * gains).astype(jnp.bfloat16)


def wide_dot(a, b):
    return jnp.dot(a, b, preferred_element_type=jnp.float32)


def twice_gelu(x):
    inner = x * (0.7978845608028654 + 0.035677408136300125 * (x * x))
    return (x + x * jnp.tanh(inner)).astype(jnp.bfloat16)


def feed_forward(stream, gains, in_ref, out_ref):
    wide = stream.astype(jnp.float32)
    normed = normalise(wide, gains)
    hidden = twice_gelu(wide_dot(normed, in_ref[...]))
    update = wide_dot(hidden, out_ref[...])
    return (wide + 0.5 * update).astype(jnp.bfloat16)


def project(stream, gains, qkv_ref):
    features = stream.shape[-1]
    normed = normalise(stream, gains)
    scale = math.log2(math.e) / math.sqrt(features // HEADS)
    query = (wide_dot(normed, qkv_ref[:, :features]) * scale).astype(jnp.bfloat16)
    key = wide_dot(normed, qkv_ref[:, features : 2 * features]).astype(jnp.bfloat16)
    value = wide_dot(normed, qkv_ref[:, 2 * features :]).astype(jnp.bfloat16)
    return query, key, value


def attend_block(query, key, value, query_marks, key_marks, with_maximum):
    tokens, features = query.shape
    size = features // HEADS
    half = features // 2
    lane = lax.broadcasted_iota(jnp.int32, (1, features), 1)

    def head_lanes(first):
        return jnp.where((lane >= first) & (lane < first + size), 1.0, 0.0).astype(jnp.bfloat16)

    results = []
    for group in range(2):
        free = features - size if group == 0 else 0
        heads = range(group * HEADS // 2, (group + 1) * HEADS // 2)
        keys = key * (1.0 - head_lanes(free)).astype(jnp.bfloat16) + key_marks[group]
        queries = jnp.concatenate(
            [query * head_lanes(h * size) + query_marks[group] for h in heads]
        )
        scores = lax.dot_general(
            queries, keys, (((1,), (1,)), ((), ())), preferred_element_type=jnp.float32
        )
        if with_maximum:
            scores = scores - jnp.max(scores, axis=-1, keepdims=True)
        weights = jnp.exp2(scores).astype(jnp.bfloat16)
        weights = [weights[n * tokens : (n + 1) * tokens] for n in range(len(heads))]
        opposite = half if group == 0 else -half
        values = [value * head_lanes(h * size) + head_lanes(h * size + opposite) for h in heads]
        total = wide_dot(jnp.concatenate(weights, axis=1), jnp.concatenate(values))
        if group == 0:
            results.append(total[:, :half] / total[:, half:])
        else:
            results.append(total[:, half:] / total[:, :half])
    return jnp.concatenate(results, axis=-1).astype(jnp.bfloat16)


def attend_blocks(projected, refs, marks, attended_ref):
    tokens, features = projected[0].shape
    block = WIN * WIN
    lane = lax.broadcasted_iota(jnp.int32, (features, 128), 1)
    head = lax.broadcasted_iota(jnp.int32, (features, 128), 0) // (features // HEADS)
    pick = jnp.where(lane == head, 1.0, 0.0).astype(jnp.bfloat16)
    norms = [jnp.max(wide_dot(p * p, pick)) for p in projected[:2]]
    safe = norms[0] * norms[1] <= 1e4
    for ref, values in zip(refs, projected):
        ref[...] = values

    @pl.when(safe)
    def _():
        @pl.loop(0, tokens // (2 * block))
        def _(b):
            for n in range(2):
                at = pl.ds(pl.multiple_of((2 * b + n) * block, block), block)
                parts = [p[at] for p in refs]
                attended_ref[at] = attend_block(*parts, *marks(at), False)

    @pl.when(jnp.logical_not(safe))
    def _():
        @pl.loop(0, tokens // block)
        def _(b):
            at = pl.ds(pl.multiple_of(b * block, block), block)
            parts = [p[at] for p in refs]
            attended_ref[at] = attend_block(*parts, *marks(at), True)


def shift_in(gains_ref, which):
    return jnp.max(gains_ref[4 + which : 5 + which, :128]).astype(jnp.int32)


def member_kernel(
    x_ref,
    gains_ref,
    qkv_ref,
    out_ref,
    in2_ref,
    out2_ref,
    o_ref,
    attended_ref,
    *projected_refs,
):
    members, points, features = x_ref.shape
    size = features // HEADS
    blocks = points // size
    x = x_ref[...].astype(jnp.float32)
    stream = jnp.concatenate(
        [x[:, b * size : (b + 1) * size].reshape(members * size, features) for b in range(blocks)]
    )
    projected = project(stream, gains_ref[0:1], qkv_ref)
    tokens = members * size
    lane = lax.broadcasted_iota(jnp.int32, (tokens, features), 1)
    point = lax.broadcasted_iota(jnp.int32, (tokens, features), 0) % size
    query_marks, key_marks = [], []
    for first in (features - size, 0):
        same = lane - first == point
        marked = (lane >= first) & (lane < first + size)
        query_marks.append(jnp.where(marked & ~same, -FAR, 0.0).astype(jnp.bfloat16))
        key_marks.append(jnp.where(same, 1.0, 0.0).astype(jnp.bfloat16))
    attend_blocks(projected, projected_refs, lambda at: (query_marks, key_marks), attended_ref)
    stream = (stream + wide_dot(attended_ref[...], out_ref[...])).astype(jnp.bfloat16)
    result = feed_forward(stream, gains_ref[1:2], in2_ref, out2_ref)
    result = [
        result[b * tokens : (b + 1) * tokens].reshape(members, size, features)
        for b in range(blocks)
    ]
    o_ref[...] = jnp.concatenate(result, axis=1)

    lat_shift = shift_in(gains_ref, 0)
    below = lat_shift <= WIN // 2
    far = lax.rem(lax.axis_index("space"), FAR_STEP) == jnp.where(below, FAR_STEP - 1, 0)
    for n in range(2):
        row = lax.axis_index("member") * 2 + n
        at = slice(n * points // 2, (n + 1) * points // 2)

        @pl.when(far & jnp.where(below, row < lat_shift, row >= lat_shift))
        def _():
            crossed = o_ref[:, at]
            o_ref[:, at] = jnp.concatenate([crossed[members // 2 :], crossed[: members // 2]])


def window_kernel(
    x_ref,
    kinds_ref,
    gains_ref,
    qkv_ref,
    out_ref,
    in2_ref,
    out2_ref,
    o_ref,
    attended_ref,
    kind_ref,
    *projected_refs,
):
    rows, longitudes, features = o_ref.shape
    windows = longitudes // WIN
    size = features // HEADS
    tokens = WIN * WIN
    lat_shift, lon_shift = shift_in(gains_ref, 0), shift_in(gains_ref, 1)
    space = lax.axis_index("space")
    spaces = kinds_ref.shape[1] // WIN
    behind = jnp.where(lat_shift <= rows // 2, spaces, spaces - 1)
    block = lax.rem(space + behind, spaces)

    def block_rows(block):
        whole = lax.div(block * WIN, 128)
        part = kinds_ref[:, pl.ds(pl.multiple_of(whole * 128, 128), 128)].astype(jnp.float32)
        return pltpu.roll(part, lax.rem(128 - (block * WIN - whole * 128), 128), 1)

    lane = lax.broadcasted_iota(jnp.int32, (longitudes, 128), 1)
    kinds = jnp.where(
        lane >= lat_shift, block_rows(block), block_rows(lax.rem(block + 1, spaces))
    )
    kinds = jnp.concatenate([kinds] * (128 // longitudes)).T[:WIN]

    column = lax.broadcasted_iota(jnp.int32, (WIN, WIN, features), 1)
    inside = column >= lon_shift
    tiles = [x_ref[:, w * WIN : (w + 1) * WIN, :].astype(jnp.float32) for w in range(windows)]
    stream = jnp.concatenate(
        [
            jnp.where(inside, tiles[w], tiles[(w + 1) % windows]).reshape(tokens, features)
            for w in range(windows)
        ]
    )
    projected = project(stream, gains_ref[2:3], qkv_ref)

    kinds = jnp.broadcast_to(kinds[:, None, :], (WIN, WIN, 128))
    kind_column = lax.broadcasted_iota(jnp.int32, (WIN, WIN, 128), 1)
    kind_lane = lax.broadcasted_iota(jnp.int32, (WIN, WIN, 128), 2)

    lane = lax.broadcasted_iota(jnp.int32, (tokens, features), 1)
    for w in range(windows):
        wanted = kind_column + jnp.where(
            kind_column >= lon_shift, w * WIN, (w + 1) % windows * WIN
        )
        kind = jnp.where(kind_lane == wanted, kinds, 0.0).reshape(tokens, 128)
        kind = jnp.sum(kind, axis=-1, keepdims=True)
        kind_ref[w * tokens : (w + 1) * tokens] = jnp.broadcast_to(kind, (tokens, features))

    def marks(at):
        kind = kind_ref[at]
        query_marks, key_marks = [], []
        for first in (features - size, 0):
            here, following = lane == first, lane == first + 1
            query_marks.append(
                jnp.where(
                    here, -FAR * kind, jnp.where(following, -FAR * (1.0 - kind), 0.0)
                ).astype(jnp.bfloat16)
            )
            key_marks.append(
                jnp.where(here, 1.0 - kind, jnp.where(following, kind, 0.0)).astype(jnp.bfloat16)
            )
        return query_marks, key_marks

    attend_blocks(projected, projected_refs, marks, attended_ref)
    stream = (stream + wide_dot(attended_ref[...], out_ref[...])).astype(jnp.bfloat16)
    result = feed_forward(stream, gains_ref[3:4], in2_ref, out2_ref).astype(jnp.float32)
    result = result.reshape(windows, WIN, WIN, features)
    for w in range(windows):
        tile = jnp.where(inside, result[w], result[(w + windows - 1) % windows])
        o_ref[:, w * WIN : (w + 1) * WIN, :] = tile.astype(jnp.bfloat16)


def cost(tokens, flops_per_token):
    return pl.CostEstimate(
        flops=tokens * flops_per_token, bytes_accessed=3 * 2**20, transcendentals=tokens * 2048
    )


TOKENS = pltpu.VMEM((1024, 256), jnp.bfloat16)
LARGE = pltpu.CompilerParams(vmem_limit_bytes=48 * 2**20)


def member_layer(points, *params):
    return pl.pallas_call(
        member_kernel,
        out_shape=jax.ShapeDtypeStruct(points.shape, jnp.bfloat16),
        in_specs=[VMEM] * (1 + len(params)),
        out_specs=VMEM,
        scratch_shapes=[TOKENS] * 4,
        compiler_params=LARGE,
        cost_estimate=cost(1024, 1600000),
    )(points, *params)


def window_layer(region, kinds, *params):
    return pl.pallas_call(
        window_kernel,
        out_shape=jax.ShapeDtypeStruct(region.shape, jnp.bfloat16),
        in_specs=[VMEM] * (2 + len(params)),
        out_specs=VMEM,
        scratch_shapes=[TOKENS, pltpu.VMEM((1024, 256), jnp.float32)] + [TOKENS] * 3,
        compiler_params=LARGE,
        cost_estimate=cost(1024, 2000000),
    )(region, kinds, *params)


def on_device(
    ensemble,
    shifts,
    land_sea,
    member_gain,
    member_qkv,
    member_out,
    first_gain,
    first_in,
    first_out,
    window_gain,
    window_qkv,
    window_out,
    second_gain,
    second_in,
    second_out,
):
    _, rows, longitudes, features = ensemble.shape
    half = rows // 2
    members = lax.axis_size("member")
    spaces = lax.axis_size("space")
    up = [(i, (i + 1) % spaces) for i in range(spaces)]
    down = [(j, i) for i, j in up]
    gains = (member_gain, first_gain, window_gain, second_gain)
    members_first = (member_qkv, member_out, first_in, first_out)
    windows_second = (window_qkv, window_out, second_in, second_out)

    def exchange(parts):
        return lax.all_to_all(parts, "member", split_axis=0, concat_axis=0, tiled=True)

    shift = shifts[0]
    classes = range(half + 1)

    def crossed(pairs):
        return [
            (m * spaces + i, (m if i // FAR_STEP == j // FAR_STEP else m ^ 4) * spaces + j)
            for m in range(members)
            for i, j in pairs
        ]

    def assembled(k, own):
        if k == 0:
            return own
        if 2 * k <= half:
            n = 2 * k
            other = lax.ppermute(own[:n], ("member", "space"), crossed(down))
            last = jnp.where(shift == n, other[n - 1 :], own[n - 1 : n])
            return jnp.concatenate([other[: n - 1], last, own[n:]])
        n = 2 * k - 1
        other = lax.ppermute(own[n:], ("member", "space"), crossed(up))
        first = jnp.where(shift == n, other[:1], own[n : n + 1])
        return jnp.concatenate([own[:n], first, other[1:]])

    def returned(k, result):
        if k == 0:
            return result
        if 2 * k <= half:
            n = 2 * k
            other = lax.ppermute(result[:n], "space", up)
            last = jnp.where(shift == n, other[n - 1 :], result[n - 1 : n])
            return jnp.concatenate([other[: n - 1], last, result[n:]])
        n = 2 * k - 1
        other = lax.ppermute(result[n:], "space", down)
        first = jnp.where(shift == n, other[:1], result[n : n + 1])
        return jnp.concatenate([result[:n], first, other[1:]])

    which = lax.shift_right_logical(shift + 1, 1)
    def begin(k, own, *vectors):
        wide = jnp.broadcast_to(shifts.astype(jnp.float32)[:, None], (2, features))
        return assembled(k, own), lax.optimization_barrier(
            jnp.concatenate([jnp.stack(vectors), wide])
        )

    region, gains = lax.switch(
        which, [lambda *x, k=k: begin(k, *x) for k in classes], ensemble[0], *gains
    )
    points = exchange(region.reshape(members, -1, features))
    points = member_layer(points, gains, *members_first)
    region = exchange(points).reshape(rows, longitudes, features)
    result = window_layer(region, land_sea.T, gains, *windows_second)
    out = lax.switch(which, [lambda x, k=k: returned(k, x) for k in classes], result)
    return out[None]


def solution(mesh):
    return jax.shard_map(
        on_device,
        mesh=mesh,
        in_specs=(P("member", "space", None, None),) + (P(),) * 14,
        out_specs=P("member", "space", None, None),
        check_vma=False,
    )
```
